256 devices in a mesh: gx: 8 (over y, core), gy: 4 (over x), gz: 8 (over z).
Axes of the slice: x: 4, y: 4, z: 8, core: 2. Of those that a mesh axis runs over, the one named last changes fastest.
Arguments:
- velocity: float32 [3, 256, 128, 1024], P(None, 'gx', 'gy', 'gz'), may hold values from -3 to 3
- box_level: float32 [8192, 16, 256], P(('gx', 'gy', 'gz')), may hold values from -9 to 9
- corners: int32 [8192, 3], P(('gx', 'gy', 'gz')), may hold values from 0 to 112, as said below
- owner_list: int32 [8192], P(('gx', 'gy', 'gz')), may hold values from -1 to 31, as said below
Outputs:
- new_velocity: float32 [3, 256, 128, 1024], P(None, 'gx', 'gy', 'gz')
- level_sets: float32 [8192, 16, 256], P(('gx', 'gy', 'gz'))
- curvature: float32 [8192, 16, 256], P(('gx', 'gy', 'gz'))
The draws below stay inside these ranges and needn't reach their ends.
Inputs may be any that keep to these rules, and one draw needn't show every extreme that they name: `owner_list`: -1 marks an empty slot. The live slots of one device name different helpers, numbered in the order of the devices of its gy+gz group (gy slowest) at the device's own index along gx; every helper is named by exactly 16 slots of its group; a device has 0 to 32 live slots, and some device of every group has 32. `corners`: columns 0, 1, 2 lie in 0 to 16, 16, 112: every box lies inside its home device's block. Boxes may intersect.
All inputs are finite; a program needn't handle non-finite values.
Results may differ from the reference program's by a relative error of at most 0.0003.
Values sent between devices are 32-bit elements; how exact they have to be, the bound alone decides.
No kernel may reach another device: no remote copies, remote signals or barrier semaphores. Data moves between devices by JAX's collectives and lax.ppermute only.
A program may use at most 128 MiB of HBM per device.

```python
import math
import jax
import jax.numpy as jnp
from jax import lax

CX = 32
CY = 32
CZ = 128
BOX = 16
ITERS = 12
GROUP = 32
HELP = 16
SLOTS = 32
SLOTS_ALL = 8192
NX = 256
NY = 128
NZ = 1024
N_GY = 4
N_GZ = 8


def draw_corners(key, part):
    along_x = jax.random.randint(jax.random.fold_in(key, 11), (SLOTS_ALL, 1), 0, CX - BOX + 1)
    along_y = jax.random.randint(jax.random.fold_in(key, 13), (SLOTS_ALL, 1), 0, CY - BOX + 1)
    along_z = jax.random.randint(jax.random.fold_in(key, 17), (SLOTS_ALL, 1), 0, CZ - BOX + 1)
    return jnp.concatenate([along_x, along_y, along_z], axis=1).astype(jnp.int32)


def group_owners(group_key):
    pair_count = GROUP // 2
    subkeys = jax.random.split(group_key, 4)
    excess = jax.random.randint(subkeys[0], (pair_count,), 0, HELP + 1)
    excess = excess.at[0].set(HELP)
    counts = jnp.concatenate([HELP + excess, HELP - excess])
    counts = counts[jax.random.permutation(subkeys[1], GROUP)]
    starts = jnp.cumsum(counts) - counts
    relabel = jax.random.permutation(subkeys[2], GROUP).astype(jnp.int32)
    position = jnp.arange(SLOTS, dtype=jnp.int32)
    serial = starts[:, None] + position[None, :]
    named_ids = jnp.where(position[None, :] < counts[:, None], relabel[serial % GROUP], -1)
    home_keys = jax.random.split(subkeys[3], GROUP)
    orders = jax.vmap(lambda home_key: jax.random.permutation(home_key, SLOTS))(home_keys)
    return jnp.take_along_axis(named_ids, orders, axis=1)


def draw_owner_list(key, part):
    group_keys = jax.random.split(jax.random.fold_in(key, 29), SLOTS_ALL // (SLOTS * GROUP))
    owners = jax.vmap(group_owners)(group_keys)
    return owners.reshape(SLOTS_ALL).astype(jnp.int32)


def shard_levels(stream_key, dims, pieces, smallest, largest):
    loudness, own = 1.0, jax.random.fold_in(stream_key, 6)
    for dim, parts in pieces:
        heights = jnp.exp(jax.random.uniform(jax.random.fold_in(own, dim), (parts,), jnp.float32, smallest / len(pieces), largest / len(pieces)))
        loudness = loudness * jnp.repeat(heights, dims[dim] // parts).reshape([-1 if axis == dim else 1 for axis in range(len(dims))])
    return loudness


def centred(own_key, dims, deviation, limit, shards=(), kind=jnp.bfloat16):
    factor_of = shard_levels(own_key, dims, shards, -0.22, 0.18) if shards else 1.0
    array = jax.random.normal(own_key, dims, jnp.float32) * deviation * factor_of
    return jnp.minimum(jnp.maximum(array, -limit), limit).astype(kind)


def setup_inputs(seed: int = 0) -> dict:
    splits = jax.random.split(jax.random.key(seed), 5)
    velocity = centred(splits[0], (3, NX, NY, NZ), 0.5, 3.0, ((1, 8), (2, 4), (3, 8)), jnp.float32)
    box_level = centred(splits[1], (SLOTS_ALL, BOX, BOX * BOX), 1.5, 9.0, ((0, 256),), jnp.float32)
    corners = draw_corners(jax.random.fold_in(splits[4], 71), 0)
    owner_list = draw_owner_list(jax.random.fold_in(splits[4], 71), 0)
    return {"velocity": velocity, "box_level": box_level, "corners": corners, "owner_list": owner_list}


box_step = 0.25
pseudo_step = 0.3
weno_floor = 1e-06
band_width = 1.5
tension = 2.0
grid_step = 0.2
viscosity = 0.1
normal_floor = 0.5

def neighbour(values, across, forward):
    length = values.shape[-2]
    plane_size = values.shape[-1]
    if across == 0:
        if forward:
            return jnp.concatenate([values[..., 1:, :], values[..., -1:, :]], axis=-2)
        return jnp.concatenate([values[..., :1, :], values[..., :-1, :]], axis=-2)
    stride = length if across == 1 else 1
    places = jnp.arange(plane_size, dtype=jnp.int32)
    column = places // length if across == 1 else places % length
    if forward:
        shifted = jnp.concatenate([values[..., stride:], values[..., :stride]], axis=-1)
        return jnp.where(column == length - 1, values, shifted)
    shifted = jnp.concatenate([values[..., plane_size - stride:], values[..., :plane_size - stride]], axis=-1)
    return jnp.where(column == 0, values, shifted)

def weno_blend(slope_one, slope_two, slope_three, slope_four, slope_five):
    smooth_one = 13.0 / 12.0 * (slope_one - 2.0 * slope_two + slope_three) ** 2 + 0.25 * (slope_one - 4.0 * slope_two + 3.0 * slope_three) ** 2
    smooth_two = 13.0 / 12.0 * (slope_two - 2.0 * slope_three + slope_four) ** 2 + 0.25 * (slope_two - slope_four) ** 2
    smooth_three = 13.0 / 12.0 * (slope_three - 2.0 * slope_four + slope_five) ** 2 + 0.25 * (3.0 * slope_three - 4.0 * slope_four + slope_five) ** 2
    weight_one = 0.1 / (weno_floor + smooth_one) ** 2
    weight_two = 0.6 / (weno_floor + smooth_two) ** 2
    weight_three = 0.3 / (weno_floor + smooth_three) ** 2
    poly_one = slope_one / 3.0 - 7.0 * slope_two / 6.0 + 11.0 * slope_three / 6.0
    poly_two = -slope_two / 6.0 + 5.0 * slope_three / 6.0 + slope_four / 3.0
    poly_three = slope_three / 3.0 + 5.0 * slope_four / 6.0 - slope_five / 6.0
    return (weight_one * poly_one + weight_two * poly_two + weight_three * poly_three) / (weight_one + weight_two + weight_three)

def upwind_slopes(values, across):
    behind = values - neighbour(values, across, False)
    back_one = neighbour(behind, across, False)
    back_two = neighbour(back_one, across, False)
    ahead_one = neighbour(behind, across, True)
    ahead_two = neighbour(ahead_one, across, True)
    ahead_three = neighbour(ahead_two, across, True)
    minus_side = weno_blend(back_two, back_one, behind, ahead_one, ahead_two)
    plus_side = weno_blend(ahead_three, ahead_two, ahead_one, behind, back_one)
    return (minus_side, plus_side)

def central_slopes(values):
    return [0.5 * (neighbour(values, across, True) - neighbour(values, across, False)) for across in range(3)]

def evolve_boxes(levels, motion):
    change = jnp.zeros_like(levels)
    for across in range(3):
        minus_side, plus_side = upwind_slopes(levels, across)
        speed_d = motion[:, across]
        change = change + jnp.maximum(speed_d, 0.0) * minus_side + jnp.minimum(speed_d, 0.0) * plus_side
    advected = levels - box_step * change
    sign_soft = advected / jnp.sqrt(advected * advected + 1.0)
    outside = advected > 0.0

    def one_sweep(counter, current):
        squared = jnp.zeros_like(current)
        for across in range(3):
            behind = current - neighbour(current, across, False)
            ahead_d = neighbour(current, across, True) - current
            upper_sq = jnp.maximum(jnp.maximum(behind, 0.0) ** 2, jnp.minimum(ahead_d, 0.0) ** 2)
            lower_sq = jnp.maximum(jnp.minimum(behind, 0.0) ** 2, jnp.maximum(ahead_d, 0.0) ** 2)
            squared = squared + jnp.where(outside, upper_sq, lower_sq)
        return current - pseudo_step * sign_soft * (jnp.sqrt(squared) - 1.0)
    settled = lax.fori_loop(0, ITERS, one_sweep, advected)
    slopes = central_slopes(settled)
    magnitude = jnp.maximum(jnp.sqrt(slopes[0] ** 2 + slopes[1] ** 2 + slopes[2] ** 2), normal_floor)
    bending = jnp.zeros_like(settled)
    for across in range(3):
        unit_d = slopes[across] / magnitude
        bending = bending + 0.5 * (neighbour(unit_d, across, True) - neighbour(unit_d, across, False))
    return (settled, bending)

def surface_force(levels, bending):
    slopes = central_slopes(levels)
    delta_band = jnp.exp(-(levels / band_width) ** 2) / (band_width * math.sqrt(math.pi))
    strength = tension * bending * delta_band
    return jnp.stack([strength * slopes[0], strength * slopes[1], strength * slopes[2]], axis=1)

def tendency(padded):
    centre = padded[:, 1:-1, 1:-1, 1:-1]
    uppers = (padded[:, 2:, 1:-1, 1:-1], padded[:, 1:-1, 2:, 1:-1], padded[:, 1:-1, 1:-1, 2:])
    lowers = (padded[:, :-2, 1:-1, 1:-1], padded[:, 1:-1, :-2, 1:-1], padded[:, 1:-1, 1:-1, :-2])
    advect = jnp.zeros_like(centre)
    spread = -6.0 * centre
    for across in range(3):
        advect = advect + centre[across:across + 1] * (uppers[across] - lowers[across]) * 0.5
        spread = spread + uppers[across] + lowers[across]
    return viscosity * spread - advect

def wrap_pad(values):
    return jnp.pad(values, ((0, 0), (1, 1), (1, 1), (1, 1)), mode='wrap')

def reference(velocity, box_level, corners, owner_list):
    alive_mask = (owner_list >= 0).astype(jnp.float32)
    slot_ids = jnp.arange(SLOTS_ALL, dtype=jnp.int32)
    device = slot_ids // SLOTS
    anchor_x = (device // (N_GY * N_GZ) * CX + corners[:, 0]).astype(jnp.int32)
    anchor_y = (device // N_GZ % N_GY * CY + corners[:, 1]).astype(jnp.int32)
    anchor_z = (device % N_GZ * CZ + corners[:, 2]).astype(jnp.int32)
    nought = jnp.zeros((), jnp.int32)

    def one_box(packed):
        level_box, place_x, place_y, place_z = packed
        motion = lax.dynamic_slice(velocity, (nought, place_x, place_y, place_z), (3, BOX, BOX, BOX))
        motion = motion.reshape(1, 3, BOX, BOX * BOX)
        settled, bending = evolve_boxes(level_box[None], motion)
        return (settled[0], bending[0])
    settled, bending = lax.map(one_box, (box_level, anchor_x, anchor_y, anchor_z))
    settled = settled * alive_mask[:, None, None]
    bending = bending * alive_mask[:, None, None]
    predictor = velocity + grid_step * tendency(wrap_pad(velocity))
    second = predictor + grid_step * tendency(wrap_pad(predictor))
    stepped = 0.5 * (velocity + second)

    def deposit(slot_no, grid_now):
        push_box = surface_force(settled[slot_no][None], bending[slot_no][None])[0].reshape(3, BOX, BOX, BOX)
        corner_at = (nought, anchor_x[slot_no], anchor_y[slot_no], anchor_z[slot_no])
        region = lax.dynamic_slice(grid_now, corner_at, (3, BOX, BOX, BOX))
        return lax.dynamic_update_slice(grid_now, region + grid_step * push_box, corner_at)
    result = lax.fori_loop(0, SLOTS_ALL, deposit, stepped)
    return (result, settled, bending)
```

```python
import functools
import math

import jax
import jax.numpy as jnp
from jax import lax
from jax.experimental import pallas as pl
from jax.experimental.pallas import tpu as pltpu
from jax.sharding import PartitionSpec as P

ITERS = 12
BOX = 16
LANES = 128
PER = 8

box_step = 0.25
pseudo_step = 0.3
weno_floor = 1e-06
band_width = 1.5
tension = 2.0
grid_step = 0.2
viscosity = 0.1
normal_floor = 0.5

F32 = jnp.float32
TILE = (8, LANES)


def iotas():
    row = lax.broadcasted_iota(jnp.int32, TILE, 0)
    lane = lax.broadcasted_iota(jnp.int32, TILE, 1)
    return row, lane


def block_transpose(x, row, lane):
    block = lane // BOX
    for s in (4, 2, 1):
        r_bit = (row // s) % 2
        q_bit = (block // s) % 2
        down = pltpu.roll(pltpu.roll(x, s, 0), LANES - BOX * s, 1)
        if s == 4:
            moved = down
        else:
            up = pltpu.roll(pltpu.roll(x, 8 - s, 0), BOX * s, 1)
            moved = jnp.where(r_bit == 1, down, up)
        x = jnp.where(r_bit == q_bit, x, moved)
    return x


def weno(a, b, c, e, f):
    ab, bc, ce, ef = a - b, b - c, c - e, e - f
    d1, d2, d3 = ab - bc, bc - ce, ce - ef
    bc2, ce2 = bc + bc, ce + ce
    t1, t2, t3 = d1 - bc2, bc + ce, d3 + ce2
    part = 3.0 / 13.0
    floor = weno_floor * 12.0 / 13.0
    s1 = (d1 * d1 + floor) + part * (t1 * t1)
    s2 = (d2 * d2 + floor) + part * (t2 * t2)
    s3 = (d3 * d3 + floor) + part * (t3 * t3)
    q1, q2, q3 = s1 * s1, s2 * s2, s3 * s3
    w1 = q2 * q3
    w2 = 6.0 * (q1 * q3)
    w3 = 3.0 * (q1 * q2)
    top = w1 * ((ab + ab) - 5.0 * bc) - w2 * (bc + ce2) + w3 * (ef - (ce2 + ce2))
    return c + top / (6.0 * (w1 + w2 + w3))


def upwind(speed, back_two, back_one, here, ahead_one, ahead_two, ahead_three):
    pos = speed > 0.0
    return speed * weno(
        jnp.where(pos, back_two, ahead_three),
        jnp.where(pos, back_one, ahead_two),
        jnp.where(pos, here, ahead_one),
        jnp.where(pos, ahead_one, here),
        jnp.where(pos, ahead_two, back_one),
    )


ROWS = 32


def box_body(
    groups,
    first,
    owner_ref,
    corner_ref,
    vel_ref,
    level_lo,
    level_hi,
    *rest,
):
    if first:
        (force_out, settled_out, bending_out, *scratch) = rest
    else:
        (_, force_in, _, _, force_out, settled_out, bending_out, *scratch) = rest
    (u_ref, l_ref, mi_ref, mj_ref, pa, pb, c_ref, s_ref, k_ref, turned_s, turned_b) = scratch
    row, lane = iotas()
    k = lane % BOX
    block = lane // BOX
    k_first, k_last = k == 0, k == BOX - 1
    top, bottom = row == 0, row == 7

    if first:

        @pl.loop(0, 32)
        def _(x):
            for c in range(3):
                force_out[c, x] = jnp.zeros((32, LANES), F32)
    else:

        @pl.loop(0, 32)
        def _(x):
            for c in range(3):
                force_out[c, x] = force_in[c, x]

    def next_k(v):
        return jnp.where(k_last, v, pltpu.roll(v, LANES - 1, 1))

    def prev_k(v):
        return jnp.where(k_first, v, pltpu.roll(v, 1, 1))

    def one_group(g):
        spots = [
            [corner_ref[g * PER + b, d] for d in range(3)] for b in range(PER)
        ]
        alive = jnp.zeros(TILE, F32)
        for b in range(PER):
            living = jnp.where(owner_ref[g * PER + b] >= 0, 1.0, 0.0)
            alive = jnp.where(block == b, living, alive)

        @pl.loop(0, BOX)
        def _(i):
            for jt in range(2):
                for c in range(3):
                    total = jnp.zeros(TILE, F32)
                    for b in range(PER):
                        px, py, pz = spots[b]
                        part = vel_ref[c, px + i, pl.ds(py + 8 * jt, 8), :]
                        part = pltpu.roll(part, (BOX * b + LANES - pz) % LANES, 1)
                        total = part if b == 0 else jnp.where(block == b, part, total)
                    u_ref[c, i, pl.ds(8 * jt, 8), :] = total
                level = (level_lo, level_hi)[jt]
                x = level[pl.ds(g * (PER * BOX) + i, 8, stride=BOX), :]
                l_ref[i, pl.ds(8 + 8 * jt, 8), :] = block_transpose(x, row, lane)

        mi_ref[0] = jnp.zeros((BOX, LANES), F32)
        mi_ref[1] = jnp.zeros((BOX, LANES), F32)
        mi_ref[2] = jnp.zeros((BOX, LANES), F32)

        @pl.loop(1, BOX)
        def _(i):
            for jt in range(2):
                at = pl.ds(8 + 8 * jt, 8)
                mi_ref[i + 2, pl.ds(8 * jt, 8), :] = l_ref[i, at, :] - l_ref[i - 1, at, :]

        for t in range(3):
            mi_ref[18 + t] = mi_ref[17]

        @pl.loop(0, BOX)
        def _(i):
            for jt in range(2):
                here = l_ref[i, pl.ds(8 + 8 * jt, 8), :]
                m = here - l_ref[i, pl.ds(7 + 8 * jt, 8), :]
                if jt == 0:
                    m = jnp.where(top, 0.0, m)
                    mj_ref[i, pl.ds(0, 8), :] = jnp.zeros(TILE, F32)
                else:
                    mj_ref[i, pl.ds(24, 8), :] = jnp.broadcast_to(m[7:8, :], TILE)
                mj_ref[i, pl.ds(8 + 8 * jt, 8), :] = m

        @pl.loop(0, BOX)
        def _(i):
            for jt in range(2):
                at = pl.ds(8 * jt, 8)
                padded_at = pl.ds(8 + 8 * jt, 8)
                here = l_ref[i, padded_at, :]
                change = upwind(u_ref[0, i, at, :], *[mi_ref[i + t, at, :] for t in range(6)])
                change += upwind(
                    u_ref[1, i, at, :],
                    *[mj_ref[i, pl.ds(6 + t + 8 * jt, 8), :] for t in range(6)],
                )
                m = here - prev_k(here)
                back_one = prev_k(m)
                ahead_one = next_k(m)
                ahead_two = next_k(ahead_one)
                change += upwind(
                    u_ref[2, i, at, :],
                    prev_k(back_one),
                    back_one,
                    m,
                    ahead_one,
                    ahead_two,
                    next_k(ahead_two),
                )
                advected = here - box_step * change
                pa[i, padded_at, :] = advected
                c_ref[i, at, :] = pseudo_step * advected * lax.rsqrt(advected * advected + 1.0)
                s_ref[i, at, :] = jnp.where(advected > 0.0, 1.0, -1.0)

        def sweep(src, dst):
            for jt in range(2):
                at = pl.ds(8 * jt, 8)
                behind_i = None
                cur = src[0, pl.ds(8 + 8 * jt, 8), :]
                for i in range(BOX):
                    s = s_ref[i, at, :]
                    terms = []
                    if i < BOX - 1:
                        nxt = src[i + 1, pl.ds(8 + 8 * jt, 8), :]
                        down_i = cur - nxt
                    else:
                        nxt = down_i = None
                    if behind_i is None:
                        terms.append(jnp.maximum(s * down_i, 0.0))
                    elif down_i is None:
                        terms.append(jnp.maximum(-(s * behind_i), 0.0))
                    else:
                        terms.append(
                            jnp.maximum(jnp.maximum(s * down_i, -(s * behind_i)), 0.0)
                        )
                    below = cur - src[i, pl.ds(7 + 8 * jt, 8), :]
                    above = cur - src[i, pl.ds(9 + 8 * jt, 8), :]
                    if jt == 0:
                        below = jnp.where(top, 0.0, below)
                    else:
                        above = jnp.where(bottom, 0.0, above)
                    terms.append(jnp.maximum(jnp.maximum(s * below, s * above), 0.0))
                    down_k = jnp.where(k_last, 0.0, cur - pltpu.roll(cur, LANES - 1, 1))
                    up_k = pltpu.roll(down_k, 1, 1)
                    terms.append(jnp.maximum(jnp.maximum(s * down_k, -(s * up_k)), 0.0))
                    squared = terms[0] * terms[0] + terms[1] * terms[1] + terms[2] * terms[2]
                    root = squared * lax.rsqrt(jnp.maximum(squared, 1e-37))
                    dst[i, pl.ds(8 + 8 * jt, 8), :] = cur - c_ref[i, at, :] * (root - 1.0)
                    behind_i, cur = down_i, nxt

        @pl.loop(0, ITERS // 2)
        def _(_):
            sweep(pa, pb)
            sweep(pb, pa)

        def central(i, jt):
            at = pl.ds(8 + 8 * jt, 8)
            cur = pa[i, at, :]
            c0 = 0.5 * (pa[jnp.minimum(i + 1, BOX - 1), at, :] - pa[jnp.maximum(i - 1, 0), at, :])
            lower = pa[i, pl.ds(7 + 8 * jt, 8), :]
            upper = pa[i, pl.ds(9 + 8 * jt, 8), :]
            if jt == 0:
                lower = jnp.where(top, cur, lower)
            else:
                upper = jnp.where(bottom, cur, upper)
            c1 = 0.5 * (upper - lower)
            c2 = 0.5 * (next_k(cur) - prev_k(cur))
            return cur, c0, c1, c2

        @pl.loop(0, BOX)
        def _(i):
            for jt in range(2):
                cur, c0, c1, c2 = central(i, jt)
                size = c0 * c0 + c1 * c1 + c2 * c2
                inverse = jnp.minimum(lax.rsqrt(size), 1.0 / normal_floor)
                at = pl.ds(8 * jt, 8)
                mi_ref[i, at, :] = c0 * inverse
                mj_ref[i, pl.ds(8 + 8 * jt, 8), :] = c1 * inverse
                n3 = c2 * inverse
                k_ref[i, at, :] = next_k(n3) - prev_k(n3)
                scaled = cur * (1.0 / band_width)
                band = jnp.exp(-(scaled * scaled)) * (
                    grid_step * tension / (band_width * math.sqrt(math.pi))
                )
                band = band * alive
                u_ref[0, i, at, :] = band * c0
                u_ref[1, i, at, :] = band * c1
                u_ref[2, i, at, :] = band * c2
                y = block_transpose(cur * alive, row, lane)
                turned_s[pl.ds(jt * (PER * BOX) + i, 8, stride=BOX), :] = y

        @pl.loop(0, BOX)
        def _(i):
            for jt in range(2):
                at = pl.ds(8 * jt, 8)
                padded_at = pl.ds(8 + 8 * jt, 8)
                d1 = mi_ref[jnp.minimum(i + 1, BOX - 1), at, :] - mi_ref[jnp.maximum(i - 1, 0), at, :]
                lower = mj_ref[i, pl.ds(7 + 8 * jt, 8), :]
                upper = mj_ref[i, pl.ds(9 + 8 * jt, 8), :]
                if jt == 0:
                    lower = jnp.where(top, mj_ref[i, padded_at, :], lower)
                else:
                    upper = jnp.where(bottom, mj_ref[i, padded_at, :], upper)
                kappa = 0.5 * (d1 + (upper - lower) + k_ref[i, at, :])
                for c in range(3):
                    u_ref[c, i, at, :] = u_ref[c, i, at, :] * kappa
                y = block_transpose(kappa * alive, row, lane)
                turned_b[pl.ds(jt * (PER * BOX) + i, 8, stride=BOX), :] = y

        for jt in range(2):
            here = pl.ds(jt * (PER * BOX), PER * BOX)
            there = pl.ds(pl.multiple_of(g * (PER * BOX), PER * BOX), PER * BOX)
            settled_out[there, pl.ds(LANES * jt, LANES)] = turned_s[here, :]
            bending_out[there, pl.ds(LANES * jt, LANES)] = turned_b[here, :]

        for b in range(PER):
            px, py, pz = spots[b]
            inside = (lane >= pz) & (lane < pz + BOX)
            turn = (pz + LANES - BOX * b) % LANES

            @pl.loop(0, 3 * BOX // 8)
            def _(step):
                c = step // 2
                i0 = (step % 2) * 8
                sums = []
                for i in range(8):
                    for jt in range(2):
                        old = force_out[c, px + i0 + i, pl.ds(py + 8 * jt, 8), :]
                        push = pltpu.roll(u_ref[c, i0 + i, pl.ds(8 * jt, 8), :], turn, 1)
                        sums.append(old + jnp.where(inside, push, 0.0))
                for i in range(8):
                    for jt in range(2):
                        force_out[c, px + i0 + i, pl.ds(py + 8 * jt, 8), :] = sums[2 * i + jt]

    @pl.loop(groups[0], groups[1])
    def _(g):
        one_group(g)


def boxes(groups, owner, corners, velocity, level_rows, carried=None):
    first = carried is None
    smem = pl.BlockSpec(memory_space=pltpu.SMEM)
    vmem = pl.BlockSpec(memory_space=pltpu.VMEM)
    halves = [
        pl.BlockSpec((level_rows.shape[0], LANES), functools.partial(lambda h, s: (0, h), h))
        for h in range(2)
    ]
    whole = pl.BlockSpec(velocity.shape, lambda s: (0, 0, 0, 0))
    rows = pl.BlockSpec(level_rows.shape, lambda s: (0, 0))
    any_ = pl.BlockSpec(memory_space=pl.ANY)
    specs = [smem, smem, whole, *halves]
    operands = [owner, corners, velocity, level_rows, level_rows]
    plane = lambda *lead: pltpu.VMEM((*lead, LANES), F32)
    return pl.pallas_call(
        functools.partial(box_body, groups, first),
        grid=(1,),
        out_shape=(
            jax.ShapeDtypeStruct(velocity.shape, F32),
            jax.ShapeDtypeStruct(level_rows.shape, F32),
            jax.ShapeDtypeStruct(level_rows.shape, F32),
        ),
        in_specs=specs,
        out_specs=(whole, rows, rows),
        scratch_shapes=[
            plane(3, BOX, BOX),
            plane(BOX, ROWS),
            plane(BOX + 5, BOX),
            plane(BOX, ROWS),
            plane(BOX, ROWS),
            plane(BOX, ROWS),
            plane(BOX, BOX),
            plane(BOX, BOX),
            plane(BOX, BOX),
            plane(2 * PER * BOX),
            plane(2 * PER * BOX),
        ],
        compiler_params=pltpu.CompilerParams(vmem_limit_bytes=32 * 2**20),
        cost_estimate=pl.CostEstimate(flops=60_000_000, bytes_accessed=5_000_000, transcendentals=0),
        name="boxes",
    )(*operands)


PLANE = 48


def take_faces(load, faces):
    xlo, xhi, ylo, yhi, zlo, zhi = faces
    row, lane = iotas()

    def one(x, packed):
        out = []
        for c in range(3):
            lo, hi = packed[2 * c], packed[2 * c + 1]
            for yt in range(4):
                n = x * 4 + yt
                turned = pltpu.roll(load(c, x, yt), n, 1)
                lo = jnp.where(lane == n, turned, lo)
                hi = jnp.where(lane == (n + LANES - 1) % LANES, turned, hi)
            out += [lo, hi]
        return tuple(out)

    packed = lax.fori_loop(0, 32, one, (jnp.zeros(TILE, F32),) * 6)
    for c in range(3):
        zlo[c] = packed[2 * c]
        zhi[c] = packed[2 * c + 1]


def faces_body(vel_ref, *faces):
    xlo, xhi, ylo, yhi, _, _ = faces
    for c in range(3):
        xlo[c] = vel_ref[pl.ds(c * 1024, 32), :]
        xhi[c] = vel_ref[pl.ds(c * 1024 + 31 * 32, 32), :]
        ylo[c] = vel_ref[pl.ds(c * 1024, 32, stride=32), :]
        yhi[c] = vel_ref[pl.ds(c * 1024 + 31, 32, stride=32), :]
    take_faces(
        lambda c, x, yt: vel_ref[pl.ds(pl.multiple_of(c * 1024 + x * 32 + 8 * yt, 8), 8), :],
        faces,
    )


FACES = tuple([(3, 32, LANES)] * 4 + [(3, 8, LANES)] * 2)


def faces_of(rows):
    vmem = pl.BlockSpec(memory_space=pltpu.VMEM)
    return pl.pallas_call(
        faces_body,
        out_shape=tuple(jax.ShapeDtypeStruct(s, F32) for s in FACES),
        in_specs=[vmem],
        out_specs=(vmem,) * 6,
        compiler_params=pltpu.CompilerParams(vmem_limit_bytes=16 * 2**20),
        name="faces",
    )(rows)


def exchange(faces):
    halos = []
    for d, axis in enumerate(("gx", "gy", "gz")):
        size = lax.axis_size(axis)
        up = [(i, (i + 1) % size) for i in range(size)]
        down = [(j, i) for i, j in up]
        halos.append(lax.ppermute(faces[2 * d + 1], axis, up))
        halos.append(lax.ppermute(faces[2 * d], axis, down))
    return halos


def fill_padded(src_ref, halos, ext):
    xlo, xhi, ylo, yhi, _, _ = halos
    for c in range(3):
        base = c * 34 * PLANE
        ext[pl.ds(base + 8, 32), :] = xlo[c]
        ext[pl.ds(base + 33 * PLANE + 8, 32), :] = xhi[c]
        ext[pl.ds(base + PLANE + 7, 32, stride=PLANE), :] = ylo[c]
        ext[pl.ds(base + PLANE + 40, 32, stride=PLANE), :] = yhi[c]

    @pl.loop(0, 32)
    def _(x):
        for c in range(3):
            at = pl.multiple_of(c * 34 * PLANE + (x + 1) * PLANE + 8, 8)
            ext[pl.ds(at, 32), :] = src_ref[pl.ds(pl.multiple_of(c * 1024 + x * 32, 8), 32), :]


def tendencies(ext, zlo, zhi, x, yt, lane):
    n = x * 4 + yt
    at = [
        pl.multiple_of(c * 34 * PLANE + (x + 1) * PLANE + 8 + 8 * yt, 8) for c in range(3)
    ]
    centre = [ext[pl.ds(at[c], 8), :] for c in range(3)]
    out = []
    for c in range(3):
        v = centre[c]
        up0 = ext[pl.ds(at[c] + PLANE, 8), :]
        lo0 = ext[pl.ds(at[c] - PLANE, 8), :]
        up1 = ext[pl.ds(at[c] + 1, 8), :]
        lo1 = ext[pl.ds(at[c] - 1, 8), :]
        lo2 = jnp.where(
            lane == 0, pltpu.roll(zlo[c], (LANES + 1 - n) % LANES, 1), pltpu.roll(v, 1, 1)
        )
        up2 = jnp.where(
            lane == LANES - 1,
            pltpu.roll(zhi[c], LANES - 1 - n, 1),
            pltpu.roll(v, LANES - 1, 1),
        )
        advect = centre[0] * (up0 - lo0) + centre[1] * (up1 - lo1) + centre[2] * (up2 - lo2)
        spread = (up0 + lo0) + (up1 + lo1) + (up2 + lo2) - 6.0 * v
        out.append(viscosity * spread - 0.5 * advect)
    return centre, out


def predictor_body(vel_ref, *refs):
    halos, out_ref, faces, ext = refs[:6], refs[6], refs[7:13], refs[13]
    fill_padded(vel_ref, halos, ext)
    row, lane = iotas()
    zlo, zhi = halos[4], halos[5]

    @pl.loop(0, 32)
    def _(x):
        zl = [zlo[c] for c in range(3)]
        zh = [zhi[c] for c in range(3)]
        for yt in range(4):
            centre, f = tendencies(ext, zl, zh, x, yt, lane)
            for c in range(3):
                out_ref[pl.ds(pl.multiple_of(c * 1024 + x * 32 + 8 * yt, 8), 8), :] = (
                    centre[c] + grid_step * f[c]
                )

    faces_body(out_ref, *faces)


def predictor_of(rows, halos):
    vmem = pl.BlockSpec(memory_space=pltpu.VMEM)
    return pl.pallas_call(
        predictor_body,
        out_shape=(
            jax.ShapeDtypeStruct(rows.shape, F32),
            *(jax.ShapeDtypeStruct(s, F32) for s in FACES),
        ),
        in_specs=[vmem] * 7,
        out_specs=(vmem,) * 7,
        scratch_shapes=[pltpu.VMEM((3 * 34 * PLANE, LANES), F32)],
        compiler_params=pltpu.CompilerParams(vmem_limit_bytes=24 * 2**20),
        name="predictor",
    )(rows, *halos)


def final_body(vel_ref, pred_ref, force_ref, *refs):
    halos, out_ref, ext = refs[:6], refs[6], refs[7]
    fill_padded(pred_ref, halos, ext)
    row, lane = iotas()
    zlo, zhi = halos[4], halos[5]

    @pl.loop(0, 32)
    def _(x):
        zl = [zlo[c] for c in range(3)]
        zh = [zhi[c] for c in range(3)]
        for yt in range(4):
            centre, f = tendencies(ext, zl, zh, x, yt, lane)
            for c in range(3):
                at = pl.ds(pl.multiple_of(c * 1024 + x * 32 + 8 * yt, 8), 8)
                second = centre[c] + grid_step * f[c]
                out_ref[at, :] = 0.5 * (vel_ref[at, :] + second) + force_ref[at, :]


def final_of(rows, predictor, force, halos):
    vmem = pl.BlockSpec(memory_space=pltpu.VMEM)
    return pl.pallas_call(
        final_body,
        out_shape=jax.ShapeDtypeStruct(rows.shape, F32),
        in_specs=[vmem] * 9,
        out_specs=vmem,
        scratch_shapes=[pltpu.VMEM((3 * 34 * PLANE, LANES), F32)],
        compiler_params=pltpu.CompilerParams(vmem_limit_bytes=24 * 2**20),
        name="final",
    )(rows, predictor, force, *halos)


def local(velocity, box_level, corners, owner_list):
    slots = box_level.shape[0]
    rows = velocity.reshape(-1, LANES)
    level_rows = box_level.reshape(slots * BOX, BOX * BOX)
    halos = exchange(faces_of(rows))
    force, settled, bending = boxes((0, slots // PER), owner_list, corners, velocity, level_rows)
    predictor, *faces = predictor_of(rows, halos)
    halos = exchange(faces)
    result = final_of(rows, predictor, force.reshape(rows.shape), halos)
    return (
        result.reshape(velocity.shape),
        settled.reshape(box_level.shape),
        bending.reshape(box_level.shape),
    )


def solution(mesh):
    placed = (
        P(None, "gx", "gy", "gz"),
        P(("gx", "gy", "gz"), None, None),
        P(("gx", "gy", "gz"), None),
        P(("gx", "gy", "gz")),
    )
    return jax.shard_map(
        local,
        mesh=mesh,
        in_specs=placed,
        out_specs=(
            P(None, "gx", "gy", "gz"),
            P(("gx", "gy", "gz"), None, None),
            P(("gx", "gy", "gz"), None, None),
        ),
        check_vma=False,
    )
```

```python
import functools
import math

import jax
import jax.numpy as jnp
from jax import lax
from jax.experimental import pallas as pl
from jax.experimental.pallas import tpu as pltpu
from jax.sharding import PartitionSpec as P

ITERS = 12
BOX = 16
LANES = 128
PER = 8

CUT, LEVEL, MI, MJ, WENO, CENTRAL, KAPPA, DEPOSIT, PLANES = 6, 8, 5, 4, 8, 8, 8, 6, 4

box_step = 0.25
pseudo_step = 0.3
weno_floor = 1e-06
band_width = 1.5
tension = 2.0
grid_step = 0.2
viscosity = 0.1
normal_floor = 0.5

F32 = jnp.float32
TILE = (8, LANES)


def iotas():
    row = lax.broadcasted_iota(jnp.int32, TILE, 0)
    lane = lax.broadcasted_iota(jnp.int32, TILE, 1)
    return row, lane


def block_transpose(x, row, lane):
    block = lane // BOX
    x = jnp.take_along_axis(x, (lane - BOX * row) % LANES, axis=1)
    x = jnp.take_along_axis(x, (block - row) % 8, axis=0)
    return jnp.take_along_axis(x, (lane + BOX * row) % LANES, axis=1)


def weno(a, b, c, e, f):
    ab, bc, ce, ef = a - b, b - c, c - e, e - f
    d1, d2, d3 = ab - bc, bc - ce, ce - ef
    bc2, ce2 = bc + bc, ce + ce
    t1, t2, t3 = d1 - bc2, bc + ce, d3 + ce2
    part = 3.0 / 13.0
    floor = weno_floor * 12.0 / 13.0
    s1 = (d1 * d1 + floor) + part * (t1 * t1)
    s2 = (d2 * d2 + floor) + part * (t2 * t2)
    s3 = (d3 * d3 + floor) + part * (t3 * t3)
    q1, q2, q3 = s1 * s1, s2 * s2, s3 * s3
    w1 = q2 * q3
    w2 = 6.0 * (q1 * q3)
    w3 = 3.0 * (q1 * q2)
    top = w1 * ((ab + ab) - 5.0 * bc) - w2 * (bc + ce2) + w3 * (ef - (ce2 + ce2))
    return c + top / (6.0 * (w1 + w2 + w3))


def upwind(speed, back_two, back_one, here, ahead_one, ahead_two, ahead_three):
    pos = speed > 0.0
    return speed * weno(
        jnp.where(pos, back_two, ahead_three),
        jnp.where(pos, back_one, ahead_two),
        jnp.where(pos, here, ahead_one),
        jnp.where(pos, ahead_one, here),
        jnp.where(pos, ahead_two, back_one),
    )


ROWS = 32


def box_body(first_group, count, owner_ref, corner_ref, vel_ref, level_lo, level_hi, *rest):
    (force_out, settled_out, bending_out, *scratch) = rest[-15:]
    (u_ref, l_ref, mi_ref, mj_ref, pa, pb, c_ref, s_ref, k_ref) = scratch[:9]
    turned, turned_kappa, sems = scratch[9], scratch[10], scratch[11]
    row, lane = iotas()
    k = lane % BOX
    block = lane // BOX
    k_first, k_last = k == 0, k == BOX - 1
    top, bottom = row == 0, row == 7

    def next_k(v):
        return jnp.where(k_last, v, pltpu.roll(v, LANES - 1, 1))

    def prev_k(v):
        return jnp.where(k_first, v, pltpu.roll(v, 1, 1))

    def one_group(own):
        g = first_group + own
        spots = [[corner_ref[g * PER + b, d] for d in range(3)] for b in range(PER)]
        alive = jnp.zeros(TILE, F32)
        for b in range(PER):
            living = jnp.where(owner_ref[g * PER + b] >= 0, 1.0, 0.0)
            alive = jnp.where(block == b, living, alive)

        for b in range(PER):
            px, py, pz = spots[b]
            turn = (BOX * b + LANES - pz) % LANES
            here = block == b

            @pl.loop(0, 6, unroll=CUT)
            def _(step):
                c = step // 2
                i0 = (step % 2) * 8
                for i in range(8):
                    for jt in range(2):
                        part = vel_ref[c, px + i0 + i, pl.ds(py + 8 * jt, 8), :]
                        pltpu.store(
                            u_ref.at[c, i0 + i, pl.ds(8 * jt, 8), :],
                            pltpu.roll(part, turn, 1),
                            mask=here,
                        )

        @pl.loop(0, BOX, unroll=LEVEL)
        def _(i):
            for jt in range(2):
                level = (level_lo, level_hi)[jt]
                x = level[pl.ds(own * (PER * BOX) + i, 8, stride=BOX), :]
                l_ref[i, pl.ds(8 + 8 * jt, 8), :] = block_transpose(x, row, lane)

        mi_ref[0] = jnp.zeros((BOX, LANES), F32)
        mi_ref[1] = jnp.zeros((BOX, LANES), F32)
        mi_ref[2] = jnp.zeros((BOX, LANES), F32)

        @pl.loop(1, BOX, unroll=MI)
        def _(i):
            for jt in range(2):
                at = pl.ds(8 + 8 * jt, 8)
                mi_ref[i + 2, pl.ds(8 * jt, 8), :] = l_ref[i, at, :] - l_ref[i - 1, at, :]

        for t in range(3):
            mi_ref[18 + t] = mi_ref[17]

        @pl.loop(0, BOX, unroll=MJ)
        def _(i):
            for jt in range(2):
                here = l_ref[i, pl.ds(8 + 8 * jt, 8), :]
                m = here - l_ref[i, pl.ds(7 + 8 * jt, 8), :]
                if jt == 0:
                    m = jnp.where(top, 0.0, m)
                    mj_ref[i, pl.ds(0, 8), :] = jnp.zeros(TILE, F32)
                else:
                    mj_ref[i, pl.ds(24, 8), :] = jnp.broadcast_to(m[7:8, :], TILE)
                mj_ref[i, pl.ds(8 + 8 * jt, 8), :] = m

        @pl.loop(0, BOX, unroll=WENO)
        def _(i):
            for jt in range(2):
                at = pl.ds(8 * jt, 8)
                padded_at = pl.ds(8 + 8 * jt, 8)
                here = l_ref[i, padded_at, :]
                change = upwind(u_ref[0, i, at, :], *[mi_ref[i + t, at, :] for t in range(6)])
                change += upwind(
                    u_ref[1, i, at, :],
                    *[mj_ref[i, pl.ds(6 + t + 8 * jt, 8), :] for t in range(6)],
                )
                m = here - prev_k(here)
                back_one = prev_k(m)
                ahead_one = next_k(m)
                ahead_two = next_k(ahead_one)
                change += upwind(
                    u_ref[2, i, at, :],
                    prev_k(back_one),
                    back_one,
                    m,
                    ahead_one,
                    ahead_two,
                    next_k(ahead_two),
                )
                advected = here - box_step * change
                pa[i, padded_at, :] = advected
                c_ref[i, at, :] = pseudo_step * advected * lax.rsqrt(advected * advected + 1.0)
                s_ref[i, at, :] = jnp.where(advected > 0.0, 1.0, -1.0)

        def sweep(src, dst):
            for jt in range(2):
                at = pl.ds(8 * jt, 8)
                behind_i = None
                cur = src[0, pl.ds(8 + 8 * jt, 8), :]
                for i in range(BOX):
                    s = s_ref[i, at, :]
                    terms = []
                    if i < BOX - 1:
                        nxt = src[i + 1, pl.ds(8 + 8 * jt, 8), :]
                        down_i = cur - nxt
                    else:
                        nxt = down_i = None
                    if behind_i is None:
                        terms.append(jnp.maximum(s * down_i, 0.0))
                    elif down_i is None:
                        terms.append(jnp.maximum(-(s * behind_i), 0.0))
                    else:
                        terms.append(
                            jnp.maximum(jnp.maximum(s * down_i, -(s * behind_i)), 0.0)
                        )
                    below = cur - src[i, pl.ds(7 + 8 * jt, 8), :]
                    above = cur - src[i, pl.ds(9 + 8 * jt, 8), :]
                    if jt == 0:
                        below = jnp.where(top, 0.0, below)
                    else:
                        above = jnp.where(bottom, 0.0, above)
                    terms.append(jnp.maximum(jnp.maximum(s * below, s * above), 0.0))
                    down_k = jnp.where(k_last, 0.0, cur - pltpu.roll(cur, LANES - 1, 1))
                    up_k = pltpu.roll(down_k, 1, 1)
                    terms.append(jnp.maximum(jnp.maximum(s * down_k, -(s * up_k)), 0.0))
                    squared = terms[0] * terms[0] + terms[1] * terms[1] + terms[2] * terms[2]
                    root = squared * lax.rsqrt(jnp.maximum(squared, 1e-37))
                    dst[i, pl.ds(8 + 8 * jt, 8), :] = cur - c_ref[i, at, :] * (root - 1.0)
                    behind_i, cur = down_i, nxt

        @pl.loop(0, ITERS // 2)
        def _(_):
            sweep(pa, pb)
            sweep(pb, pa)

        def central(i, jt):
            at = pl.ds(8 + 8 * jt, 8)
            cur = pa[i, at, :]
            c0 = 0.5 * (pa[jnp.minimum(i + 1, BOX - 1), at, :] - pa[jnp.maximum(i - 1, 0), at, :])
            lower = pa[i, pl.ds(7 + 8 * jt, 8), :]
            upper = pa[i, pl.ds(9 + 8 * jt, 8), :]
            if jt == 0:
                lower = jnp.where(top, cur, lower)
            else:
                upper = jnp.where(bottom, cur, upper)
            c1 = 0.5 * (upper - lower)
            c2 = 0.5 * (next_k(cur) - prev_k(cur))
            return cur, c0, c1, c2

        @pl.loop(0, BOX, unroll=CENTRAL)
        def _(i):
            for jt in range(2):
                cur, c0, c1, c2 = central(i, jt)
                size = c0 * c0 + c1 * c1 + c2 * c2
                inverse = jnp.minimum(lax.rsqrt(size), 1.0 / normal_floor)
                at = pl.ds(8 * jt, 8)
                mi_ref[i, at, :] = c0 * inverse
                mj_ref[i, pl.ds(8 + 8 * jt, 8), :] = c1 * inverse
                n3 = c2 * inverse
                k_ref[i, at, :] = next_k(n3) - prev_k(n3)
                scaled = cur * (1.0 / band_width)
                band = jnp.exp(-(scaled * scaled)) * (
                    grid_step * tension / (band_width * math.sqrt(math.pi))
                )
                band = band * alive
                for c, slope in enumerate((c0, c1, c2)):
                    force_out[own, c, i, at, :] = band * slope
                y = block_transpose(cur * alive, row, lane)
                turned[pl.ds((own * 2 + jt) * (PER * BOX) + i, 8, stride=BOX), :] = y

        @pl.loop(0, BOX, unroll=KAPPA)
        def _(i):
            for jt in range(2):
                at = pl.ds(8 * jt, 8)
                padded_at = pl.ds(8 + 8 * jt, 8)
                d1 = mi_ref[jnp.minimum(i + 1, BOX - 1), at, :] - mi_ref[jnp.maximum(i - 1, 0), at, :]
                lower = mj_ref[i, pl.ds(7 + 8 * jt, 8), :]
                upper = mj_ref[i, pl.ds(9 + 8 * jt, 8), :]
                if jt == 0:
                    lower = jnp.where(top, mj_ref[i, padded_at, :], lower)
                else:
                    upper = jnp.where(bottom, mj_ref[i, padded_at, :], upper)
                kappa = 0.5 * (d1 + (upper - lower) + k_ref[i, at, :])
                for c in range(3):
                    force_out[own, c, i, at, :] = force_out[own, c, i, at, :] * kappa
                y = block_transpose(kappa * alive, row, lane)
                turned_kappa[pl.ds((own * 2 + jt) * (PER * BOX) + i, 8, stride=BOX), :] = y

        for copy in sent(own):
            copy.start()

    def sent(own):
        copies = []
        for n, (src, dst) in enumerate(((turned, settled_out), (turned_kappa, bending_out))):
            for jt in range(2):
                rows = (first_group + own) * (PER * BOX)
                copies.append(
                    pltpu.make_async_copy(
                        src.at[pl.ds((own * 2 + jt) * (PER * BOX), PER * BOX), :],
                        dst.at[pl.ds(rows, PER * BOX), pl.ds(LANES * jt, LANES)],
                        sems.at[own, 2 * n + jt],
                    )
                )
        return copies

    @pl.loop(0, count)
    def _(own):
        one_group(own)

    for own in range(count):
        for copy in sent(own):
            copy.wait()


def boxes(first_group, count, owner, corners, velocity, level_rows, after, carried=()):
    smem = pl.BlockSpec(memory_space=pltpu.SMEM)
    any_ = pl.BlockSpec(memory_space=pl.ANY)
    vmem = pl.BlockSpec(memory_space=pltpu.VMEM)
    halves = [
        pl.BlockSpec(
            (count * PER * BOX, LANES),
            functools.partial(lambda h, s: (first_group // count, h), h),
        )
        for h in range(2)
    ]
    whole = pl.BlockSpec(velocity.shape, lambda s: (0, 0, 0, 0))
    plane = lambda *lead: pltpu.VMEM((*lead, LANES), F32)
    force = (count, 3, BOX, BOX, LANES)
    operands = [owner, corners, velocity, level_rows, level_rows, after, *carried]
    return pl.pallas_call(
        functools.partial(box_body, first_group, count),
        grid=(1,),
        out_shape=(
            jax.ShapeDtypeStruct(force, F32),
            jax.ShapeDtypeStruct(level_rows.shape, F32),
            jax.ShapeDtypeStruct(level_rows.shape, F32),
        ),
        in_specs=[smem, smem, whole, *halves, any_] + [any_] * len(carried),
        out_specs=(pl.BlockSpec(force, lambda s: (0,) * 5), any_, any_),
        input_output_aliases={6: 1, 7: 2} if carried else {},
        scratch_shapes=[
            plane(3, BOX, BOX),
            plane(BOX, ROWS),
            plane(BOX + 5, BOX),
            plane(BOX, ROWS),
            plane(BOX, ROWS),
            plane(BOX, ROWS),
            plane(BOX, BOX),
            plane(BOX, BOX),
            plane(BOX, BOX),
            plane(count * 2 * PER * BOX),
            plane(count * 2 * PER * BOX),
            pltpu.SemaphoreType.DMA((count, 4)),
        ],
        compiler_params=pltpu.CompilerParams(vmem_limit_bytes=20 * 2**20),
        cost_estimate=pl.CostEstimate(
            flops=30_000_000, bytes_accessed=5_000_000, transcendentals=0
        ),
        name="boxes",
    )(*operands)


def deposit(force_refs, corner_ref, grid_ref):
    _, lane = iotas()

    def one_group(ref, own, g):
        for b in range(PER):
            px, py, pz = [corner_ref[g * PER + b, d] for d in range(3)]
            inside = (lane >= pz) & (lane < pz + BOX)
            turn = (pz + LANES - BOX * b) % LANES
            base = px * 32 + py

            @pl.loop(0, 6, unroll=DEPOSIT)
            def _(step):
                c = step // 2
                i0 = (step % 2) * 8
                sums = []
                for i in range(8):
                    for jt in range(2):
                        old = grid_ref[pl.ds(base + c * 1024 + (i0 + i) * 32 + 8 * jt, 8), :]
                        push = pltpu.roll(ref[own, c, i0 + i, pl.ds(8 * jt, 8), :], turn, 1)
                        sums.append(old + jnp.where(inside, push, 0.0))
                for i in range(8):
                    for jt in range(2):
                        grid_ref[pl.ds(base + c * 1024 + (i0 + i) * 32 + 8 * jt, 8), :] = sums[
                            2 * i + jt
                        ]

    done = 0
    for ref in force_refs:
        count = ref.shape[0]

        @pl.loop(0, count)
        def _(own):
            one_group(ref, own, done + own)

        done += count


PLANE = 48


def side_faces(rows_ref, xlo, xhi, ylo, yhi):
    for c in range(3):
        xlo[c] = rows_ref[pl.ds(c * 1024, 32), :]
        xhi[c] = rows_ref[pl.ds(c * 1024 + 31 * 32, 32), :]
        ylo[c] = rows_ref[pl.ds(c * 1024, 32, stride=32), :]
        yhi[c] = rows_ref[pl.ds(c * 1024 + 31, 32, stride=32), :]


def end_faces_body(rows_ref, zlo, zhi):
    _, lane = iotas()

    def one(x, packed):
        out = []
        for c in range(3):
            lo, hi = packed[2 * c], packed[2 * c + 1]
            for yt in range(4):
                n = x * 4 + yt
                at = pl.multiple_of(c * 1024 + x * 32 + 8 * yt, 8)
                turned = pltpu.roll(rows_ref[pl.ds(at, 8), :], n, 1)
                lo = jnp.where(lane == n, turned, lo)
                hi = jnp.where(lane == (n + LANES - 1) % LANES, turned, hi)
            out += [lo, hi]
        return tuple(out)

    packed = lax.fori_loop(0, 32, one, (jnp.zeros(TILE, F32),) * 6, unroll=PLANES)
    for c in range(3):
        zlo[c] = packed[2 * c]
        zhi[c] = packed[2 * c + 1]


SIDES = jax.ShapeDtypeStruct((3, 32, LANES), F32)
ENDS = jax.ShapeDtypeStruct((3, 8, LANES), F32)


def in_vmem(body, out_shape, operands, scratch=(), limit=16, name=None, smem=0):
    vmem = pl.BlockSpec(memory_space=pltpu.VMEM)
    return pl.pallas_call(
        body,
        out_shape=out_shape,
        in_specs=[vmem] * (len(operands) - smem) + [pl.BlockSpec(memory_space=pltpu.SMEM)] * smem,
        out_specs=jax.tree.map(lambda _: vmem, out_shape),
        scratch_shapes=scratch,
        compiler_params=pltpu.CompilerParams(vmem_limit_bytes=limit * 2**20),
        name=name,
    )(*operands)


def exchange(faces, axes):
    halos = []
    for d, axis in enumerate(axes):
        size = lax.axis_size(axis)
        up = [(i, (i + 1) % size) for i in range(size)]
        down = [(j, i) for i, j in up]
        halos.append(lax.ppermute(faces[2 * d + 1], axis, up))
        halos.append(lax.ppermute(faces[2 * d], axis, down))
    return halos


def fill_padded(src_ref, halos, ext):
    xlo, xhi, ylo, yhi, _, _ = halos
    for c in range(3):
        base = c * 34 * PLANE
        ext[pl.ds(base + 8, 32), :] = xlo[c]
        ext[pl.ds(base + 33 * PLANE + 8, 32), :] = xhi[c]
        ext[pl.ds(base + PLANE + 7, 32, stride=PLANE), :] = ylo[c]
        ext[pl.ds(base + PLANE + 40, 32, stride=PLANE), :] = yhi[c]

    @pl.loop(0, 32)
    def _(x):
        for c in range(3):
            at = pl.multiple_of(c * 34 * PLANE + (x + 1) * PLANE + 8, 8)
            ext[pl.ds(at, 32), :] = src_ref[pl.ds(pl.multiple_of(c * 1024 + x * 32, 8), 32), :]


def tendencies(ext, zlo, zhi, x, yt, lane):
    n = x * 4 + yt
    at = [
        pl.multiple_of(c * 34 * PLANE + (x + 1) * PLANE + 8 + 8 * yt, 8) for c in range(3)
    ]
    centre = [ext[pl.ds(at[c], 8), :] for c in range(3)]
    out = []
    for c in range(3):
        v = centre[c]
        up0 = ext[pl.ds(at[c] + PLANE, 8), :]
        lo0 = ext[pl.ds(at[c] - PLANE, 8), :]
        up1 = ext[pl.ds(at[c] + 1, 8), :]
        lo1 = ext[pl.ds(at[c] - 1, 8), :]
        lo2 = jnp.where(
            lane == 0, pltpu.roll(zlo[c], (LANES + 1 - n) % LANES, 1), pltpu.roll(v, 1, 1)
        )
        up2 = jnp.where(
            lane == LANES - 1,
            pltpu.roll(zhi[c], LANES - 1 - n, 1),
            pltpu.roll(v, LANES - 1, 1),
        )
        advect = centre[0] * (up0 - lo0) + centre[1] * (up1 - lo1) + centre[2] * (up2 - lo2)
        spread = (up0 + lo0) + (up1 + lo1) + (up2 + lo2) - 6.0 * v
        out.append(viscosity * spread - 0.5 * advect)
    return centre, out


PADDED = [pltpu.VMEM((3 * 34 * PLANE, LANES), F32)]


def stage(src_ref, halos, ext, write):
    fill_padded(src_ref, halos, ext)
    _, lane = iotas()
    zlo, zhi = halos[4], halos[5]

    @pl.loop(0, 32, unroll=PLANES)
    def _(x):
        zl = [zlo[c] for c in range(3)]
        zh = [zhi[c] for c in range(3)]
        for yt in range(4):
            centre, f = tendencies(ext, zl, zh, x, yt, lane)
            for c in range(3):
                at = pl.ds(pl.multiple_of(c * 1024 + x * 32 + 8 * yt, 8), 8)
                write(at, centre[c] + grid_step * f[c])


def predictor_body(vel_ref, *refs):
    halos, out_ref, sides, ext = refs[:6], refs[-6], refs[-5:-1], refs[-1]

    def write(at, value):
        out_ref[at, :] = value

    stage(vel_ref, halos, ext, write)
    side_faces(out_ref, *sides)


def final_body(vel_ref, pred_ref, *refs):
    halos, forces, corner_ref, out_ref, ext = refs[:6], refs[6:-3], refs[-3], refs[-2], refs[-1]

    def write(at, value):
        out_ref[at, :] = 0.5 * (vel_ref[at, :] + value)

    stage(pred_ref, halos, ext, write)
    deposit(forces, corner_ref, out_ref)


def local(velocity, box_level, corners, owner_list):
    slots = box_level.shape[0]
    rows = velocity.reshape(-1, LANES)
    level_rows = box_level.reshape(slots * BOX, BOX * BOX)
    half = slots // PER // 2
    sides = in_vmem(side_faces, (SIDES,) * 4, [rows], name="side_faces")
    halos = exchange(sides, ("gx", "gy"))
    ends = in_vmem(end_faces_body, (ENDS,) * 2, [rows], name="end_faces")
    halos += exchange(ends, ("gz",))
    force_a, settled, bending = boxes(
        0, half, owner_list, corners, velocity, level_rows, ends[0]
    )
    predictor, *sides = in_vmem(
        predictor_body,
        (jax.ShapeDtypeStruct(rows.shape, F32), *(SIDES,) * 4),
        [rows, *halos, force_a[0, 0, 0]],
        PADDED,
        24,
        "predictor",
    )
    halos = exchange(sides, ("gx", "gy"))
    ends = in_vmem(end_faces_body, (ENDS,) * 2, [predictor], name="end_faces")
    halos += exchange(ends, ("gz",))
    force_b, settled, bending = boxes(
        half, half, owner_list, corners, velocity, level_rows, ends[0], (settled, bending)
    )
    result = in_vmem(
        final_body,
        jax.ShapeDtypeStruct(rows.shape, F32),
        [rows, predictor, *halos, force_a, force_b, corners],
        PADDED,
        32,
        "final",
        smem=1,
    )
    return (
        result.reshape(velocity.shape),
        settled.reshape(box_level.shape),
        bending.reshape(box_level.shape),
    )


def solution(mesh):
    placed = (
        P(None, "gx", "gy", "gz"),
        P(("gx", "gy", "gz"), None, None),
        P(("gx", "gy", "gz"), None),
        P(("gx", "gy", "gz")),
    )
    return jax.shard_map(
        local,
        mesh=mesh,
        in_specs=placed,
        out_specs=(
            P(None, "gx", "gy", "gz"),
            P(("gx", "gy", "gz"), None, None),
            P(("gx", "gy", "gz"), None, None),
        ),
        check_vma=False,
    )
```

```python
import functools
import math

import jax
import jax.numpy as jnp
from jax import lax
from jax.experimental import pallas as pl
from jax.experimental.pallas import tpu as pltpu
from jax.sharding import PartitionSpec as P

ITERS = 12
BOX = 16
LANES = 128
PER = 8

CUT, LEVEL, MI, MJ, WENO, CENTRAL, KAPPA, DEPOSIT, PLANES = 6, 8, 5, 4, 16, 8, 16, 6, 4

box_step = 0.25
pseudo_step = 0.3
weno_floor = 1e-06
band_width = 1.5
tension = 2.0
grid_step = 0.2
viscosity = 0.1
normal_floor = 0.5

F32 = jnp.float32
TILE = (8, LANES)


def iotas():
    row = lax.broadcasted_iota(jnp.int32, TILE, 0)
    lane = lax.broadcasted_iota(jnp.int32, TILE, 1)
    return row, lane


def block_transpose(x, row, lane):
    block = lane // BOX
    x = jnp.take_along_axis(x, (lane - BOX * row) % LANES, axis=1)
    x = jnp.take_along_axis(x, (block - row) % 8, axis=0)
    return jnp.take_along_axis(x, (lane + BOX * row) % LANES, axis=1)


def weno(a, b, c, e, f):
    ab, bc, ce, ef = a - b, b - c, c - e, e - f
    d1, d2, d3 = ab - bc, bc - ce, ce - ef
    bc2, ce2 = bc + bc, ce + ce
    t1, t2, t3 = d1 - bc2, bc + ce, d3 + ce2
    part = 3.0 / 13.0
    floor = weno_floor * 12.0 / 13.0
    s1 = (d1 * d1 + floor) + part * (t1 * t1)
    s2 = (d2 * d2 + floor) + part * (t2 * t2)
    s3 = (d3 * d3 + floor) + part * (t3 * t3)
    q1, q2, q3 = s1 * s1, s2 * s2, s3 * s3
    w1 = q2 * q3
    w2 = 6.0 * (q1 * q3)
    w3 = 3.0 * (q1 * q2)
    top = w1 * ((ab + ab) - 5.0 * bc) - w2 * (bc + ce2) + w3 * (ef - (ce2 + ce2))
    return c + top / (6.0 * (w1 + w2 + w3))


def upwind(speed, back_two, back_one, here, ahead_one, ahead_two, ahead_three):
    pos = speed > 0.0
    return speed * weno(
        jnp.where(pos, back_two, ahead_three),
        jnp.where(pos, back_one, ahead_two),
        jnp.where(pos, here, ahead_one),
        jnp.where(pos, ahead_one, here),
        jnp.where(pos, ahead_two, back_one),
    )


ROWS = 32


def box_body(first_group, count, owner_ref, corner_ref, vel_ref, level_ref, *rest):
    (force_out, settled_out, bending_out, *scratch) = rest[-17:]
    (u_ref, l_ref, mi_ref, mj_ref, pa, pb, c_ref, s_ref, k_ref) = scratch[:9]
    turned, turned_kappa, levels, sems, level_sems = scratch[9:]
    row, lane = iotas()
    k = lane % BOX
    block = lane // BOX
    k_first, k_last = k == 0, k == BOX - 1
    top, bottom = row == 0, row == 7

    def next_k(v):
        return jnp.where(k_last, v, pltpu.roll(v, LANES - 1, 1))

    def prev_k(v):
        return jnp.where(k_first, v, pltpu.roll(v, 1, 1))

    def one_group(own):
        g = first_group + own
        spots = [[corner_ref[g * PER + b, d] for d in range(3)] for b in range(PER)]
        alive = jnp.zeros(TILE, F32)
        for b in range(PER):
            living = jnp.where(owner_ref[g * PER + b] >= 0, 1.0, 0.0)
            alive = jnp.where(block == b, living, alive)

        for b in range(PER):
            px, py, pz = spots[b]
            turn = (BOX * b + LANES - pz) % LANES
            here = block == b

            @pl.loop(0, 6, unroll=CUT)
            def _(step):
                c = step // 2
                i0 = (step % 2) * 8
                for i in range(8):
                    for jt in range(2):
                        part = vel_ref[c, px + i0 + i, pl.ds(py + 8 * jt, 8), :]
                        pltpu.store(
                            u_ref.at[c, i0 + i, pl.ds(8 * jt, 8), :],
                            pltpu.roll(part, turn, 1),
                            mask=here,
                        )

        for jt in range(2):
            come(own, jt).wait()

        @pl.loop(0, BOX, unroll=LEVEL)
        def _(i):
            for jt in range(2):
                x = levels[pl.ds((own + count * jt) * (PER * BOX) + i, 8, stride=BOX), :]
                l_ref[i, pl.ds(8 + 8 * jt, 8), :] = block_transpose(x, row, lane)

        mi_ref[0] = jnp.zeros((BOX, LANES), F32)
        mi_ref[1] = jnp.zeros((BOX, LANES), F32)
        mi_ref[2] = jnp.zeros((BOX, LANES), F32)

        @pl.loop(1, BOX, unroll=MI)
        def _(i):
            for jt in range(2):
                at = pl.ds(8 + 8 * jt, 8)
                mi_ref[i + 2, pl.ds(8 * jt, 8), :] = l_ref[i, at, :] - l_ref[i - 1, at, :]

        for t in range(3):
            mi_ref[18 + t] = mi_ref[17]

        @pl.loop(0, BOX, unroll=MJ)
        def _(i):
            for jt in range(2):
                here = l_ref[i, pl.ds(8 + 8 * jt, 8), :]
                m = here - l_ref[i, pl.ds(7 + 8 * jt, 8), :]
                if jt == 0:
                    m = jnp.where(top, 0.0, m)
                    mj_ref[i, pl.ds(0, 8), :] = jnp.zeros(TILE, F32)
                else:
                    mj_ref[i, pl.ds(24, 8), :] = jnp.broadcast_to(m[7:8, :], TILE)
                mj_ref[i, pl.ds(8 + 8 * jt, 8), :] = m

        @pl.loop(0, BOX, unroll=WENO)
        def _(i):
            for jt in range(2):
                at = pl.ds(8 * jt, 8)
                padded_at = pl.ds(8 + 8 * jt, 8)
                here = l_ref[i, padded_at, :]
                change = upwind(u_ref[0, i, at, :], *[mi_ref[i + t, at, :] for t in range(6)])
                change += upwind(
                    u_ref[1, i, at, :],
                    *[mj_ref[i, pl.ds(6 + t + 8 * jt, 8), :] for t in range(6)],
                )
                m = here - prev_k(here)
                back_one = prev_k(m)
                ahead_one = next_k(m)
                ahead_two = next_k(ahead_one)
                change += upwind(
                    u_ref[2, i, at, :],
                    prev_k(back_one),
                    back_one,
                    m,
                    ahead_one,
                    ahead_two,
                    next_k(ahead_two),
                )
                advected = here - box_step * change
                pa[i, padded_at, :] = advected
                c_ref[i, at, :] = pseudo_step * advected * lax.rsqrt(advected * advected + 1.0)
                s_ref[i, at, :] = jnp.where(advected > 0.0, 1.0, -1.0)

        def sweep(src, dst):
            for jt in range(2):
                at = pl.ds(8 * jt, 8)
                behind_i = None
                cur = src[0, pl.ds(8 + 8 * jt, 8), :]
                for i in range(BOX):
                    s = s_ref[i, at, :]
                    terms = []
                    if i < BOX - 1:
                        nxt = src[i + 1, pl.ds(8 + 8 * jt, 8), :]
                        down_i = cur - nxt
                    else:
                        nxt = down_i = None
                    if behind_i is None:
                        terms.append(jnp.maximum(s * down_i, 0.0))
                    elif down_i is None:
                        terms.append(jnp.maximum(-(s * behind_i), 0.0))
                    else:
                        terms.append(
                            jnp.maximum(jnp.maximum(s * down_i, -(s * behind_i)), 0.0)
                        )
                    below = cur - src[i, pl.ds(7 + 8 * jt, 8), :]
                    above = cur - src[i, pl.ds(9 + 8 * jt, 8), :]
                    if jt == 0:
                        below = jnp.where(top, 0.0, below)
                    else:
                        above = jnp.where(bottom, 0.0, above)
                    terms.append(jnp.maximum(jnp.maximum(s * below, s * above), 0.0))
                    down_k = jnp.where(k_last, 0.0, cur - pltpu.roll(cur, LANES - 1, 1))
                    up_k = pltpu.roll(down_k, 1, 1)
                    terms.append(jnp.maximum(jnp.maximum(s * down_k, -(s * up_k)), 0.0))
                    squared = terms[0] * terms[0] + terms[1] * terms[1] + terms[2] * terms[2]
                    root = squared * lax.rsqrt(jnp.maximum(squared, 1e-37))
                    dst[i, pl.ds(8 + 8 * jt, 8), :] = cur - c_ref[i, at, :] * (root - 1.0)
                    behind_i, cur = down_i, nxt

        @pl.loop(0, ITERS // 2)
        def _(_):
            sweep(pa, pb)
            sweep(pb, pa)

        def central(i, jt):
            at = pl.ds(8 + 8 * jt, 8)
            cur = pa[i, at, :]
            c0 = 0.5 * (pa[jnp.minimum(i + 1, BOX - 1), at, :] - pa[jnp.maximum(i - 1, 0), at, :])
            lower = pa[i, pl.ds(7 + 8 * jt, 8), :]
            upper = pa[i, pl.ds(9 + 8 * jt, 8), :]
            if jt == 0:
                lower = jnp.where(top, cur, lower)
            else:
                upper = jnp.where(bottom, cur, upper)
            c1 = 0.5 * (upper - lower)
            c2 = 0.5 * (next_k(cur) - prev_k(cur))
            return cur, c0, c1, c2

        @pl.loop(0, BOX, unroll=CENTRAL)
        def _(i):
            for jt in range(2):
                cur, c0, c1, c2 = central(i, jt)
                size = c0 * c0 + c1 * c1 + c2 * c2
                inverse = jnp.minimum(lax.rsqrt(size), 1.0 / normal_floor)
                at = pl.ds(8 * jt, 8)
                mi_ref[i, at, :] = c0 * inverse
                mj_ref[i, pl.ds(8 + 8 * jt, 8), :] = c1 * inverse
                n3 = c2 * inverse
                k_ref[i, at, :] = next_k(n3) - prev_k(n3)
                scaled = cur * (1.0 / band_width)
                band = jnp.exp(-(scaled * scaled)) * (
                    grid_step * tension / (band_width * math.sqrt(math.pi))
                )
                band = band * alive
                for c, slope in enumerate((c0, c1, c2)):
                    force_out[own, c, i, at, :] = band * slope
                y = block_transpose(cur * alive, row, lane)
                turned[pl.ds((own * 2 + jt) * (PER * BOX) + i, 8, stride=BOX), :] = y

        @pl.loop(0, BOX, unroll=KAPPA)
        def _(i):
            for jt in range(2):
                at = pl.ds(8 * jt, 8)
                padded_at = pl.ds(8 + 8 * jt, 8)
                d1 = mi_ref[jnp.minimum(i + 1, BOX - 1), at, :] - mi_ref[jnp.maximum(i - 1, 0), at, :]
                lower = mj_ref[i, pl.ds(7 + 8 * jt, 8), :]
                upper = mj_ref[i, pl.ds(9 + 8 * jt, 8), :]
                if jt == 0:
                    lower = jnp.where(top, mj_ref[i, padded_at, :], lower)
                else:
                    upper = jnp.where(bottom, mj_ref[i, padded_at, :], upper)
                kappa = 0.5 * (d1 + (upper - lower) + k_ref[i, at, :])
                for c in range(3):
                    force_out[own, c, i, at, :] = force_out[own, c, i, at, :] * kappa
                y = block_transpose(kappa * alive, row, lane)
                turned_kappa[pl.ds((own * 2 + jt) * (PER * BOX) + i, 8, stride=BOX), :] = y

        for copy in sent(own):
            copy.start()

    def come(own, jt):
        return pltpu.make_async_copy(
            level_ref.at[
                pl.ds((first_group + own) * (PER * BOX), PER * BOX), pl.ds(LANES * jt, LANES)
            ],
            levels.at[pl.ds((own + count * jt) * (PER * BOX), PER * BOX), :],
            level_sems.at[own, jt],
        )

    def sent(own):
        copies = []
        for n, (src, dst) in enumerate(((turned, settled_out), (turned_kappa, bending_out))):
            for jt in range(2):
                rows = (first_group + own) * (PER * BOX)
                copies.append(
                    pltpu.make_async_copy(
                        src.at[pl.ds((own * 2 + jt) * (PER * BOX), PER * BOX), :],
                        dst.at[pl.ds(rows, PER * BOX), pl.ds(LANES * jt, LANES)],
                        sems.at[own, 2 * n + jt],
                    )
                )
        return copies

    for own in range(count):
        for jt in range(2):
            come(own, jt).start()

    @pl.loop(0, count)
    def _(own):
        one_group(own)

    for own in range(count):
        for copy in sent(own):
            copy.wait()


def boxes(first_group, count, owner, corners, velocity, level_rows, after, carried=()):
    smem = pl.BlockSpec(memory_space=pltpu.SMEM)
    any_ = pl.BlockSpec(memory_space=pl.ANY)
    vmem = pl.BlockSpec(memory_space=pltpu.VMEM)
    plane = lambda *lead: pltpu.VMEM((*lead, LANES), F32)
    force = (count, 3, BOX, BOX, LANES)
    operands = [owner, corners, velocity, level_rows, after, *carried]
    return pl.pallas_call(
        functools.partial(box_body, first_group, count),
        out_shape=(
            jax.ShapeDtypeStruct(force, F32),
            jax.ShapeDtypeStruct(level_rows.shape, F32),
            jax.ShapeDtypeStruct(level_rows.shape, F32),
        ),
        in_specs=[smem, smem, vmem, any_, any_] + [any_] * len(carried),
        out_specs=(vmem, any_, any_),
        input_output_aliases={5: 1, 6: 2} if carried else {},
        scratch_shapes=[
            plane(3, BOX, BOX),
            plane(BOX, ROWS),
            plane(BOX + 5, BOX),
            plane(BOX, ROWS),
            plane(BOX, ROWS),
            plane(BOX, ROWS),
            plane(BOX, BOX),
            plane(BOX, BOX),
            plane(BOX, BOX),
            plane(count * 2 * PER * BOX),
            plane(count * 2 * PER * BOX),
            plane(count * 2 * PER * BOX),
            pltpu.SemaphoreType.DMA((count, 4)),
            pltpu.SemaphoreType.DMA((count, 2)),
        ],
        compiler_params=pltpu.CompilerParams(vmem_limit_bytes=20 * 2**20),
        cost_estimate=pl.CostEstimate(
            flops=30_000_000, bytes_accessed=5_000_000, transcendentals=0
        ),
        name="boxes",
    )(*operands)


def deposit(force_refs, corner_ref, grid_ref):
    _, lane = iotas()

    def one_group(ref, own, g):
        for b in range(PER):
            px, py, pz = [corner_ref[g * PER + b, d] for d in range(3)]
            inside = (lane >= pz) & (lane < pz + BOX)
            turn = (pz + LANES - BOX * b) % LANES
            base = px * 32 + py

            @pl.loop(0, 6, unroll=DEPOSIT)
            def _(step):
                c = step // 2
                i0 = (step % 2) * 8
                sums = []
                for i in range(8):
                    for jt in range(2):
                        old = grid_ref[pl.ds(base + c * 1024 + (i0 + i) * 32 + 8 * jt, 8), :]
                        push = pltpu.roll(ref[own, c, i0 + i, pl.ds(8 * jt, 8), :], turn, 1)
                        sums.append(old + jnp.where(inside, push, 0.0))
                for i in range(8):
                    for jt in range(2):
                        grid_ref[pl.ds(base + c * 1024 + (i0 + i) * 32 + 8 * jt, 8), :] = sums[
                            2 * i + jt
                        ]

    done = 0
    for ref in force_refs:
        count = ref.shape[0]

        @pl.loop(0, count)
        def _(own):
            one_group(ref, own, done + own)

        done += count


PLANE = 48


PACKED = jax.ShapeDtypeStruct((2, 3, 8, LANES), F32)
Y_ROWS = 80
X_ROWS = 88


def z_faces(rows_ref, lo_ref, hi_ref):
    _, lane = iotas()

    def one(x, packed):
        out = []
        for c in range(3):
            parts = packed[4 * c : 4 * c + 4]
            for yt in range(4):
                n = x * 4 + yt
                at = pl.multiple_of(c * 1024 + x * 32 + 8 * yt, 8)
                turned = pltpu.roll(rows_ref[pl.ds(at, 8), :], n, 1)
                parts = [
                    jnp.where(lane == (n + shift + LANES) % LANES, turned, part)
                    for shift, part in zip((0, 1, -1, -2), parts)
                ]
            out += parts
        return tuple(out)

    packed = lax.fori_loop(0, 32, one, (jnp.zeros(TILE, F32),) * 12, unroll=PLANES)
    for c in range(3):
        first, second, last, before = packed[4 * c : 4 * c + 4]
        lo_ref[0, c] = first
        lo_ref[1, c] = pltpu.roll(second, LANES - 1, 1)
        hi_ref[0, c] = pltpu.roll(last, 1, 1)
        hi_ref[1, c] = pltpu.roll(before, 2, 1)


def y_faces(rows_ref, below_ref, above_ref, _, lo_ref, hi_ref):
    for c in range(3):
        for out, layers in ((lo_ref, (0, 1)), (hi_ref, (31, 30))):
            for n, y in enumerate(layers):
                out[c, pl.ds(32 * n, 32), :] = rows_ref[pl.ds(c * 1024 + y, 32, stride=32), :]
            out[c, pl.ds(64, 8), :] = below_ref[0, c]
            out[c, pl.ds(72, 8), :] = above_ref[0, c]


def x_faces(rows_ref, below_ref, above_ref, left_ref, right_ref, _, lo_ref, hi_ref):
    for c in range(3):
        for out, layers in ((lo_ref, (0, 1)), (hi_ref, (31, 30))):
            for n, x in enumerate(layers):
                out[c, pl.ds(32 * n, 32), :] = rows_ref[pl.ds(c * 1024 + 32 * x, 32), :]
            out[c, pl.ds(64, 8), :] = jnp.zeros(TILE, F32)
            out[c, pl.ds(64, 1), :] = left_ref[c, pl.ds(layers[0], 1), :]
            out[c, pl.ds(65, 1), :] = right_ref[c, pl.ds(layers[0], 1), :]
            out[c, pl.ds(72, 8), :] = below_ref[0, c]
            out[c, pl.ds(80, 8), :] = above_ref[0, c]


def exchange(lo, hi, axis):
    size = lax.axis_size(axis)
    up = [(i, (i + 1) % size) for i in range(size)]
    down = [(j, i) for i, j in up]
    return lax.ppermute(hi, axis, up), lax.ppermute(lo, axis, down)


def slopes_to_f(centre, v, lower, upper):
    advect = sum(centre[d] * (upper[d] - lower[d]) for d in range(3))
    spread = (upper[0] + lower[0]) + (upper[1] + lower[1]) + (upper[2] + lower[2]) - 6.0 * v
    return viscosity * spread - 0.5 * advect


def along_z(v, before, after, lane):
    lower = jnp.where(lane == 0, before, pltpu.roll(v, 1, 1))
    upper = jnp.where(lane == LANES - 1, after, pltpu.roll(v, LANES - 1, 1))
    return lower, upper


def tile_step(ext, planes, plane, yt, below, above, n, lane):
    at = [
        pl.multiple_of((c * planes + plane) * PLANE + 8 + 8 * yt, 8) for c in range(3)
    ]
    centre = [ext[pl.ds(at[c], 8), :] for c in range(3)]
    out = []
    for c in range(3):
        v = centre[c]
        lower2, upper2 = along_z(
            v,
            pltpu.roll(below[c], (LANES - n) % LANES, 1),
            pltpu.roll(above[c], LANES - 1 - n, 1),
            lane,
        )
        lower = (ext[pl.ds(at[c] - PLANE, 8), :], ext[pl.ds(at[c] - 1, 8), :], lower2)
        upper = (ext[pl.ds(at[c] + PLANE, 8), :], ext[pl.ds(at[c] + 1, 8), :], upper2)
        out.append(v + grid_step * slopes_to_f(centre, v, lower, upper))
    return out


def packed_step(own, beyond, inner, x_sides, y_sides, outward, row, lane):
    out = []
    for c in range(3):
        v = own[c]
        x_lower = jnp.where(lane < 4, pltpu.roll(x_sides[0][c], 4, 1), pltpu.roll(v, 4, 1))
        x_upper = jnp.where(
            lane >= LANES - 4,
            pltpu.roll(x_sides[1][c], LANES - 4, 1),
            pltpu.roll(v, LANES - 4, 1),
        )
        down = pltpu.roll(v, 1, 0)
        down_side = pltpu.roll(pltpu.roll(y_sides[0][c], 1, 0), LANES - 3, 1)
        y_lower = jnp.where(
            row == 0, jnp.where(lane % 4 == 0, down_side, pltpu.roll(down, 1, 1)), down
        )
        up = pltpu.roll(v, 7, 0)
        up_side = pltpu.roll(pltpu.roll(y_sides[1][c], 7, 0), 3, 1)
        y_upper = jnp.where(
            row == 7, jnp.where(lane % 4 == 3, up_side, pltpu.roll(up, LANES - 1, 1)), up
        )
        pair = (inner[c], beyond[c]) if outward else (beyond[c], inner[c])
        f = slopes_to_f(own, v, (x_lower, y_lower, pair[0]), (x_upper, y_upper, pair[1]))
        out.append(v + grid_step * f)
    return out


def momentum_body(
    vel_ref, z_lo, z_hi, below, above, left, right, front, back, force_a, force_b, force_c,
    corner_ref, out_ref, ext, later, sides, packed,
):
    row, lane = iotas()
    for c in range(3):
        base = c * 36 * PLANE
        for plane, halo, layer in ((1, front, 0), (0, front, 1), (34, back, 0), (35, back, 1)):
            ext[pl.ds(base + plane * PLANE + 8, 32), :] = halo[c, pl.ds(32 * layer, 32), :]
        for plane, halo in ((1, front), (34, back)):
            ext[pl.ds(base + plane * PLANE + 7, 1), :] = halo[c, pl.ds(64, 1), :]
            ext[pl.ds(base + plane * PLANE + 40, 1), :] = halo[c, pl.ds(65, 1), :]
        ext[pl.ds(base + 2 * PLANE + 7, 32, stride=PLANE), :] = left[c, pl.ds(0, 32), :]
        ext[pl.ds(base + 2 * PLANE + 40, 32, stride=PLANE), :] = right[c, pl.ds(0, 32), :]

    @pl.loop(0, 32)
    def _(x):
        for c in range(3):
            at = pl.multiple_of((c * 36 + x + 2) * PLANE + 8, 8)
            ext[pl.ds(at, 32), :] = vel_ref[pl.ds(pl.multiple_of(c * 1024 + x * 32, 8), 32), :]

    @pl.loop(0, 32, unroll=PLANES)
    def _(x):
        lo = [below[0, c] for c in range(3)]
        hi = [above[0, c] for c in range(3)]
        for yt in range(4):
            new = tile_step(ext, 36, x + 2, yt, lo, hi, x * 4 + yt, lane)
            for c in range(3):
                at = pl.multiple_of((c * 34 + x + 1) * PLANE + 8 + 8 * yt, 8)
                later[pl.ds(at, 8), :] = new[c]

    for halo, plane, x in ((front, 1, 31), (back, 34, 0)):
        lo = [halo[c, pl.ds(72, 8), :] for c in range(3)]
        hi = [halo[c, pl.ds(80, 8), :] for c in range(3)]
        for yt in range(4):
            new = tile_step(ext, 36, plane, yt, lo, hi, x * 4 + yt, lane)
            for c in range(3):
                later[pl.ds((c * 34 + plane - 1) * PLANE + 8 + 8 * yt, 8), :] = new[c]

    for halo, out_row, y, inside in ((left, 7, 31, 0), (right, 40, 0, 31)):
        for c in range(3):
            sides[c, pl.ds(8, 32), :] = halo[c, pl.ds(0, 32), :]
            for at, end in ((7, front), (40, back)):
                sides[c, pl.ds(at, 1), :] = end[c, pl.ds(64 if out_row == 7 else 65, 1), :]
        for t in range(4):
            at = pl.ds(8 + 8 * t, 8)
            centre = [sides[c, at, :] for c in range(3)]
            where_x = 4 * (8 * t + row) + y // 8
            for c in range(3):
                v = centre[c]
                ends = [
                    jnp.take_along_axis(
                        jnp.broadcast_to(halo[c, pl.ds(64 + 8 * e + y % 8, 1), :], TILE),
                        where_x,
                        axis=1,
                    )
                    for e in range(2)
                ]
                lower2, upper2 = along_z(v, *ends, lane)
                beyond = halo[c, pl.ds(32 + 8 * t, 8), :]
                inner = vel_ref[pl.ds(c * 1024 + 8 * t * 32 + inside, 8, stride=32), :]
                pair = (beyond, inner) if out_row == 7 else (inner, beyond)
                lower = (sides[c, pl.ds(7 + 8 * t, 8), :], pair[0], lower2)
                upper = (sides[c, pl.ds(9 + 8 * t, 8), :], pair[1], upper2)
                new = v + grid_step * slopes_to_f(centre, v, lower, upper)
                rows = pl.ds((c * 34 + 8 * t + 1) * PLANE + out_row, 8, stride=PLANE)
                later[rows, :] = new

    for outward, halo, own_face in ((0, below, z_lo), (1, above, z_hi)):
        x_at, y_at = pl.ds(72 + 8 * outward, 8), pl.ds(64 + 8 * outward, 8)
        new = packed_step(
            [halo[0, c] for c in range(3)],
            [halo[1, c] for c in range(3)],
            [own_face[0, c] for c in range(3)],
            [[side[c, x_at, :] for c in range(3)] for side in (front, back)],
            [[side[c, y_at, :] for c in range(3)] for side in (left, right)],
            outward,
            row,
            lane,
        )
        for c in range(3):
            packed[outward, c] = new[c]

    @pl.loop(0, 32, unroll=PLANES)
    def _(x):
        lo = [packed[0, c] for c in range(3)]
        hi = [packed[1, c] for c in range(3)]
        for yt in range(4):
            new = tile_step(later, 34, x + 1, yt, lo, hi, x * 4 + yt, lane)
            for c in range(3):
                at = pl.ds(pl.multiple_of(c * 1024 + x * 32 + 8 * yt, 8), 8)
                out_ref[at, :] = 0.5 * (vel_ref[at, :] + new[c])

    deposit((force_a, force_b, force_c), corner_ref, out_ref)


def call(body, out_shape, operands, name, unread=0, corners=None, scratch=(), limit=16):
    vmem = pl.BlockSpec(memory_space=pltpu.VMEM)
    specs = [vmem] * (len(operands) - unread) + [pl.BlockSpec(memory_space=pl.ANY)] * unread
    if corners is not None:
        operands = [*operands, corners]
        specs.append(pl.BlockSpec(memory_space=pltpu.SMEM))
    return pl.pallas_call(
        body,
        out_shape=out_shape,
        in_specs=specs,
        out_specs=jax.tree.map(lambda _: vmem, out_shape),
        scratch_shapes=scratch,
        compiler_params=pltpu.CompilerParams(vmem_limit_bytes=limit * 2**20),
        name=name,
    )(*operands)


def local(velocity, box_level, corners, owner_list):
    slots = box_level.shape[0]
    rows = velocity.reshape(-1, LANES)
    level_rows = box_level.reshape(slots * BOX, BOX * BOX)
    work = functools.partial(boxes, owner=owner_list, corners=corners, velocity=velocity, level_rows=level_rows)
    z_lo, z_hi = call(z_faces, (PACKED,) * 2, [rows], "z_faces")
    below, above = exchange(z_lo, z_hi, "gz")
    force_a, *done = work(0, 1, after=z_lo)
    sent = jax.ShapeDtypeStruct((3, Y_ROWS, LANES), F32)
    faces = call(y_faces, (sent,) * 2, [rows, below, above, force_a], "y_faces", unread=1)
    left, right = exchange(*faces, "gy")
    force_b, *done = work(1, 1, after=faces[0], carried=done)
    sent = jax.ShapeDtypeStruct((3, X_ROWS, LANES), F32)
    faces = call(
        x_faces, (sent,) * 2, [rows, below, above, left, right, force_b], "x_faces", unread=1
    )
    front, back = exchange(*faces, "gx")
    force_c, settled, bending = work(2, slots // PER - 2, after=faces[0], carried=done)
    result = call(
        momentum_body,
        jax.ShapeDtypeStruct(rows.shape, F32),
        [rows, z_lo, z_hi, below, above, left, right, front, back, force_a, force_b, force_c],
        "momentum",
        corners=corners,
        scratch=[
            pltpu.VMEM((3 * 36 * PLANE, LANES), F32),
            pltpu.VMEM((3 * 34 * PLANE, LANES), F32),
            pltpu.VMEM((3, PLANE, LANES), F32),
            pltpu.VMEM((2, 3, 8, LANES), F32),
        ],
        limit=32,
    )
    return (
        result.reshape(velocity.shape),
        settled.reshape(box_level.shape),
        bending.reshape(box_level.shape),
    )


def solution(mesh):
    placed = (
        P(None, "gx", "gy", "gz"),
        P(("gx", "gy", "gz"), None, None),
        P(("gx", "gy", "gz"), None),
        P(("gx", "gy", "gz")),
    )
    return jax.shard_map(
        local,
        mesh=mesh,
        in_specs=placed,
        out_specs=(
            P(None, "gx", "gy", "gz"),
            P(("gx", "gy", "gz"), None, None),
            P(("gx", "gy", "gz"), None, None),
        ),
        check_vma=False,
    )
```

```python
import functools
import math

import jax
import jax.numpy as jnp
from jax import lax
from jax.experimental import pallas as pl
from jax.experimental.pallas import tpu as pltpu
from jax.sharding import PartitionSpec as P

ITERS = 12
BOX = 16
LANES = 128
PER = 8

CUT, LEVEL, MI, MJ, WENO, CENTRAL, KAPPA, PLANES = 6, 8, 5, 4, 16, 8, 16, 4

box_step = 0.25
pseudo_step = 0.3
weno_floor = 1e-06
band_width = 1.5
tension = 2.0
grid_step = 0.2
viscosity = 0.1
normal_floor = 0.5

F32 = jnp.float32
TILE = (8, LANES)


def iotas():
    row = lax.broadcasted_iota(jnp.int32, TILE, 0)
    lane = lax.broadcasted_iota(jnp.int32, TILE, 1)
    return row, lane


def block_transpose(x, row, lane):
    block = lane // BOX
    x = jnp.take_along_axis(x, (lane - BOX * row) % LANES, axis=1)
    x = jnp.take_along_axis(x, (block - row) % 8, axis=0)
    return jnp.take_along_axis(x, (lane + BOX * row) % LANES, axis=1)


def weno(a, b, c, e, f):
    ab, bc, ce, ef = a - b, b - c, c - e, e - f
    d1, d2, d3 = ab - bc, bc - ce, ce - ef
    bc2, ce2 = bc + bc, ce + ce
    t1, t2, t3 = d1 - bc2, bc + ce, d3 + ce2
    part = 3.0 / 13.0
    floor = weno_floor * 12.0 / 13.0
    s1 = (d1 * d1 + floor) + part * (t1 * t1)
    s2 = (d2 * d2 + floor) + part * (t2 * t2)
    s3 = (d3 * d3 + floor) + part * (t3 * t3)
    q1, q2, q3 = s1 * s1, s2 * s2, s3 * s3
    w1 = q2 * q3
    w2 = 6.0 * (q1 * q3)
    w3 = 3.0 * (q1 * q2)
    top = w1 * ((ab + ab) - 5.0 * bc) - w2 * (bc + ce2) + w3 * (ef - (ce2 + ce2))
    return c + top / (6.0 * (w1 + w2 + w3))


def upwind(speed, back_two, back_one, here, ahead_one, ahead_two, ahead_three):
    pos = speed > 0.0
    return speed * weno(
        jnp.where(pos, back_two, ahead_three),
        jnp.where(pos, back_one, ahead_two),
        jnp.where(pos, here, ahead_one),
        jnp.where(pos, ahead_one, here),
        jnp.where(pos, ahead_two, back_one),
    )


ROWS = 32


def box_body(first_group, count, owner_ref, corner_ref, vel_ref, level_ref, *rest):
    (force_out, turned, turned_kappa, *scratch) = rest[-14:]
    (u_ref, l_ref, mi_ref, mj_ref, pa, pb, c_ref, s_ref, k_ref) = scratch[:9]
    levels, level_sems = scratch[9:]
    row, lane = iotas()
    k = lane % BOX
    block = lane // BOX
    k_first, k_last = k == 0, k == BOX - 1
    top, bottom = row == 0, row == 7

    def next_k(v):
        return jnp.where(k_last, v, pltpu.roll(v, LANES - 1, 1))

    def prev_k(v):
        return jnp.where(k_first, v, pltpu.roll(v, 1, 1))

    def one_group(own):
        g = first_group + own
        spots = [[corner_ref[g * PER + b, d] for d in range(3)] for b in range(PER)]
        alive = jnp.zeros(TILE, F32)
        for b in range(PER):
            living = jnp.where(owner_ref[g * PER + b] >= 0, 1.0, 0.0)
            alive = jnp.where(block == b, living, alive)

        for b in range(PER):
            px, py, pz = spots[b]
            turn = (BOX * b + LANES - pz) % LANES
            here = block == b
            base = px * 32 + py

            @pl.loop(0, 6, unroll=CUT)
            def _(step):
                c = step // 2
                i0 = (step % 2) * 8
                for i in range(8):
                    for jt in range(2):
                        part = vel_ref[pl.ds(base + c * 1024 + (i0 + i) * 32 + 8 * jt, 8), :]
                        pltpu.store(
                            u_ref.at[c, i0 + i, pl.ds(8 * jt, 8), :],
                            pltpu.roll(part, turn, 1),
                            mask=here,
                        )

        for jt in range(2):
            come(own, jt).wait()

        @pl.loop(0, BOX, unroll=LEVEL)
        def _(i):
            for jt in range(2):
                x = levels[pl.ds((own + count * jt) * (PER * BOX) + i, 8, stride=BOX), :]
                l_ref[i, pl.ds(8 + 8 * jt, 8), :] = block_transpose(x, row, lane)

        mi_ref[0] = jnp.zeros((BOX, LANES), F32)
        mi_ref[1] = jnp.zeros((BOX, LANES), F32)
        mi_ref[2] = jnp.zeros((BOX, LANES), F32)

        @pl.loop(1, BOX, unroll=MI)
        def _(i):
            for jt in range(2):
                at = pl.ds(8 + 8 * jt, 8)
                mi_ref[i + 2, pl.ds(8 * jt, 8), :] = l_ref[i, at, :] - l_ref[i - 1, at, :]

        for t in range(3):
            mi_ref[18 + t] = mi_ref[17]

        @pl.loop(0, BOX, unroll=MJ)
        def _(i):
            for jt in range(2):
                here = l_ref[i, pl.ds(8 + 8 * jt, 8), :]
                m = here - l_ref[i, pl.ds(7 + 8 * jt, 8), :]
                if jt == 0:
                    m = jnp.where(top, 0.0, m)
                    mj_ref[i, pl.ds(0, 8), :] = jnp.zeros(TILE, F32)
                else:
                    mj_ref[i, pl.ds(24, 8), :] = jnp.broadcast_to(m[7:8, :], TILE)
                mj_ref[i, pl.ds(8 + 8 * jt, 8), :] = m

        @pl.loop(0, BOX, unroll=WENO)
        def _(i):
            for jt in range(2):
                at = pl.ds(8 * jt, 8)
                padded_at = pl.ds(8 + 8 * jt, 8)
                here = l_ref[i, padded_at, :]
                change = upwind(u_ref[0, i, at, :], *[mi_ref[i + t, at, :] for t in range(6)])
                change += upwind(
                    u_ref[1, i, at, :],
                    *[mj_ref[i, pl.ds(6 + t + 8 * jt, 8), :] for t in range(6)],
                )
                m = here - prev_k(here)
                back_one = prev_k(m)
                ahead_one = next_k(m)
                ahead_two = next_k(ahead_one)
                change += upwind(
                    u_ref[2, i, at, :],
                    prev_k(back_one),
                    back_one,
                    m,
                    ahead_one,
                    ahead_two,
                    next_k(ahead_two),
                )
                advected = here - box_step * change
                pa[i, padded_at, :] = advected
                c_ref[i, at, :] = pseudo_step * advected * lax.rsqrt(advected * advected + 1.0)
                s_ref[i, at, :] = jnp.where(advected > 0.0, 1.0, -1.0)

        def sweep(src, dst):
            for jt in range(2):
                at = pl.ds(8 * jt, 8)
                behind_i = None
                cur = src[0, pl.ds(8 + 8 * jt, 8), :]
                for i in range(BOX):
                    s = s_ref[i, at, :]
                    terms = []
                    if i < BOX - 1:
                        nxt = src[i + 1, pl.ds(8 + 8 * jt, 8), :]
                        down_i = cur - nxt
                    else:
                        nxt = down_i = None
                    if behind_i is None:
                        terms.append(jnp.maximum(s * down_i, 0.0))
                    elif down_i is None:
                        terms.append(jnp.maximum(-(s * behind_i), 0.0))
                    else:
                        terms.append(
                            jnp.maximum(jnp.maximum(s * down_i, -(s * behind_i)), 0.0)
                        )
                    below = cur - src[i, pl.ds(7 + 8 * jt, 8), :]
                    above = cur - src[i, pl.ds(9 + 8 * jt, 8), :]
                    if jt == 0:
                        below = jnp.where(top, 0.0, below)
                    else:
                        above = jnp.where(bottom, 0.0, above)
                    terms.append(jnp.maximum(jnp.maximum(s * below, s * above), 0.0))
                    down_k = jnp.where(k_last, 0.0, cur - pltpu.roll(cur, LANES - 1, 1))
                    up_k = pltpu.roll(down_k, 1, 1)
                    terms.append(jnp.maximum(jnp.maximum(s * down_k, -(s * up_k)), 0.0))
                    squared = terms[0] * terms[0] + terms[1] * terms[1] + terms[2] * terms[2]
                    root = squared * lax.rsqrt(jnp.maximum(squared, 1e-37))
                    dst[i, pl.ds(8 + 8 * jt, 8), :] = cur - c_ref[i, at, :] * (root - 1.0)
                    behind_i, cur = down_i, nxt

        @pl.loop(0, ITERS // 2)
        def _(_):
            sweep(pa, pb)
            sweep(pb, pa)

        def central(i, jt):
            at = pl.ds(8 + 8 * jt, 8)
            cur = pa[i, at, :]
            c0 = 0.5 * (pa[jnp.minimum(i + 1, BOX - 1), at, :] - pa[jnp.maximum(i - 1, 0), at, :])
            lower = pa[i, pl.ds(7 + 8 * jt, 8), :]
            upper = pa[i, pl.ds(9 + 8 * jt, 8), :]
            if jt == 0:
                lower = jnp.where(top, cur, lower)
            else:
                upper = jnp.where(bottom, cur, upper)
            c1 = 0.5 * (upper - lower)
            c2 = 0.5 * (next_k(cur) - prev_k(cur))
            return cur, c0, c1, c2

        @pl.loop(0, BOX, unroll=CENTRAL)
        def _(i):
            for jt in range(2):
                cur, c0, c1, c2 = central(i, jt)
                size = c0 * c0 + c1 * c1 + c2 * c2
                inverse = jnp.minimum(lax.rsqrt(size), 1.0 / normal_floor)
                at = pl.ds(8 * jt, 8)
                mi_ref[i, at, :] = c0 * inverse
                mj_ref[i, pl.ds(8 + 8 * jt, 8), :] = c1 * inverse
                n3 = c2 * inverse
                k_ref[i, at, :] = next_k(n3) - prev_k(n3)
                scaled = cur * (1.0 / band_width)
                band = jnp.exp(-(scaled * scaled)) * (
                    grid_step * tension / (band_width * math.sqrt(math.pi))
                )
                band = band * alive
                for c, slope in enumerate((c0, c1, c2)):
                    force_out[own, c, i, at, :] = band * slope
                y = block_transpose(cur * alive, row, lane)
                turned[pl.ds((own * 2 + jt) * (PER * BOX) + i, 8, stride=BOX), :] = y

        @pl.loop(0, BOX, unroll=KAPPA)
        def _(i):
            for jt in range(2):
                at = pl.ds(8 * jt, 8)
                padded_at = pl.ds(8 + 8 * jt, 8)
                d1 = mi_ref[jnp.minimum(i + 1, BOX - 1), at, :] - mi_ref[jnp.maximum(i - 1, 0), at, :]
                lower = mj_ref[i, pl.ds(7 + 8 * jt, 8), :]
                upper = mj_ref[i, pl.ds(9 + 8 * jt, 8), :]
                if jt == 0:
                    lower = jnp.where(top, mj_ref[i, padded_at, :], lower)
                else:
                    upper = jnp.where(bottom, mj_ref[i, padded_at, :], upper)
                kappa = 0.5 * (d1 + (upper - lower) + k_ref[i, at, :])
                for c in range(3):
                    force_out[own, c, i, at, :] = force_out[own, c, i, at, :] * kappa
                y = block_transpose(kappa * alive, row, lane)
                turned_kappa[pl.ds((own * 2 + jt) * (PER * BOX) + i, 8, stride=BOX), :] = y

    def come(own, jt):
        return pltpu.make_async_copy(
            level_ref.at[
                pl.ds((first_group + own) * (PER * BOX), PER * BOX), pl.ds(LANES * jt, LANES)
            ],
            levels.at[pl.ds((own + count * jt) * (PER * BOX), PER * BOX), :],
            level_sems.at[own, jt],
        )

    for own in range(count):
        for jt in range(2):
            come(own, jt).start()

    @pl.loop(0, count)
    def _(own):
        one_group(own)


def boxes(first_group, count, owner, corners, rows, level_rows, after):
    smem = pl.BlockSpec(memory_space=pltpu.SMEM)
    hbm = pl.BlockSpec(memory_space=pltpu.HBM)
    vmem = pl.BlockSpec(memory_space=pltpu.VMEM)
    any_ = pl.BlockSpec(memory_space=pl.ANY)
    plane = lambda *lead: pltpu.VMEM((*lead, LANES), F32)
    turned = jax.ShapeDtypeStruct((count * 2 * PER * BOX, LANES), F32)
    return pl.pallas_call(
        functools.partial(box_body, first_group, count),
        out_shape=(jax.ShapeDtypeStruct((count, 3, BOX, BOX, LANES), F32), turned, turned),
        in_specs=[smem, smem, vmem, hbm, any_],
        out_specs=(vmem,) * 3,
        scratch_shapes=[
            plane(3, BOX, BOX),
            plane(BOX, ROWS),
            plane(BOX + 5, BOX),
            plane(BOX, ROWS),
            plane(BOX, ROWS),
            plane(BOX, ROWS),
            plane(BOX, BOX),
            plane(BOX, BOX),
            plane(BOX, BOX),
            plane(count * 2 * PER * BOX),
            pltpu.SemaphoreType.DMA((count, 2)),
        ],
        compiler_params=pltpu.CompilerParams(vmem_limit_bytes=16 * 2**20),
        cost_estimate=pl.CostEstimate(
            flops=30_000_000, bytes_accessed=5_000_000, transcendentals=0
        ),
        name="boxes",
    )(owner, corners, rows, level_rows, after)


def deposit(force_refs, corner_ref, grid_ref, c):
    _, lane = iotas()

    def one_group(ref, own, g):
        for b in range(PER):
            px, py, pz = [corner_ref[g * PER + b, d] for d in range(3)]
            inside = (lane >= pz) & (lane < pz + BOX)
            turn = (pz + LANES - BOX * b) % LANES
            base = c * 1024 + px * 32 + py
            for i0 in (0, 8):
                sums = []
                for i in range(8):
                    for jt in range(2):
                        old = grid_ref[pl.ds(base + (i0 + i) * 32 + 8 * jt, 8), :]
                        push = pltpu.roll(ref[own, c, i0 + i, pl.ds(8 * jt, 8), :], turn, 1)
                        sums.append(old + jnp.where(inside, push, 0.0))
                for i in range(8):
                    for jt in range(2):
                        grid_ref[pl.ds(base + (i0 + i) * 32 + 8 * jt, 8), :] = sums[2 * i + jt]

    done = 0
    for ref in force_refs:
        count = ref.shape[0]

        @pl.loop(0, count)
        def _(own):
            one_group(ref, own, done + own)

        done += count


PLANE = 48


PACKED = jax.ShapeDtypeStruct((2, 3, 8, LANES), F32)
Y_ROWS = 80
X_ROWS = 88


def z_faces(rows_ref, kept_ref, lo_ref, hi_ref):
    _, lane = iotas()
    for c in range(3):

        def one(x, parts):
            for yt in range(4):
                n = x * 4 + yt
                at = pl.multiple_of(c * 1024 + x * 32 + 8 * yt, 8)
                tile = rows_ref[pl.ds(at, 8), :]
                kept_ref[pl.ds(at, 8), :] = tile
                turned = pltpu.roll(tile, n, 1)
                parts = tuple(
                    jnp.where(lane == (n + shift + LANES) % LANES, turned, part)
                    for shift, part in zip((0, 1, -1, -2), parts)
                )
            return parts

        first, second, last, before = lax.fori_loop(
            0, 32, one, (jnp.zeros(TILE, F32),) * 4, unroll=2 * PLANES
        )
        lo_ref[0, c] = first
        lo_ref[1, c] = pltpu.roll(second, LANES - 1, 1)
        hi_ref[0, c] = pltpu.roll(last, 1, 1)
        hi_ref[1, c] = pltpu.roll(before, 2, 1)


def y_faces(rows_ref, below_ref, above_ref, _, lo_ref, hi_ref):
    for c in range(3):
        for out, layers in ((lo_ref, (0, 1)), (hi_ref, (31, 30))):
            for n, y in enumerate(layers):
                out[c, pl.ds(32 * n, 32), :] = rows_ref[pl.ds(c * 1024 + y, 32, stride=32), :]
            out[c, pl.ds(64, 8), :] = below_ref[0, c]
            out[c, pl.ds(72, 8), :] = above_ref[0, c]


def x_faces(rows_ref, below_ref, above_ref, left_ref, right_ref, _, lo_ref, hi_ref):
    for c in range(3):
        for out, layers in ((lo_ref, (0, 1)), (hi_ref, (31, 30))):
            for n, x in enumerate(layers):
                out[c, pl.ds(32 * n, 32), :] = rows_ref[pl.ds(c * 1024 + 32 * x, 32), :]
            out[c, pl.ds(64, 8), :] = jnp.zeros(TILE, F32)
            out[c, pl.ds(64, 1), :] = left_ref[c, pl.ds(layers[0], 1), :]
            out[c, pl.ds(65, 1), :] = right_ref[c, pl.ds(layers[0], 1), :]
            out[c, pl.ds(72, 8), :] = below_ref[0, c]
            out[c, pl.ds(80, 8), :] = above_ref[0, c]


def exchange(lo, hi, axis):
    size = lax.axis_size(axis)
    up = [(i, (i + 1) % size) for i in range(size)]
    down = [(j, i) for i, j in up]
    return lax.ppermute(hi, axis, up), lax.ppermute(lo, axis, down)


def slopes_to_f(centre, v, lower, upper):
    advect = sum(centre[d] * (upper[d] - lower[d]) for d in range(3))
    spread = (upper[0] + lower[0]) + (upper[1] + lower[1]) + (upper[2] + lower[2]) - 6.0 * v
    return viscosity * spread - 0.5 * advect


def along_z(v, before, after, lane):
    lower = jnp.where(lane == 0, before, pltpu.roll(v, 1, 1))
    upper = jnp.where(lane == LANES - 1, after, pltpu.roll(v, LANES - 1, 1))
    return lower, upper


def tile_step(ext, planes, plane, yt, below, above, n, lane):
    at = [
        pl.multiple_of((c * planes + plane) * PLANE + 8 + 8 * yt, 8) for c in range(3)
    ]
    centre = [ext[pl.ds(at[c], 8), :] for c in range(3)]
    out = []
    for c in range(3):
        v = centre[c]
        lower2, upper2 = along_z(
            v,
            pltpu.roll(below[c], (LANES - n) % LANES, 1),
            pltpu.roll(above[c], LANES - 1 - n, 1),
            lane,
        )
        lower = (ext[pl.ds(at[c] - PLANE, 8), :], ext[pl.ds(at[c] - 1, 8), :], lower2)
        upper = (ext[pl.ds(at[c] + PLANE, 8), :], ext[pl.ds(at[c] + 1, 8), :], upper2)
        out.append(v + grid_step * slopes_to_f(centre, v, lower, upper))
    return out


def packed_step(own, beyond, inner, x_sides, y_sides, outward, row, lane):
    out = []
    for c in range(3):
        v = own[c]
        x_lower = jnp.where(lane < 4, pltpu.roll(x_sides[0][c], 4, 1), pltpu.roll(v, 4, 1))
        x_upper = jnp.where(
            lane >= LANES - 4,
            pltpu.roll(x_sides[1][c], LANES - 4, 1),
            pltpu.roll(v, LANES - 4, 1),
        )
        down = pltpu.roll(v, 1, 0)
        down_side = pltpu.roll(pltpu.roll(y_sides[0][c], 1, 0), LANES - 3, 1)
        y_lower = jnp.where(
            row == 0, jnp.where(lane % 4 == 0, down_side, pltpu.roll(down, 1, 1)), down
        )
        up = pltpu.roll(v, 7, 0)
        up_side = pltpu.roll(pltpu.roll(y_sides[1][c], 7, 0), 3, 1)
        y_upper = jnp.where(
            row == 7, jnp.where(lane % 4 == 3, up_side, pltpu.roll(up, LANES - 1, 1)), up
        )
        pair = (inner[c], beyond[c]) if outward else (beyond[c], inner[c])
        f = slopes_to_f(own, v, (x_lower, y_lower, pair[0]), (x_upper, y_upper, pair[1]))
        out.append(v + grid_step * f)
    return out


def momentum_body(
    vel_ref, z_lo, z_hi, below, above, left, right, front, back, *refs,
):
    forces, settled, bending, corner_ref = refs[:3], refs[3:6], refs[6:9], refs[9]
    new_out, settled_out, bending_out, ext, later, sides, packed, out_ref, sems, grid_sems = refs[10:]
    row, lane = iotas()

    leaving = []
    for n, (parts, out) in enumerate(((settled, settled_out), (bending, bending_out))):
        group = 0
        for part in parts:
            for own in range(part.shape[0] // (2 * PER * BOX)):
                for jt in range(2):
                    leaving.append(
                        pltpu.make_async_copy(
                            part.at[pl.ds((own * 2 + jt) * (PER * BOX), PER * BOX), :],
                            out.at[
                                pl.ds(group * (PER * BOX), PER * BOX), pl.ds(LANES * jt, LANES)
                            ],
                            sems.at[n, group, jt],
                        )
                    )
                group += 1
    for copy in leaving:
        copy.start()

    for c in range(3):
        base = c * 36 * PLANE
        for plane, halo, layer in ((1, front, 0), (0, front, 1), (34, back, 0), (35, back, 1)):
            ext[pl.ds(base + plane * PLANE + 8, 32), :] = halo[c, pl.ds(32 * layer, 32), :]
        for plane, halo in ((1, front), (34, back)):
            ext[pl.ds(base + plane * PLANE + 7, 1), :] = halo[c, pl.ds(64, 1), :]
            ext[pl.ds(base + plane * PLANE + 40, 1), :] = halo[c, pl.ds(65, 1), :]
        ext[pl.ds(base + 2 * PLANE + 7, 32, stride=PLANE), :] = left[c, pl.ds(0, 32), :]
        ext[pl.ds(base + 2 * PLANE + 40, 32, stride=PLANE), :] = right[c, pl.ds(0, 32), :]

    @pl.loop(0, 32)
    def _(x):
        for c in range(3):
            at = pl.multiple_of((c * 36 + x + 2) * PLANE + 8, 8)
            ext[pl.ds(at, 32), :] = vel_ref[pl.ds(pl.multiple_of(c * 1024 + x * 32, 8), 32), :]

    @pl.loop(0, 32, unroll=PLANES)
    def _(x):
        lo = [below[0, c] for c in range(3)]
        hi = [above[0, c] for c in range(3)]
        for yt in range(4):
            new = tile_step(ext, 36, x + 2, yt, lo, hi, x * 4 + yt, lane)
            for c in range(3):
                at = pl.multiple_of((c * 34 + x + 1) * PLANE + 8 + 8 * yt, 8)
                later[pl.ds(at, 8), :] = new[c]

    for halo, plane, x in ((front, 1, 31), (back, 34, 0)):
        lo = [halo[c, pl.ds(72, 8), :] for c in range(3)]
        hi = [halo[c, pl.ds(80, 8), :] for c in range(3)]
        for yt in range(4):
            new = tile_step(ext, 36, plane, yt, lo, hi, x * 4 + yt, lane)
            for c in range(3):
                later[pl.ds((c * 34 + plane - 1) * PLANE + 8 + 8 * yt, 8), :] = new[c]

    for halo, out_row, y, inside in ((left, 7, 31, 0), (right, 40, 0, 31)):
        for c in range(3):
            sides[c, pl.ds(8, 32), :] = halo[c, pl.ds(0, 32), :]
            for at, end in ((7, front), (40, back)):
                sides[c, pl.ds(at, 1), :] = end[c, pl.ds(64 if out_row == 7 else 65, 1), :]
        for t in range(4):
            at = pl.ds(8 + 8 * t, 8)
            centre = [sides[c, at, :] for c in range(3)]
            where_x = 4 * (8 * t + row) + y // 8
            for c in range(3):
                v = centre[c]
                ends = [
                    jnp.take_along_axis(
                        jnp.broadcast_to(halo[c, pl.ds(64 + 8 * e + y % 8, 1), :], TILE),
                        where_x,
                        axis=1,
                    )
                    for e in range(2)
                ]
                lower2, upper2 = along_z(v, *ends, lane)
                beyond = halo[c, pl.ds(32 + 8 * t, 8), :]
                inner = vel_ref[pl.ds(c * 1024 + 8 * t * 32 + inside, 8, stride=32), :]
                pair = (beyond, inner) if out_row == 7 else (inner, beyond)
                lower = (sides[c, pl.ds(7 + 8 * t, 8), :], pair[0], lower2)
                upper = (sides[c, pl.ds(9 + 8 * t, 8), :], pair[1], upper2)
                new = v + grid_step * slopes_to_f(centre, v, lower, upper)
                rows = pl.ds((c * 34 + 8 * t + 1) * PLANE + out_row, 8, stride=PLANE)
                later[rows, :] = new

    for outward, halo, own_face in ((0, below, z_lo), (1, above, z_hi)):
        x_at, y_at = pl.ds(72 + 8 * outward, 8), pl.ds(64 + 8 * outward, 8)
        new = packed_step(
            [halo[0, c] for c in range(3)],
            [halo[1, c] for c in range(3)],
            [own_face[0, c] for c in range(3)],
            [[side[c, x_at, :] for c in range(3)] for side in (front, back)],
            [[side[c, y_at, :] for c in range(3)] for side in (left, right)],
            outward,
            row,
            lane,
        )
        for c in range(3):
            packed[outward, c] = new[c]

    @pl.loop(0, 32, unroll=PLANES)
    def _(x):
        lo = [packed[0, c] for c in range(3)]
        hi = [packed[1, c] for c in range(3)]
        for yt in range(4):
            new = tile_step(later, 34, x + 1, yt, lo, hi, x * 4 + yt, lane)
            for c in range(3):
                at = pl.ds(pl.multiple_of(c * 1024 + x * 32 + 8 * yt, 8), 8)
                out_ref[at, :] = 0.5 * (vel_ref[at, :] + new[c])

    for c in range(3):
        deposit(forces, corner_ref, out_ref, c)
        at = pl.ds(c * 1024, 1024)
        leaving.append(
            pltpu.make_async_copy(out_ref.at[at, :], new_out.at[at, :], grid_sems.at[c])
        )
        leaving[-1].start()
    for copy in leaving:
        copy.wait()


def call(body, out_shape, operands, name, unread=0):
    vmem = pl.BlockSpec(memory_space=pltpu.VMEM)
    specs = [vmem] * (len(operands) - unread) + [pl.BlockSpec(memory_space=pl.ANY)] * unread
    return pl.pallas_call(
        body,
        out_shape=out_shape,
        in_specs=specs,
        out_specs=jax.tree.map(lambda _: vmem, out_shape),
        compiler_params=pltpu.CompilerParams(vmem_limit_bytes=8 * 2**20),
        name=name,
    )(*operands)


def local(velocity, box_level, corners, owner_list):
    slots = box_level.shape[0]
    level_rows = box_level.reshape(slots * BOX, BOX * BOX)
    rows = velocity.reshape(-1, LANES)
    kept = jax.ShapeDtypeStruct(rows.shape, F32)
    rows, z_lo, z_hi = call(z_faces, (kept, PACKED, PACKED), [rows], "z_faces")
    below, above = exchange(z_lo, z_hi, "gz")
    work = functools.partial(
        boxes, owner=owner_list, corners=corners, rows=rows, level_rows=level_rows
    )
    first = work(0, 1, after=z_lo)
    sent = jax.ShapeDtypeStruct((3, Y_ROWS, LANES), F32)
    faces = call(y_faces, (sent,) * 2, [rows, below, above, first[0]], "y_faces", unread=1)
    left, right = exchange(*faces, "gy")
    second = work(1, 1, after=faces[0])
    sent = jax.ShapeDtypeStruct((3, X_ROWS, LANES), F32)
    faces = call(
        x_faces, (sent,) * 2, [rows, below, above, left, right, second[0]], "x_faces", unread=1
    )
    front, back = exchange(*faces, "gx")
    third = work(2, slots // PER - 2, after=faces[0])
    parts = [part for kind in zip(first, second, third) for part in kind]
    operands = [rows, z_lo, z_hi, below, above, left, right, front, back, *parts]
    hbm = pl.BlockSpec(memory_space=pltpu.HBM)
    boxed = jax.ShapeDtypeStruct(level_rows.shape, F32)
    result, settled, bending = pl.pallas_call(
        momentum_body,
        out_shape=(jax.ShapeDtypeStruct(rows.shape, F32), boxed, boxed),
        in_specs=[pl.BlockSpec(memory_space=pltpu.VMEM)] * len(operands)
        + [pl.BlockSpec(memory_space=pltpu.SMEM)],
        out_specs=(hbm,) * 3,
        scratch_shapes=[
            pltpu.VMEM((3 * 36 * PLANE, LANES), F32),
            pltpu.VMEM((3 * 34 * PLANE, LANES), F32),
            pltpu.VMEM((3, PLANE, LANES), F32),
            pltpu.VMEM((2, 3, 8, LANES), F32),
            pltpu.VMEM(rows.shape, F32),
            pltpu.SemaphoreType.DMA((2, slots // PER, 2)),
            pltpu.SemaphoreType.DMA((3,)),
        ],
        compiler_params=pltpu.CompilerParams(vmem_limit_bytes=24 * 2**20),
        name="momentum",
    )(*operands, corners)
    return (
        result.reshape(velocity.shape),
        settled.reshape(box_level.shape),
        bending.reshape(box_level.shape),
    )


def solution(mesh):
    placed = (
        P(None, "gx", "gy", "gz"),
        P(("gx", "gy", "gz"), None, None),
        P(("gx", "gy", "gz"), None),
        P(("gx", "gy", "gz")),
    )
    return jax.shard_map(
        local,
        mesh=mesh,
        in_specs=placed,
        out_specs=(
            P(None, "gx", "gy", "gz"),
            P(("gx", "gy", "gz"), None, None),
            P(("gx", "gy", "gz"), None, None),
        ),
        check_vma=False,
    )
```

```python
import functools
import math

import jax
import jax.numpy as jnp
from jax import lax
from jax.experimental import pallas as pl
from jax.experimental.pallas import tpu as pltpu
from jax.sharding import PartitionSpec as P

ITERS = 12
BOX = 16
LANES = 128
PER = 8

CUT, LEVEL, MI, MJ, WENO, CENTRAL, KAPPA, PLANES = 6, 8, 5, 4, 16, 8, 16, 8

box_step = 0.25
pseudo_step = 0.3
weno_floor = 1e-06
band_width = 1.5
tension = 2.0
grid_step = 0.2
viscosity = 0.1
normal_floor = 0.5

F32 = jnp.float32
TILE = (8, LANES)


def iotas():
    row = lax.broadcasted_iota(jnp.int32, TILE, 0)
    lane = lax.broadcasted_iota(jnp.int32, TILE, 1)
    return row, lane


def block_transpose(x, row, lane):
    block = lane // BOX
    x = jnp.take_along_axis(x, (lane - BOX * row) % LANES, axis=1)
    x = jnp.take_along_axis(x, (block - row) % 8, axis=0)
    return jnp.take_along_axis(x, (lane + BOX * row) % LANES, axis=1)


def weno(a, b, c, e, f):
    ab, bc, ce, ef = a - b, b - c, c - e, e - f
    d1, d2, d3 = ab - bc, bc - ce, ce - ef
    bc2, ce2 = bc + bc, ce + ce
    t1, t2, t3 = d1 - bc2, bc + ce, d3 + ce2
    part = 3.0 / 13.0
    floor = weno_floor * 12.0 / 13.0
    s1 = (d1 * d1 + floor) + part * (t1 * t1)
    s2 = (d2 * d2 + floor) + part * (t2 * t2)
    s3 = (d3 * d3 + floor) + part * (t3 * t3)
    q1, q2, q3 = s1 * s1, s2 * s2, s3 * s3
    w1 = q2 * q3
    w2 = 6.0 * (q1 * q3)
    w3 = 3.0 * (q1 * q2)
    top = w1 * ((ab + ab) - 5.0 * bc) - w2 * (bc + ce2) + w3 * (ef - (ce2 + ce2))
    return c + top / (6.0 * (w1 + w2 + w3))


def upwind(speed, back_two, back_one, here, ahead_one, ahead_two, ahead_three):
    pos = speed > 0.0
    return speed * weno(
        jnp.where(pos, back_two, ahead_three),
        jnp.where(pos, back_one, ahead_two),
        jnp.where(pos, here, ahead_one),
        jnp.where(pos, ahead_one, here),
        jnp.where(pos, ahead_two, back_one),
    )


ROWS = 32


def box_body(first_group, count, owner_ref, corner_ref, vel_ref, level_ref, *rest):
    (force_out, turned, turned_kappa, *scratch) = rest[-14:]
    (u_ref, l_ref, mi_ref, mj_ref, pa, pb, c_ref, s_ref, k_ref) = scratch[:9]
    levels, level_sems = scratch[9:]
    row, lane = iotas()
    k = lane % BOX
    block = lane // BOX
    k_first, k_last = k == 0, k == BOX - 1
    top, bottom = row == 0, row == 7

    def next_k(v):
        return jnp.where(k_last, v, pltpu.roll(v, LANES - 1, 1))

    def prev_k(v):
        return jnp.where(k_first, v, pltpu.roll(v, 1, 1))

    def one_group(own):
        g = first_group + own
        spots = [[corner_ref[g * PER + b, d] for d in range(3)] for b in range(PER)]
        alive = jnp.zeros(TILE, F32)
        for b in range(PER):
            living = jnp.where(owner_ref[g * PER + b] >= 0, 1.0, 0.0)
            alive = jnp.where(block == b, living, alive)

        for b in range(PER):
            px, py, pz = spots[b]
            turn = (BOX * b + LANES - pz) % LANES
            here = block == b
            base = px * 32 + py

            @pl.loop(0, 6, unroll=CUT)
            def _(step):
                c = step // 2
                i0 = (step % 2) * 8
                for i in range(8):
                    for jt in range(2):
                        part = vel_ref[pl.ds(base + c * 1024 + (i0 + i) * 32 + 8 * jt, 8), :]
                        pltpu.store(
                            u_ref.at[c, i0 + i, pl.ds(8 * jt, 8), :],
                            pltpu.roll(part, turn, 1),
                            mask=here,
                        )

        for jt in range(2):
            come(own, jt).wait()

        @pl.loop(0, BOX, unroll=LEVEL)
        def _(i):
            for jt in range(2):
                x = levels[pl.ds((own + count * jt) * (PER * BOX) + i, 8, stride=BOX), :]
                l_ref[i, pl.ds(8 + 8 * jt, 8), :] = block_transpose(x, row, lane)

        mi_ref[0] = jnp.zeros((BOX, LANES), F32)
        mi_ref[1] = jnp.zeros((BOX, LANES), F32)
        mi_ref[2] = jnp.zeros((BOX, LANES), F32)

        @pl.loop(1, BOX, unroll=MI)
        def _(i):
            for jt in range(2):
                at = pl.ds(8 + 8 * jt, 8)
                mi_ref[i + 2, pl.ds(8 * jt, 8), :] = l_ref[i, at, :] - l_ref[i - 1, at, :]

        for t in range(3):
            mi_ref[18 + t] = mi_ref[17]

        @pl.loop(0, BOX, unroll=MJ)
        def _(i):
            for jt in range(2):
                here = l_ref[i, pl.ds(8 + 8 * jt, 8), :]
                m = here - l_ref[i, pl.ds(7 + 8 * jt, 8), :]
                if jt == 0:
                    m = jnp.where(top, 0.0, m)
                    mj_ref[i, pl.ds(0, 8), :] = jnp.zeros(TILE, F32)
                else:
                    mj_ref[i, pl.ds(24, 8), :] = jnp.broadcast_to(m[7:8, :], TILE)
                mj_ref[i, pl.ds(8 + 8 * jt, 8), :] = m

        @pl.loop(0, BOX, unroll=WENO)
        def _(i):
            for jt in range(2):
                at = pl.ds(8 * jt, 8)
                padded_at = pl.ds(8 + 8 * jt, 8)
                here = l_ref[i, padded_at, :]
                change = upwind(u_ref[0, i, at, :], *[mi_ref[i + t, at, :] for t in range(6)])
                change += upwind(
                    u_ref[1, i, at, :],
                    *[mj_ref[i, pl.ds(6 + t + 8 * jt, 8), :] for t in range(6)],
                )
                m = here - prev_k(here)
                back_one = prev_k(m)
                ahead_one = next_k(m)
                ahead_two = next_k(ahead_one)
                change += upwind(
                    u_ref[2, i, at, :],
                    prev_k(back_one),
                    back_one,
                    m,
                    ahead_one,
                    ahead_two,
                    next_k(ahead_two),
                )
                advected = here - box_step * change
                pa[i, padded_at, :] = advected
                c_ref[i, at, :] = pseudo_step * advected * lax.rsqrt(advected * advected + 1.0)
                s_ref[i, at, :] = jnp.where(advected > 0.0, 1.0, -1.0)

        def sweep(src, dst):
            for jt in range(2):
                at = pl.ds(8 * jt, 8)
                behind_i = None
                cur = src[0, pl.ds(8 + 8 * jt, 8), :]
                for i in range(BOX):
                    s = s_ref[i, at, :]
                    terms = []
                    sc = s * cur
                    if i < BOX - 1:
                        nxt = src[i + 1, pl.ds(8 + 8 * jt, 8), :]
                        sides = s * nxt if behind_i is None else jnp.minimum(s * nxt, s * behind_i)
                    else:
                        nxt = None
                        sides = s * behind_i
                    terms.append(sc - jnp.minimum(sides, sc))
                    lower = src[i, pl.ds(7 + 8 * jt, 8), :]
                    upper = src[i, pl.ds(9 + 8 * jt, 8), :]
                    if jt == 0:
                        lower = jnp.where(top, cur, lower)
                    else:
                        upper = jnp.where(bottom, cur, upper)
                    terms.append(sc - jnp.minimum(jnp.minimum(s * lower, s * upper), sc))
                    lower = jnp.where(k_first, cur, pltpu.roll(cur, 1, 1))
                    upper = jnp.where(k_last, cur, pltpu.roll(cur, LANES - 1, 1))
                    terms.append(sc - jnp.minimum(jnp.minimum(s * lower, s * upper), sc))
                    squared = terms[0] * terms[0] + terms[1] * terms[1] + terms[2] * terms[2]
                    root = squared * lax.rsqrt(jnp.maximum(squared, 1e-37))
                    dst[i, pl.ds(8 + 8 * jt, 8), :] = cur - c_ref[i, at, :] * (root - 1.0)
                    behind_i, cur = cur, nxt

        @pl.loop(0, ITERS // 2)
        def _(_):
            sweep(pa, pb)
            sweep(pb, pa)

        def central(i, jt):
            at = pl.ds(8 + 8 * jt, 8)
            cur = pa[i, at, :]
            c0 = 0.5 * (pa[jnp.minimum(i + 1, BOX - 1), at, :] - pa[jnp.maximum(i - 1, 0), at, :])
            lower = pa[i, pl.ds(7 + 8 * jt, 8), :]
            upper = pa[i, pl.ds(9 + 8 * jt, 8), :]
            if jt == 0:
                lower = jnp.where(top, cur, lower)
            else:
                upper = jnp.where(bottom, cur, upper)
            c1 = 0.5 * (upper - lower)
            c2 = 0.5 * (next_k(cur) - prev_k(cur))
            return cur, c0, c1, c2

        @pl.loop(0, BOX, unroll=CENTRAL)
        def _(i):
            for jt in range(2):
                cur, c0, c1, c2 = central(i, jt)
                size = c0 * c0 + c1 * c1 + c2 * c2
                inverse = jnp.minimum(lax.rsqrt(size), 1.0 / normal_floor)
                at = pl.ds(8 * jt, 8)
                mi_ref[i, at, :] = c0 * inverse
                mj_ref[i, pl.ds(8 + 8 * jt, 8), :] = c1 * inverse
                n3 = c2 * inverse
                k_ref[i, at, :] = next_k(n3) - prev_k(n3)
                scaled = cur * (1.0 / band_width)
                band = jnp.exp(-(scaled * scaled)) * (
                    grid_step * tension / (band_width * math.sqrt(math.pi))
                )
                band = band * alive
                for c, slope in enumerate((c0, c1, c2)):
                    force_out[own, c, i, at, :] = band * slope
                y = block_transpose(cur * alive, row, lane)
                turned[pl.ds((own * 2 + jt) * (PER * BOX) + i, 8, stride=BOX), :] = y

        @pl.loop(0, BOX, unroll=KAPPA)
        def _(i):
            for jt in range(2):
                at = pl.ds(8 * jt, 8)
                padded_at = pl.ds(8 + 8 * jt, 8)
                d1 = mi_ref[jnp.minimum(i + 1, BOX - 1), at, :] - mi_ref[jnp.maximum(i - 1, 0), at, :]
                lower = mj_ref[i, pl.ds(7 + 8 * jt, 8), :]
                upper = mj_ref[i, pl.ds(9 + 8 * jt, 8), :]
                if jt == 0:
                    lower = jnp.where(top, mj_ref[i, padded_at, :], lower)
                else:
                    upper = jnp.where(bottom, mj_ref[i, padded_at, :], upper)
                kappa = 0.5 * (d1 + (upper - lower) + k_ref[i, at, :])
                for c in range(3):
                    force_out[own, c, i, at, :] = force_out[own, c, i, at, :] * kappa
                y = block_transpose(kappa * alive, row, lane)
                turned_kappa[pl.ds((own * 2 + jt) * (PER * BOX) + i, 8, stride=BOX), :] = y

    def come(own, jt):
        return pltpu.make_async_copy(
            level_ref.at[
                pl.ds((first_group + own) * (PER * BOX), PER * BOX), pl.ds(LANES * jt, LANES)
            ],
            levels.at[pl.ds((own + count * jt) * (PER * BOX), PER * BOX), :],
            level_sems.at[own, jt],
        )

    for own in range(count):
        for jt in range(2):
            come(own, jt).start()

    @pl.loop(0, count)
    def _(own):
        one_group(own)


def boxes(first_group, count, owner, corners, rows, level_rows, after):
    smem = pl.BlockSpec(memory_space=pltpu.SMEM)
    hbm = pl.BlockSpec(memory_space=pltpu.HBM)
    vmem = pl.BlockSpec(memory_space=pltpu.VMEM)
    any_ = pl.BlockSpec(memory_space=pl.ANY)
    plane = lambda *lead: pltpu.VMEM((*lead, LANES), F32)
    turned = jax.ShapeDtypeStruct((count * 2 * PER * BOX, LANES), F32)
    return pl.pallas_call(
        functools.partial(box_body, first_group, count),
        out_shape=(jax.ShapeDtypeStruct((count, 3, BOX, BOX, LANES), F32), turned, turned),
        in_specs=[smem, smem, vmem, hbm, any_],
        out_specs=(vmem,) * 3,
        scratch_shapes=[
            plane(3, BOX, BOX),
            plane(BOX, ROWS),
            plane(BOX + 5, BOX),
            plane(BOX, ROWS),
            plane(BOX, ROWS),
            plane(BOX, ROWS),
            plane(BOX, BOX),
            plane(BOX, BOX),
            plane(BOX, BOX),
            plane(count * 2 * PER * BOX),
            pltpu.SemaphoreType.DMA((count, 2)),
        ],
        compiler_params=pltpu.CompilerParams(vmem_limit_bytes=16 * 2**20),
        cost_estimate=pl.CostEstimate(
            flops=30_000_000, bytes_accessed=5_000_000, transcendentals=0
        ),
        name="boxes",
    )(owner, corners, rows, level_rows, after)


def deposit(force_refs, corner_ref, grid_ref, c):
    _, lane = iotas()

    def one_group(ref, own, g):
        for b in range(PER):
            px, py, pz = [corner_ref[g * PER + b, d] for d in range(3)]
            inside = (lane >= pz) & (lane < pz + BOX)
            turn = (pz + LANES - BOX * b) % LANES
            base = c * 1024 + px * 32 + py
            for i0 in (0, 8):
                sums = []
                for i in range(8):
                    for jt in range(2):
                        old = grid_ref[pl.ds(base + (i0 + i) * 32 + 8 * jt, 8), :]
                        push = pltpu.roll(ref[own, c, i0 + i, pl.ds(8 * jt, 8), :], turn, 1)
                        sums.append(old + jnp.where(inside, push, 0.0))
                for i in range(8):
                    for jt in range(2):
                        grid_ref[pl.ds(base + (i0 + i) * 32 + 8 * jt, 8), :] = sums[2 * i + jt]

    done = 0
    for ref in force_refs:
        count = ref.shape[0]

        @pl.loop(0, count)
        def _(own):
            one_group(ref, own, done + own)

        done += count


PLANE = 48


PACKED = jax.ShapeDtypeStruct((2, 3, 8, LANES), F32)
Y_ROWS = 80
X_ROWS = 88


def z_faces(rows_ref, kept_ref, near_ref, far_ref):
    _, lane = iotas()
    even = is_even("gz")

    def one(x, packed):
        out = []
        for c in range(3):
            parts = packed[4 * c : 4 * c + 4]
            for yt in range(4):
                n = x * 4 + yt
                at = pl.multiple_of(c * 1024 + x * 32 + 8 * yt, 8)
                tile = rows_ref[pl.ds(at, 8), :]
                kept_ref[pl.ds(at, 8), :] = tile
                turned = pltpu.roll(tile, n, 1)
                parts = [
                    jnp.where(lane == (n + shift + LANES) % LANES, turned, part)
                    for shift, part in zip((0, 1, -1, -2), parts)
                ]
            out += parts
        return tuple(out)

    packed = lax.fori_loop(0, 32, one, (jnp.zeros(TILE, F32),) * 12, unroll=PLANES)
    for c in range(3):
        first, second, last, before = packed[4 * c : 4 * c + 4]
        lower = (first, pltpu.roll(second, LANES - 1, 1))
        upper = (pltpu.roll(last, 1, 1), pltpu.roll(before, 2, 1))
        for layer in range(2):
            near_ref[layer, c] = jnp.where(even, upper[layer], lower[layer])
            far_ref[layer, c] = jnp.where(even, lower[layer], upper[layer])


def y_faces(rows_ref, z_near, z_far, _, near_ref, far_ref):
    even, z_even = is_even("gy"), is_even("gz")
    for out, upper in ((near_ref, even), (far_ref, jnp.logical_not(even))):
        for c in range(3):
            for n in range(2):
                y = jnp.where(upper, 31 - n, n)
                out[c, pl.ds(32 * n, 32), :] = rows_ref[pl.ds(c * 1024 + y, 32, stride=32), :]
            out[c, pl.ds(64, 8), :] = jnp.where(z_even, z_far[0, c], z_near[0, c])
            out[c, pl.ds(72, 8), :] = jnp.where(z_even, z_near[0, c], z_far[0, c])


def x_faces(rows_ref, z_near, z_far, y_near, y_far, _, near_ref, far_ref):
    even, y_even, z_even = is_even("gx"), is_even("gy"), is_even("gz")
    for out, upper in ((near_ref, even), (far_ref, jnp.logical_not(even))):
        for c in range(3):
            for n in range(2):
                x = jnp.where(upper, 31 - n, n)
                at = pl.multiple_of(c * 1024 + 32 * x, 8)
                out[c, pl.ds(32 * n, 32), :] = rows_ref[pl.ds(at, 32), :]
            x = jnp.where(upper, 31, 0)
            near, far = y_near[c, pl.ds(x, 1), :], y_far[c, pl.ds(x, 1), :]
            out[c, pl.ds(64, 8), :] = jnp.zeros(TILE, F32)
            out[c, pl.ds(64, 1), :] = jnp.where(y_even, far, near)
            out[c, pl.ds(65, 1), :] = jnp.where(y_even, near, far)
            out[c, pl.ds(72, 8), :] = jnp.where(z_even, z_far[0, c], z_near[0, c])
            out[c, pl.ds(80, 8), :] = jnp.where(z_even, z_near[0, c], z_far[0, c])


def exchange(first, second, axis):
    size = lax.axis_size(axis)
    near = [(i, i ^ 1) for i in range(size)]
    far = [(i, (i + 1) % size if i % 2 else (i - 1) % size) for i in range(size)]
    return lax.ppermute(first, axis, near), lax.ppermute(second, axis, far)


def is_even(axis):
    return lax.axis_index(axis) % 2 == 0


def slopes_to_f(centre, v, lower, upper):
    advect = sum(centre[d] * (upper[d] - lower[d]) for d in range(3))
    spread = (upper[0] + lower[0]) + (upper[1] + lower[1]) + (upper[2] + lower[2]) - 6.0 * v
    return viscosity * spread - 0.5 * advect


def along_z(v, before, after, lane):
    lower = jnp.where(lane == 0, before, pltpu.roll(v, 1, 1))
    upper = jnp.where(lane == LANES - 1, after, pltpu.roll(v, LANES - 1, 1))
    return lower, upper


def tile_step(ext, planes, plane, yt, below, above, n, lane):
    at = [
        pl.multiple_of((c * planes + plane) * PLANE + 8 + 8 * yt, 8) for c in range(3)
    ]
    centre = [ext[pl.ds(at[c], 8), :] for c in range(3)]
    out = []
    for c in range(3):
        v = centre[c]
        lower2, upper2 = along_z(
            v,
            pltpu.roll(below[c], (LANES - n) % LANES, 1),
            pltpu.roll(above[c], LANES - 1 - n, 1),
            lane,
        )
        lower = (ext[pl.ds(at[c] - PLANE, 8), :], ext[pl.ds(at[c] - 1, 8), :], lower2)
        upper = (ext[pl.ds(at[c] + PLANE, 8), :], ext[pl.ds(at[c] + 1, 8), :], upper2)
        out.append(v + grid_step * slopes_to_f(centre, v, lower, upper))
    return out


def packed_step(own, beyond, inner, x_sides, y_sides, outward, row, lane):
    out = []
    for c in range(3):
        v = own[c]
        x_lower = jnp.where(lane < 4, pltpu.roll(x_sides[0][c], 4, 1), pltpu.roll(v, 4, 1))
        x_upper = jnp.where(
            lane >= LANES - 4,
            pltpu.roll(x_sides[1][c], LANES - 4, 1),
            pltpu.roll(v, LANES - 4, 1),
        )
        down = pltpu.roll(v, 1, 0)
        down_side = pltpu.roll(pltpu.roll(y_sides[0][c], 1, 0), LANES - 3, 1)
        y_lower = jnp.where(
            row == 0, jnp.where(lane % 4 == 0, down_side, pltpu.roll(down, 1, 1)), down
        )
        up = pltpu.roll(v, 7, 0)
        up_side = pltpu.roll(pltpu.roll(y_sides[1][c], 7, 0), 3, 1)
        y_upper = jnp.where(
            row == 7, jnp.where(lane % 4 == 3, up_side, pltpu.roll(up, LANES - 1, 1)), up
        )
        pair = (inner[c], beyond[c]) if outward else (beyond[c], inner[c])
        f = slopes_to_f(own, v, (x_lower, y_lower, pair[0]), (x_upper, y_upper, pair[1]))
        out.append(v + grid_step * f)
    return out


def momentum_body(
    vel_ref, face_near, face_far, z_near, z_far, y_near, y_far, x_near, x_far, *refs,
):
    forces, settled, bending, corner_ref = refs[:3], refs[3:6], refs[6:9], refs[9]
    new_out, settled_out, bending_out, ext, later, sides, packed, out_ref, sems, grid_sems = refs[10:20]
    own_faces, z_halos, y_halos, x_halos = refs[20:]
    row, lane = iotas()
    for axis, kept, near, far in (
        ("gz", own_faces, face_near, face_far),
        ("gz", z_halos, z_near, z_far),
        ("gy", y_halos, y_near, y_far),
        ("gx", x_halos, x_near, x_far),
    ):
        upper = jnp.where(is_even(axis), 1, 0)
        kept[upper] = near[...]
        kept[1 - upper] = far[...]
    z_lo, z_hi = own_faces.at[0], own_faces.at[1]
    below, above = z_halos.at[0], z_halos.at[1]
    left, right = y_halos.at[0], y_halos.at[1]
    front, back = x_halos.at[0], x_halos.at[1]

    leaving = []
    for n, (parts, out) in enumerate(((settled, settled_out), (bending, bending_out))):
        group = 0
        for part in parts:
            for own in range(part.shape[0] // (2 * PER * BOX)):
                for jt in range(2):
                    leaving.append(
                        pltpu.make_async_copy(
                            part.at[pl.ds((own * 2 + jt) * (PER * BOX), PER * BOX), :],
                            out.at[
                                pl.ds(group * (PER * BOX), PER * BOX), pl.ds(LANES * jt, LANES)
                            ],
                            sems.at[n, group, jt],
                        )
                    )
                group += 1
    for copy in leaving:
        copy.start()

    for c in range(3):
        base = c * 36 * PLANE
        for plane, halo, layer in ((1, front, 0), (0, front, 1), (34, back, 0), (35, back, 1)):
            ext[pl.ds(base + plane * PLANE + 8, 32), :] = halo[c, pl.ds(32 * layer, 32), :]
        for plane, halo in ((1, front), (34, back)):
            ext[pl.ds(base + plane * PLANE + 7, 1), :] = halo[c, pl.ds(64, 1), :]
            ext[pl.ds(base + plane * PLANE + 40, 1), :] = halo[c, pl.ds(65, 1), :]
        ext[pl.ds(base + 2 * PLANE + 7, 32, stride=PLANE), :] = left[c, pl.ds(0, 32), :]
        ext[pl.ds(base + 2 * PLANE + 40, 32, stride=PLANE), :] = right[c, pl.ds(0, 32), :]

    @pl.loop(0, 32)
    def _(x):
        for c in range(3):
            at = pl.multiple_of((c * 36 + x + 2) * PLANE + 8, 8)
            ext[pl.ds(at, 32), :] = vel_ref[pl.ds(pl.multiple_of(c * 1024 + x * 32, 8), 32), :]

    @pl.loop(0, 32, unroll=PLANES)
    def _(x):
        lo = [below[0, c] for c in range(3)]
        hi = [above[0, c] for c in range(3)]
        for yt in range(4):
            new = tile_step(ext, 36, x + 2, yt, lo, hi, x * 4 + yt, lane)
            for c in range(3):
                at = pl.multiple_of((c * 34 + x + 1) * PLANE + 8 + 8 * yt, 8)
                later[pl.ds(at, 8), :] = new[c]

    for halo, plane, x in ((front, 1, 31), (back, 34, 0)):
        lo = [halo[c, pl.ds(72, 8), :] for c in range(3)]
        hi = [halo[c, pl.ds(80, 8), :] for c in range(3)]
        for yt in range(4):
            new = tile_step(ext, 36, plane, yt, lo, hi, x * 4 + yt, lane)
            for c in range(3):
                later[pl.ds((c * 34 + plane - 1) * PLANE + 8 + 8 * yt, 8), :] = new[c]

    for halo, out_row, y, inside in ((left, 7, 31, 0), (right, 40, 0, 31)):
        for c in range(3):
            sides[c, pl.ds(8, 32), :] = halo[c, pl.ds(0, 32), :]
            for at, end in ((7, front), (40, back)):
                sides[c, pl.ds(at, 1), :] = end[c, pl.ds(64 if out_row == 7 else 65, 1), :]
        for t in range(4):
            at = pl.ds(8 + 8 * t, 8)
            centre = [sides[c, at, :] for c in range(3)]
            where_x = 4 * (8 * t + row) + y // 8
            for c in range(3):
                v = centre[c]
                ends = [
                    jnp.take_along_axis(
                        jnp.broadcast_to(halo[c, pl.ds(64 + 8 * e + y % 8, 1), :], TILE),
                        where_x,
                        axis=1,
                    )
                    for e in range(2)
                ]
                lower2, upper2 = along_z(v, *ends, lane)
                beyond = halo[c, pl.ds(32 + 8 * t, 8), :]
                inner = vel_ref[pl.ds(c * 1024 + 8 * t * 32 + inside, 8, stride=32), :]
                pair = (beyond, inner) if out_row == 7 else (inner, beyond)
                lower = (sides[c, pl.ds(7 + 8 * t, 8), :], pair[0], lower2)
                upper = (sides[c, pl.ds(9 + 8 * t, 8), :], pair[1], upper2)
                new = v + grid_step * slopes_to_f(centre, v, lower, upper)
                rows = pl.ds((c * 34 + 8 * t + 1) * PLANE + out_row, 8, stride=PLANE)
                later[rows, :] = new

    for outward, halo, own_face in ((0, below, z_lo), (1, above, z_hi)):
        x_at, y_at = pl.ds(72 + 8 * outward, 8), pl.ds(64 + 8 * outward, 8)
        new = packed_step(
            [halo[0, c] for c in range(3)],
            [halo[1, c] for c in range(3)],
            [own_face[0, c] for c in range(3)],
            [[side[c, x_at, :] for c in range(3)] for side in (front, back)],
            [[side[c, y_at, :] for c in range(3)] for side in (left, right)],
            outward,
            row,
            lane,
        )
        for c in range(3):
            packed[outward, c] = new[c]

    @pl.loop(0, 32, unroll=PLANES)
    def _(x):
        lo = [packed[0, c] for c in range(3)]
        hi = [packed[1, c] for c in range(3)]
        for yt in range(4):
            new = tile_step(later, 34, x + 1, yt, lo, hi, x * 4 + yt, lane)
            for c in range(3):
                at = pl.ds(pl.multiple_of(c * 1024 + x * 32 + 8 * yt, 8), 8)
                out_ref[at, :] = 0.5 * (vel_ref[at, :] + new[c])

    for c in range(3):
        deposit(forces, corner_ref, out_ref, c)
        at = pl.ds(c * 1024, 1024)
        leaving.append(
            pltpu.make_async_copy(out_ref.at[at, :], new_out.at[at, :], grid_sems.at[c])
        )
        leaving[-1].start()
    for copy in leaving:
        copy.wait()


def call(body, out_shape, operands, name, unread=0):
    vmem = pl.BlockSpec(memory_space=pltpu.VMEM)
    specs = [vmem] * (len(operands) - unread) + [pl.BlockSpec(memory_space=pl.ANY)] * unread
    return pl.pallas_call(
        body,
        out_shape=out_shape,
        in_specs=specs,
        out_specs=jax.tree.map(lambda _: vmem, out_shape),
        compiler_params=pltpu.CompilerParams(vmem_limit_bytes=8 * 2**20),
        name=name,
    )(*operands)


def local(velocity, box_level, corners, owner_list):
    slots = box_level.shape[0]
    level_rows = box_level.reshape(slots * BOX, BOX * BOX)
    rows = velocity.reshape(-1, LANES)
    kept = jax.ShapeDtypeStruct(rows.shape, F32)
    rows, *z_own = call(z_faces, (kept, PACKED, PACKED), [rows], "z_faces")
    z_halos = exchange(*z_own, "gz")
    work = functools.partial(
        boxes, owner=owner_list, corners=corners, rows=rows, level_rows=level_rows
    )
    first = work(0, 1, after=z_own[0])
    sent = jax.ShapeDtypeStruct((3, Y_ROWS, LANES), F32)
    faces = call(y_faces, (sent,) * 2, [rows, *z_halos, first[0]], "y_faces", unread=1)
    y_halos = exchange(*faces, "gy")
    second = work(1, 1, after=faces[0])
    sent = jax.ShapeDtypeStruct((3, X_ROWS, LANES), F32)
    faces = call(
        x_faces, (sent,) * 2, [rows, *z_halos, *y_halos, second[0]], "x_faces", unread=1
    )
    x_halos = exchange(*faces, "gx")
    third = work(2, slots // PER - 2, after=faces[0])
    parts = [part for kind in zip(first, second, third) for part in kind]
    operands = [rows, *z_own, *z_halos, *y_halos, *x_halos, *parts]
    hbm = pl.BlockSpec(memory_space=pltpu.HBM)
    boxed = jax.ShapeDtypeStruct(level_rows.shape, F32)
    result, settled, bending = pl.pallas_call(
        momentum_body,
        out_shape=(jax.ShapeDtypeStruct(rows.shape, F32), boxed, boxed),
        in_specs=[pl.BlockSpec(memory_space=pltpu.VMEM)] * len(operands)
        + [pl.BlockSpec(memory_space=pltpu.SMEM)],
        out_specs=(hbm,) * 3,
        scratch_shapes=[
            pltpu.VMEM((3 * 36 * PLANE, LANES), F32),
            pltpu.VMEM((3 * 34 * PLANE, LANES), F32),
            pltpu.VMEM((3, PLANE, LANES), F32),
            pltpu.VMEM((2, 3, 8, LANES), F32),
            pltpu.VMEM(rows.shape, F32),
            pltpu.SemaphoreType.DMA((2, slots // PER, 2)),
            pltpu.SemaphoreType.DMA((3,)),
            pltpu.VMEM((2, *PACKED.shape), F32),
            pltpu.VMEM((2, *PACKED.shape), F32),
            pltpu.VMEM((2, 3, Y_ROWS, LANES), F32),
            pltpu.VMEM((2, 3, X_ROWS, LANES), F32),
        ],
        compiler_params=pltpu.CompilerParams(vmem_limit_bytes=24 * 2**20),
        name="momentum",
    )(*operands, corners)
    return (
        result.reshape(velocity.shape),
        settled.reshape(box_level.shape),
        bending.reshape(box_level.shape),
    )


def solution(mesh):
    placed = (
        P(None, "gx", "gy", "gz"),
        P(("gx", "gy", "gz"), None, None),
        P(("gx", "gy", "gz"), None),
        P(("gx", "gy", "gz")),
    )
    return jax.shard_map(
        local,
        mesh=mesh,
        in_specs=placed,
        out_specs=(
            P(None, "gx", "gy", "gz"),
            P(("gx", "gy", "gz"), None, None),
            P(("gx", "gy", "gz"), None, None),
        ),
        check_vma=False,
    )
```

```python
import functools
import math

import jax
import jax.numpy as jnp
from jax import lax
from jax.experimental import pallas as pl
from jax.experimental.pallas import tpu as pltpu
from jax.sharding import PartitionSpec as P

ITERS = 12
BOX = 16
LANES = 128
PER = 8

CUT, LEVEL, MI, MJ, WENO, CENTRAL, KAPPA, PLANES = 6, 8, 5, 4, 16, 8, 16, 8

box_step = 0.25
pseudo_step = 0.3
weno_floor = 1e-06
band_width = 1.5
tension = 2.0
grid_step = 0.2
viscosity = 0.1
normal_floor = 0.5

F32 = jnp.float32
TILE = (8, LANES)


def iotas():
    row = lax.broadcasted_iota(jnp.int32, TILE, 0)
    lane = lax.broadcasted_iota(jnp.int32, TILE, 1)
    return row, lane


def block_transpose(x, row, lane):
    block = lane // BOX
    x = jnp.take_along_axis(x, (lane - BOX * row) % LANES, axis=1)
    x = jnp.take_along_axis(x, (block - row) % 8, axis=0)
    return jnp.take_along_axis(x, (lane + BOX * row) % LANES, axis=1)


def weno(a, b, c, e, f):
    ab, bc, ce, ef = a - b, b - c, c - e, e - f
    d1, d2, d3 = ab - bc, bc - ce, ce - ef
    bc2, ce2 = bc + bc, ce + ce
    t1, t2, t3 = d1 - bc2, bc + ce, d3 + ce2
    part = 3.0 / 13.0
    floor = weno_floor * 12.0 / 13.0
    s1 = (d1 * d1 + floor) + part * (t1 * t1)
    s2 = (d2 * d2 + floor) + part * (t2 * t2)
    s3 = (d3 * d3 + floor) + part * (t3 * t3)
    q1, q2, q3 = s1 * s1, s2 * s2, s3 * s3
    w1 = q2 * q3
    w2 = 6.0 * (q1 * q3)
    w3 = 3.0 * (q1 * q2)
    top = w1 * ((ab + ab) - 5.0 * bc) - w2 * (bc + ce2) + w3 * (ef - (ce2 + ce2))
    return c + top / (6.0 * (w1 + w2 + w3))


def upwind(speed, back_two, back_one, here, ahead_one, ahead_two, ahead_three):
    pos = speed > 0.0
    return speed * weno(
        jnp.where(pos, back_two, ahead_three),
        jnp.where(pos, back_one, ahead_two),
        jnp.where(pos, here, ahead_one),
        jnp.where(pos, ahead_one, here),
        jnp.where(pos, ahead_two, back_one),
    )


ROWS = 32


def box_body(first_group, count, owner_ref, corner_ref, vel_ref, level_ref, *rest):
    (force_out, turned, turned_kappa, *scratch) = rest[-14:]
    (u_ref, l_ref, mi_ref, mj_ref, pa, pb, c_ref, s_ref, k_ref) = scratch[:9]
    levels, level_sems = scratch[9:]
    row, lane = iotas()
    k = lane % BOX
    block = lane // BOX
    k_first, k_last = k == 0, k == BOX - 1
    top, bottom = row == 0, row == 7

    def next_k(v):
        return jnp.where(k_last, v, pltpu.roll(v, LANES - 1, 1))

    def prev_k(v):
        return jnp.where(k_first, v, pltpu.roll(v, 1, 1))

    def one_group(own):
        g = first_group + own
        spots = [[corner_ref[g * PER + b, d] for d in range(3)] for b in range(PER)]
        alive = jnp.zeros(TILE, F32)
        for b in range(PER):
            living = jnp.where(owner_ref[g * PER + b] >= 0, 1.0, 0.0)
            alive = jnp.where(block == b, living, alive)

        for b in range(PER):
            px, py, pz = spots[b]
            turn = (BOX * b + LANES - pz) % LANES
            here = block == b
            base = px * 32 + py

            @pl.loop(0, 6, unroll=CUT)
            def _(step):
                c = step // 2
                i0 = (step % 2) * 8
                for i in range(8):
                    for jt in range(2):
                        part = vel_ref[pl.ds(base + c * 1024 + (i0 + i) * 32 + 8 * jt, 8), :]
                        pltpu.store(
                            u_ref.at[c, i0 + i, pl.ds(8 * jt, 8), :],
                            pltpu.roll(part, turn, 1),
                            mask=here,
                        )

        for jt in range(2):
            come(own, jt).wait()

        @pl.loop(0, BOX, unroll=LEVEL)
        def _(i):
            for jt in range(2):
                x = levels[pl.ds((own + count * jt) * (PER * BOX) + i, 8, stride=BOX), :]
                l_ref[i, pl.ds(8 + 8 * jt, 8), :] = block_transpose(x, row, lane)

        mi_ref[0] = jnp.zeros((BOX, LANES), F32)
        mi_ref[1] = jnp.zeros((BOX, LANES), F32)
        mi_ref[2] = jnp.zeros((BOX, LANES), F32)

        @pl.loop(1, BOX, unroll=MI)
        def _(i):
            for jt in range(2):
                at = pl.ds(8 + 8 * jt, 8)
                mi_ref[i + 2, pl.ds(8 * jt, 8), :] = l_ref[i, at, :] - l_ref[i - 1, at, :]

        for t in range(3):
            mi_ref[18 + t] = mi_ref[17]

        @pl.loop(0, BOX, unroll=MJ)
        def _(i):
            for jt in range(2):
                here = l_ref[i, pl.ds(8 + 8 * jt, 8), :]
                m = here - l_ref[i, pl.ds(7 + 8 * jt, 8), :]
                if jt == 0:
                    m = jnp.where(top, 0.0, m)
                    mj_ref[i, pl.ds(0, 8), :] = jnp.zeros(TILE, F32)
                else:
                    mj_ref[i, pl.ds(24, 8), :] = jnp.broadcast_to(m[7:8, :], TILE)
                mj_ref[i, pl.ds(8 + 8 * jt, 8), :] = m

        @pl.loop(0, BOX, unroll=WENO)
        def _(i):
            for jt in range(2):
                at = pl.ds(8 * jt, 8)
                padded_at = pl.ds(8 + 8 * jt, 8)
                here = l_ref[i, padded_at, :]
                change = upwind(u_ref[0, i, at, :], *[mi_ref[i + t, at, :] for t in range(6)])
                change += upwind(
                    u_ref[1, i, at, :],
                    *[mj_ref[i, pl.ds(6 + t + 8 * jt, 8), :] for t in range(6)],
                )
                m = here - prev_k(here)
                back_one = prev_k(m)
                ahead_one = next_k(m)
                ahead_two = next_k(ahead_one)
                change += upwind(
                    u_ref[2, i, at, :],
                    prev_k(back_one),
                    back_one,
                    m,
                    ahead_one,
                    ahead_two,
                    next_k(ahead_two),
                )
                advected = here - box_step * change
                pa[i, padded_at, :] = advected
                c_ref[i, at, :] = pseudo_step * advected * lax.rsqrt(advected * advected + 1.0)
                s_ref[i, at, :] = jnp.where(advected > 0.0, 1.0, -1.0)

        def sweep(src, dst):
            for jt in range(2):
                at = pl.ds(8 * jt, 8)
                behind_i = None
                cur = src[0, pl.ds(8 + 8 * jt, 8), :]
                for i in range(BOX):
                    s = s_ref[i, at, :]
                    terms = []
                    sc = s * cur
                    if i < BOX - 1:
                        nxt = src[i + 1, pl.ds(8 + 8 * jt, 8), :]
                        sides = s * nxt if behind_i is None else jnp.minimum(s * nxt, s * behind_i)
                    else:
                        nxt = None
                        sides = s * behind_i
                    terms.append(sc - jnp.minimum(sides, sc))
                    lower = src[i, pl.ds(7 + 8 * jt, 8), :]
                    upper = src[i, pl.ds(9 + 8 * jt, 8), :]
                    if jt == 0:
                        lower = jnp.where(top, cur, lower)
                    else:
                        upper = jnp.where(bottom, cur, upper)
                    terms.append(sc - jnp.minimum(jnp.minimum(s * lower, s * upper), sc))
                    lower = jnp.where(k_first, cur, pltpu.roll(cur, 1, 1))
                    upper = jnp.where(k_last, cur, pltpu.roll(cur, LANES - 1, 1))
                    terms.append(sc - jnp.minimum(jnp.minimum(s * lower, s * upper), sc))
                    squared = terms[0] * terms[0] + terms[1] * terms[1] + terms[2] * terms[2]
                    root = squared * lax.rsqrt(jnp.maximum(squared, 1e-37))
                    dst[i, pl.ds(8 + 8 * jt, 8), :] = cur - c_ref[i, at, :] * (root - 1.0)
                    behind_i, cur = cur, nxt

        @pl.loop(0, ITERS // 2)
        def _(_):
            sweep(pa, pb)
            sweep(pb, pa)

        def central(i, jt):
            at = pl.ds(8 + 8 * jt, 8)
            cur = pa[i, at, :]
            c0 = 0.5 * (pa[jnp.minimum(i + 1, BOX - 1), at, :] - pa[jnp.maximum(i - 1, 0), at, :])
            lower = pa[i, pl.ds(7 + 8 * jt, 8), :]
            upper = pa[i, pl.ds(9 + 8 * jt, 8), :]
            if jt == 0:
                lower = jnp.where(top, cur, lower)
            else:
                upper = jnp.where(bottom, cur, upper)
            c1 = 0.5 * (upper - lower)
            c2 = 0.5 * (next_k(cur) - prev_k(cur))
            return cur, c0, c1, c2

        @pl.loop(0, BOX, unroll=CENTRAL)
        def _(i):
            for jt in range(2):
                cur, c0, c1, c2 = central(i, jt)
                size = c0 * c0 + c1 * c1 + c2 * c2
                inverse = jnp.minimum(lax.rsqrt(size), 1.0 / normal_floor)
                at = pl.ds(8 * jt, 8)
                mi_ref[i, at, :] = c0 * inverse
                mj_ref[i, pl.ds(8 + 8 * jt, 8), :] = c1 * inverse
                n3 = c2 * inverse
                k_ref[i, at, :] = next_k(n3) - prev_k(n3)
                scaled = cur * (1.0 / band_width)
                band = jnp.exp(-(scaled * scaled)) * (
                    grid_step * tension / (band_width * math.sqrt(math.pi))
                )
                band = band * alive
                for c, slope in enumerate((c0, c1, c2)):
                    force_out[own, c, i, at, :] = band * slope
                y = block_transpose(cur * alive, row, lane)
                turned[pl.ds((own * 2 + jt) * (PER * BOX) + i, 8, stride=BOX), :] = y

        @pl.loop(0, BOX, unroll=KAPPA)
        def _(i):
            for jt in range(2):
                at = pl.ds(8 * jt, 8)
                padded_at = pl.ds(8 + 8 * jt, 8)
                d1 = mi_ref[jnp.minimum(i + 1, BOX - 1), at, :] - mi_ref[jnp.maximum(i - 1, 0), at, :]
                lower = mj_ref[i, pl.ds(7 + 8 * jt, 8), :]
                upper = mj_ref[i, pl.ds(9 + 8 * jt, 8), :]
                if jt == 0:
                    lower = jnp.where(top, mj_ref[i, padded_at, :], lower)
                else:
                    upper = jnp.where(bottom, mj_ref[i, padded_at, :], upper)
                kappa = 0.5 * (d1 + (upper - lower) + k_ref[i, at, :])
                for c in range(3):
                    force_out[own, c, i, at, :] = force_out[own, c, i, at, :] * kappa
                y = block_transpose(kappa * alive, row, lane)
                turned_kappa[pl.ds((own * 2 + jt) * (PER * BOX) + i, 8, stride=BOX), :] = y

    def come(own, jt):
        return pltpu.make_async_copy(
            level_ref.at[
                pl.ds((first_group + own) * (PER * BOX), PER * BOX), pl.ds(LANES * jt, LANES)
            ],
            levels.at[pl.ds((own + count * jt) * (PER * BOX), PER * BOX), :],
            level_sems.at[own, jt],
        )

    for own in range(count):
        for jt in range(2):
            come(own, jt).start()

    @pl.loop(0, count)
    def _(own):
        one_group(own)


def boxes(first_group, count, owner, corners, rows, level_rows, after):
    smem = pl.BlockSpec(memory_space=pltpu.SMEM)
    hbm = pl.BlockSpec(memory_space=pltpu.HBM)
    vmem = pl.BlockSpec(memory_space=pltpu.VMEM)
    any_ = pl.BlockSpec(memory_space=pl.ANY)
    plane = lambda *lead: pltpu.VMEM((*lead, LANES), F32)
    turned = jax.ShapeDtypeStruct((count * 2 * PER * BOX, LANES), F32)
    return pl.pallas_call(
        functools.partial(box_body, first_group, count),
        out_shape=(jax.ShapeDtypeStruct((count, 3, BOX, BOX, LANES), F32), turned, turned),
        in_specs=[smem, smem, vmem, hbm, any_],
        out_specs=(vmem,) * 3,
        scratch_shapes=[
            plane(3, BOX, BOX),
            plane(BOX, ROWS),
            plane(BOX + 5, BOX),
            plane(BOX, ROWS),
            plane(BOX, ROWS),
            plane(BOX, ROWS),
            plane(BOX, BOX),
            plane(BOX, BOX),
            plane(BOX, BOX),
            plane(count * 2 * PER * BOX),
            pltpu.SemaphoreType.DMA((count, 2)),
        ],
        compiler_params=pltpu.CompilerParams(vmem_limit_bytes=16 * 2**20),
        cost_estimate=pl.CostEstimate(
            flops=30_000_000, bytes_accessed=5_000_000, transcendentals=0
        ),
        name="boxes",
    )(owner, corners, rows, level_rows, after)


def deposit(force_refs, corner_ref, grid_ref, c):
    _, lane = iotas()

    def one_group(ref, own, g):
        for b in range(PER):
            px, py, pz = [corner_ref[g * PER + b, d] for d in range(3)]
            inside = (lane >= pz) & (lane < pz + BOX)
            turn = (pz + LANES - BOX * b) % LANES
            base = c * 1024 + px * 32 + py
            for i0 in (0, 8):
                sums = []
                for i in range(8):
                    for jt in range(2):
                        old = grid_ref[pl.ds(base + (i0 + i) * 32 + 8 * jt, 8), :]
                        push = pltpu.roll(ref[own, c, i0 + i, pl.ds(8 * jt, 8), :], turn, 1)
                        sums.append(old + jnp.where(inside, push, 0.0))
                for i in range(8):
                    for jt in range(2):
                        grid_ref[pl.ds(base + (i0 + i) * 32 + 8 * jt, 8), :] = sums[2 * i + jt]

    done = 0
    for ref in force_refs:
        count = ref.shape[0]

        @pl.loop(0, count)
        def _(own):
            one_group(ref, own, done + own)

        done += count


PLANE = 48


PACKED = jax.ShapeDtypeStruct((2, 3, 8, LANES), F32)
Y_ROWS = 80
X_ROWS = 88


def z_faces(rows_ref, kept_ref, near_ref, far_ref):
    _, lane = iotas()
    even = is_even("gz")

    def one(x, packed):
        out = []
        for c in range(3):
            parts = packed[4 * c : 4 * c + 4]
            for yt in range(4):
                n = x * 4 + yt
                at = pl.multiple_of(c * 1024 + x * 32 + 8 * yt, 8)
                tile = rows_ref[pl.ds(at, 8), :]
                kept_ref[pl.ds(at, 8), :] = tile
                turned = pltpu.roll(tile, n, 1)
                parts = [
                    jnp.where(lane == (n + shift + LANES) % LANES, turned, part)
                    for shift, part in zip((0, 1, -1, -2), parts)
                ]
            out += parts
        return tuple(out)

    packed = lax.fori_loop(0, 32, one, (jnp.zeros(TILE, F32),) * 12, unroll=PLANES)
    for c in range(3):
        first, second, last, before = packed[4 * c : 4 * c + 4]
        lower = (first, pltpu.roll(second, LANES - 1, 1))
        upper = (pltpu.roll(last, 1, 1), pltpu.roll(before, 2, 1))
        for layer in range(2):
            near_ref[layer, c] = jnp.where(even, upper[layer], lower[layer])
            far_ref[layer, c] = jnp.where(even, lower[layer], upper[layer])


def y_faces(rows_ref, z_near, z_far, _, near_ref, far_ref):
    even, z_even = is_even("gy"), is_even("gz")
    for out, upper in ((near_ref, even), (far_ref, jnp.logical_not(even))):
        for c in range(3):
            for n in range(2):
                y = jnp.where(upper, 31 - n, n)
                out[c, pl.ds(32 * n, 32), :] = rows_ref[pl.ds(c * 1024 + y, 32, stride=32), :]
            out[c, pl.ds(64, 8), :] = jnp.where(z_even, z_far[0, c], z_near[0, c])
            out[c, pl.ds(72, 8), :] = jnp.where(z_even, z_near[0, c], z_far[0, c])


def x_faces(rows_ref, z_near, z_far, y_near, y_far, _, near_ref, far_ref):
    even, y_even, z_even = is_even("gx"), is_even("gy"), is_even("gz")
    for out, upper in ((near_ref, even), (far_ref, jnp.logical_not(even))):
        for c in range(3):
            for n in range(2):
                x = jnp.where(upper, 31 - n, n)
                at = pl.multiple_of(c * 1024 + 32 * x, 8)
                out[c, pl.ds(32 * n, 32), :] = rows_ref[pl.ds(at, 32), :]
            x = jnp.where(upper, 31, 0)
            near, far = y_near[c, pl.ds(x, 1), :], y_far[c, pl.ds(x, 1), :]
            out[c, pl.ds(64, 8), :] = jnp.zeros(TILE, F32)
            out[c, pl.ds(64, 1), :] = jnp.where(y_even, far, near)
            out[c, pl.ds(65, 1), :] = jnp.where(y_even, near, far)
            out[c, pl.ds(72, 8), :] = jnp.where(z_even, z_far[0, c], z_near[0, c])
            out[c, pl.ds(80, 8), :] = jnp.where(z_even, z_near[0, c], z_far[0, c])


def exchange(first, second, axis):
    size = lax.axis_size(axis)
    near = [(i, i ^ 1) for i in range(size)]
    far = [(i, (i + 1) % size if i % 2 else (i - 1) % size) for i in range(size)]
    return lax.ppermute(first, axis, near), lax.ppermute(second, axis, far)


def is_even(axis):
    return lax.axis_index(axis) % 2 == 0


def slopes_to_f(centre, v, lower, upper):
    advect = sum(centre[d] * (upper[d] - lower[d]) for d in range(3))
    spread = (upper[0] + lower[0]) + (upper[1] + lower[1]) + (upper[2] + lower[2]) - 6.0 * v
    return viscosity * spread - 0.5 * advect


def along_z(v, before, after, lane):
    lower = jnp.where(lane == 0, before, pltpu.roll(v, 1, 1))
    upper = jnp.where(lane == LANES - 1, after, pltpu.roll(v, LANES - 1, 1))
    return lower, upper


def z_ends(below, above, lane):
    even = lane % 2 == 0
    out = []
    for lower, upper in zip(below, above):
        upper = pltpu.roll(upper, LANES - 1, 1)
        out.append((jnp.where(even, lower, upper), jnp.where(even, upper, lower)))
    return out


def tile_step(ext, planes, plane, yt, ends, n, lane):
    at = [
        pl.multiple_of((c * planes + plane) * PLANE + 8 + 8 * yt, 8) for c in range(3)
    ]
    centre = [ext[pl.ds(at[c], 8), :] for c in range(3)]
    out = []
    for c in range(3):
        v = centre[c]
        end = pltpu.roll(ends[c][yt % 2], (LANES - n) % LANES, 1)
        lower2, upper2 = along_z(v, end, end, lane)
        lower = (ext[pl.ds(at[c] - PLANE, 8), :], ext[pl.ds(at[c] - 1, 8), :], lower2)
        upper = (ext[pl.ds(at[c] + PLANE, 8), :], ext[pl.ds(at[c] + 1, 8), :], upper2)
        out.append(v + grid_step * slopes_to_f(centre, v, lower, upper))
    return out


def packed_step(own, beyond, inner, x_sides, y_sides, outward, row, lane):
    out = []
    for c in range(3):
        v = own[c]
        x_lower = jnp.where(lane < 4, pltpu.roll(x_sides[0][c], 4, 1), pltpu.roll(v, 4, 1))
        x_upper = jnp.where(
            lane >= LANES - 4,
            pltpu.roll(x_sides[1][c], LANES - 4, 1),
            pltpu.roll(v, LANES - 4, 1),
        )
        down = pltpu.roll(v, 1, 0)
        down_side = pltpu.roll(pltpu.roll(y_sides[0][c], 1, 0), LANES - 3, 1)
        y_lower = jnp.where(
            row == 0, jnp.where(lane % 4 == 0, down_side, pltpu.roll(down, 1, 1)), down
        )
        up = pltpu.roll(v, 7, 0)
        up_side = pltpu.roll(pltpu.roll(y_sides[1][c], 7, 0), 3, 1)
        y_upper = jnp.where(
            row == 7, jnp.where(lane % 4 == 3, up_side, pltpu.roll(up, LANES - 1, 1)), up
        )
        pair = (inner[c], beyond[c]) if outward else (beyond[c], inner[c])
        f = slopes_to_f(own, v, (x_lower, y_lower, pair[0]), (x_upper, y_upper, pair[1]))
        out.append(v + grid_step * f)
    return out


def momentum_body(
    vel_ref, face_near, face_far, z_near, z_far, y_near, y_far, x_near, x_far, *refs,
):
    forces, settled, bending, corner_ref = refs[:3], refs[3:6], refs[6:9], refs[9]
    new_out, settled_out, bending_out, ext, later, sides, packed, out_ref, sems, grid_sems = refs[10:20]
    own_faces, z_halos, y_halos, x_halos = refs[20:]
    row, lane = iotas()
    for axis, kept, near, far in (
        ("gz", own_faces, face_near, face_far),
        ("gz", z_halos, z_near, z_far),
        ("gy", y_halos, y_near, y_far),
        ("gx", x_halos, x_near, x_far),
    ):
        upper = jnp.where(is_even(axis), 1, 0)
        kept[upper] = near[...]
        kept[1 - upper] = far[...]
    z_lo, z_hi = own_faces.at[0], own_faces.at[1]
    below, above = z_halos.at[0], z_halos.at[1]
    left, right = y_halos.at[0], y_halos.at[1]
    front, back = x_halos.at[0], x_halos.at[1]

    leaving = []
    for n, (parts, out) in enumerate(((settled, settled_out), (bending, bending_out))):
        group = 0
        for part in parts:
            for own in range(part.shape[0] // (2 * PER * BOX)):
                for jt in range(2):
                    leaving.append(
                        pltpu.make_async_copy(
                            part.at[pl.ds((own * 2 + jt) * (PER * BOX), PER * BOX), :],
                            out.at[
                                pl.ds(group * (PER * BOX), PER * BOX), pl.ds(LANES * jt, LANES)
                            ],
                            sems.at[n, group, jt],
                        )
                    )
                group += 1
    for copy in leaving:
        copy.start()

    for c in range(3):
        base = c * 36 * PLANE
        for plane, halo, layer in ((1, front, 0), (0, front, 1), (34, back, 0), (35, back, 1)):
            ext[pl.ds(base + plane * PLANE + 8, 32), :] = halo[c, pl.ds(32 * layer, 32), :]
        for plane, halo in ((1, front), (34, back)):
            ext[pl.ds(base + plane * PLANE + 7, 1), :] = halo[c, pl.ds(64, 1), :]
            ext[pl.ds(base + plane * PLANE + 40, 1), :] = halo[c, pl.ds(65, 1), :]
        ext[pl.ds(base + 2 * PLANE + 7, 32, stride=PLANE), :] = left[c, pl.ds(0, 32), :]
        ext[pl.ds(base + 2 * PLANE + 40, 32, stride=PLANE), :] = right[c, pl.ds(0, 32), :]

    @pl.loop(0, 32)
    def _(x):
        for c in range(3):
            at = pl.multiple_of((c * 36 + x + 2) * PLANE + 8, 8)
            ext[pl.ds(at, 32), :] = vel_ref[pl.ds(pl.multiple_of(c * 1024 + x * 32, 8), 32), :]

    ends = z_ends([below[0, c] for c in range(3)], [above[0, c] for c in range(3)], lane)

    @pl.loop(0, 32, unroll=PLANES)
    def _(x):
        for yt in range(4):
            new = tile_step(ext, 36, x + 2, yt, ends, x * 4 + yt, lane)
            for c in range(3):
                at = pl.multiple_of((c * 34 + x + 1) * PLANE + 8 + 8 * yt, 8)
                later[pl.ds(at, 8), :] = new[c]

    for halo, plane, x in ((front, 1, 31), (back, 34, 0)):
        side_ends = z_ends(
            [halo[c, pl.ds(72, 8), :] for c in range(3)],
            [halo[c, pl.ds(80, 8), :] for c in range(3)],
            lane,
        )
        for yt in range(4):
            new = tile_step(ext, 36, plane, yt, side_ends, x * 4 + yt, lane)
            for c in range(3):
                later[pl.ds((c * 34 + plane - 1) * PLANE + 8 + 8 * yt, 8), :] = new[c]

    for halo, out_row, y, inside in ((left, 7, 31, 0), (right, 40, 0, 31)):
        for c in range(3):
            sides[c, pl.ds(8, 32), :] = halo[c, pl.ds(0, 32), :]
            for at, end in ((7, front), (40, back)):
                sides[c, pl.ds(at, 1), :] = end[c, pl.ds(64 if out_row == 7 else 65, 1), :]
        for t in range(4):
            at = pl.ds(8 + 8 * t, 8)
            centre = [sides[c, at, :] for c in range(3)]
            where_x = 4 * (8 * t + row) + y // 8
            for c in range(3):
                v = centre[c]
                ends = [
                    jnp.take_along_axis(
                        jnp.broadcast_to(halo[c, pl.ds(64 + 8 * e + y % 8, 1), :], TILE),
                        where_x,
                        axis=1,
                    )
                    for e in range(2)
                ]
                lower2, upper2 = along_z(v, *ends, lane)
                beyond = halo[c, pl.ds(32 + 8 * t, 8), :]
                inner = vel_ref[pl.ds(c * 1024 + 8 * t * 32 + inside, 8, stride=32), :]
                pair = (beyond, inner) if out_row == 7 else (inner, beyond)
                lower = (sides[c, pl.ds(7 + 8 * t, 8), :], pair[0], lower2)
                upper = (sides[c, pl.ds(9 + 8 * t, 8), :], pair[1], upper2)
                new = v + grid_step * slopes_to_f(centre, v, lower, upper)
                rows = pl.ds((c * 34 + 8 * t + 1) * PLANE + out_row, 8, stride=PLANE)
                later[rows, :] = new

    for outward, halo, own_face in ((0, below, z_lo), (1, above, z_hi)):
        x_at, y_at = pl.ds(72 + 8 * outward, 8), pl.ds(64 + 8 * outward, 8)
        new = packed_step(
            [halo[0, c] for c in range(3)],
            [halo[1, c] for c in range(3)],
            [own_face[0, c] for c in range(3)],
            [[side[c, x_at, :] for c in range(3)] for side in (front, back)],
            [[side[c, y_at, :] for c in range(3)] for side in (left, right)],
            outward,
            row,
            lane,
        )
        for c in range(3):
            packed[outward, c] = new[c]

    later_ends = z_ends(
        [packed[0, c] for c in range(3)], [packed[1, c] for c in range(3)], lane
    )

    @pl.loop(0, 32, unroll=PLANES)
    def _(x):
        for yt in range(4):
            new = tile_step(later, 34, x + 1, yt, later_ends, x * 4 + yt, lane)
            for c in range(3):
                at = pl.ds(pl.multiple_of(c * 1024 + x * 32 + 8 * yt, 8), 8)
                out_ref[at, :] = 0.5 * (vel_ref[at, :] + new[c])

    for c in range(3):
        deposit(forces, corner_ref, out_ref, c)
        at = pl.ds(c * 1024, 1024)
        leaving.append(
            pltpu.make_async_copy(out_ref.at[at, :], new_out.at[at, :], grid_sems.at[c])
        )
        leaving[-1].start()
    for copy in leaving:
        copy.wait()


def call(body, out_shape, operands, name, unread=0):
    vmem = pl.BlockSpec(memory_space=pltpu.VMEM)
    specs = [vmem] * (len(operands) - unread) + [pl.BlockSpec(memory_space=pl.ANY)] * unread
    return pl.pallas_call(
        body,
        out_shape=out_shape,
        in_specs=specs,
        out_specs=jax.tree.map(lambda _: vmem, out_shape),
        compiler_params=pltpu.CompilerParams(vmem_limit_bytes=8 * 2**20),
        name=name,
    )(*operands)


def local(velocity, box_level, corners, owner_list):
    slots = box_level.shape[0]
    level_rows = box_level.reshape(slots * BOX, BOX * BOX)
    rows = velocity.reshape(-1, LANES)
    kept = jax.ShapeDtypeStruct(rows.shape, F32)
    rows, *z_own = call(z_faces, (kept, PACKED, PACKED), [rows], "z_faces")
    z_halos = exchange(*z_own, "gz")
    work = functools.partial(
        boxes, owner=owner_list, corners=corners, rows=rows, level_rows=level_rows
    )
    first = work(0, 1, after=z_own[0])
    sent = jax.ShapeDtypeStruct((3, Y_ROWS, LANES), F32)
    faces = call(y_faces, (sent,) * 2, [rows, *z_halos, first[0]], "y_faces", unread=1)
    y_halos = exchange(*faces, "gy")
    second = work(1, 1, after=faces[0])
    sent = jax.ShapeDtypeStruct((3, X_ROWS, LANES), F32)
    faces = call(
        x_faces, (sent,) * 2, [rows, *z_halos, *y_halos, second[0]], "x_faces", unread=1
    )
    x_halos = exchange(*faces, "gx")
    third = work(2, slots // PER - 2, after=faces[0])
    parts = [part for kind in zip(first, second, third) for part in kind]
    operands = [rows, *z_own, *z_halos, *y_halos, *x_halos, *parts]
    hbm = pl.BlockSpec(memory_space=pltpu.HBM)
    boxed = jax.ShapeDtypeStruct(level_rows.shape, F32)
    result, settled, bending = pl.pallas_call(
        momentum_body,
        out_shape=(jax.ShapeDtypeStruct(rows.shape, F32), boxed, boxed),
        in_specs=[pl.BlockSpec(memory_space=pltpu.VMEM)] * len(operands)
        + [pl.BlockSpec(memory_space=pltpu.SMEM)],
        out_specs=(hbm,) * 3,
        scratch_shapes=[
            pltpu.VMEM((3 * 36 * PLANE, LANES), F32),
            pltpu.VMEM((3 * 34 * PLANE, LANES), F32),
            pltpu.VMEM((3, PLANE, LANES), F32),
            pltpu.VMEM((2, 3, 8, LANES), F32),
            pltpu.VMEM(rows.shape, F32),
            pltpu.SemaphoreType.DMA((2, slots // PER, 2)),
            pltpu.SemaphoreType.DMA((3,)),
            pltpu.VMEM((2, *PACKED.shape), F32),
            pltpu.VMEM((2, *PACKED.shape), F32),
            pltpu.VMEM((2, 3, Y_ROWS, LANES), F32),
            pltpu.VMEM((2, 3, X_ROWS, LANES), F32),
        ],
        compiler_params=pltpu.CompilerParams(vmem_limit_bytes=24 * 2**20),
        name="momentum",
    )(*operands, corners)
    return (
        result.reshape(velocity.shape),
        settled.reshape(box_level.shape),
        bending.reshape(box_level.shape),
    )


def solution(mesh):
    placed = (
        P(None, "gx", "gy", "gz"),
        P(("gx", "gy", "gz"), None, None),
        P(("gx", "gy", "gz"), None),
        P(("gx", "gy", "gz")),
    )
    return jax.shard_map(
        local,
        mesh=mesh,
        in_specs=placed,
        out_specs=(
            P(None, "gx", "gy", "gz"),
            P(("gx", "gy", "gz"), None, None),
            P(("gx", "gy", "gz"), None, None),
        ),
        check_vma=False,
    )
```

```python
import functools
import math

import jax
import jax.numpy as jnp
from jax import lax
from jax.experimental import pallas as pl
from jax.experimental.pallas import tpu as pltpu
from jax.sharding import PartitionSpec as P

ITERS = 12
BOX = 16
LANES = 128
PER = 8

CUT, LEVEL, MI, MJ, WENO, CENTRAL, KAPPA, PLANES = 6, 8, 5, 4, 16, 8, 16, 8

box_step = 0.25
pseudo_step = 0.3
weno_floor = 1e-06
band_width = 1.5
tension = 2.0
grid_step = 0.2
viscosity = 0.1
normal_floor = 0.5

F32 = jnp.float32
TILE = (8, LANES)


def iotas():
    row = lax.broadcasted_iota(jnp.int32, TILE, 0)
    lane = lax.broadcasted_iota(jnp.int32, TILE, 1)
    return row, lane


def block_transpose(x, row, lane):
    block = lane // BOX
    x = jnp.take_along_axis(x, (lane - BOX * row) % LANES, axis=1)
    x = jnp.take_along_axis(x, (block - row) % 8, axis=0)
    return jnp.take_along_axis(x, (lane + BOX * row) % LANES, axis=1)


def weno(ab, bc, ce, ef):
    d1, d2, d3 = ab - bc, bc - ce, ce - ef
    bc2, ce2 = bc + bc, ce + ce
    t1, t2, t3 = d1 - bc2, bc + ce, d3 + ce2
    part = 3.0 / 13.0
    floor = weno_floor * 12.0 / 13.0
    s1 = (d1 * d1 + floor) + part * (t1 * t1)
    s2 = (d2 * d2 + floor) + part * (t2 * t2)
    s3 = (d3 * d3 + floor) + part * (t3 * t3)
    q1, q2, q3 = s1 * s1, s2 * s2, s3 * s3
    w1 = q2 * q3
    w2 = 6.0 * (q1 * q3)
    w3 = 3.0 * (q1 * q2)
    top = w1 * ((ab + ab) - 5.0 * bc) - w2 * (bc + ce2) + w3 * (ef - (ce2 + ce2))
    return top / (6.0 * (w1 + w2 + w3))


def upwind(speed, here, ahead, far_back, back, middle, front, far_front):
    pos = speed > 0.0
    turn = weno(
        jnp.where(pos, far_back, far_front),
        jnp.where(pos, back, front),
        middle,
        jnp.where(pos, front, back),
    )
    return speed * jnp.where(pos, here, ahead) - jnp.abs(speed) * turn


ROWS = 32


def box_body(first_group, count, owner_ref, corner_ref, vel_ref, level_ref, *rest):
    (force_out, turned, turned_kappa, *scratch) = rest[-14:]
    (u_ref, l_ref, mi_ref, mj_ref, pa, pb, c_ref, s_ref, k_ref) = scratch[:9]
    levels, level_sems = scratch[9:]
    row, lane = iotas()
    k = lane % BOX
    block = lane // BOX
    k_first, k_last = k == 0, k == BOX - 1
    top, bottom = row == 0, row == 7

    def next_k(v):
        return jnp.where(k_last, v, pltpu.roll(v, LANES - 1, 1))

    def prev_k(v):
        return jnp.where(k_first, v, pltpu.roll(v, 1, 1))

    def one_group(own):
        g = first_group + own
        spots = [[corner_ref[g * PER + b, d] for d in range(3)] for b in range(PER)]
        alive = jnp.zeros(TILE, F32)
        for b in range(PER):
            living = jnp.where(owner_ref[g * PER + b] >= 0, 1.0, 0.0)
            alive = jnp.where(block == b, living, alive)

        for b in range(PER):
            px, py, pz = spots[b]
            turn = (BOX * b + LANES - pz) % LANES
            here = block == b
            base = px * 32 + py

            @pl.loop(0, 6, unroll=CUT)
            def _(step):
                c = step // 2
                i0 = (step % 2) * 8
                for i in range(8):
                    for jt in range(2):
                        part = vel_ref[pl.ds(base + c * 1024 + (i0 + i) * 32 + 8 * jt, 8), :]
                        pltpu.store(
                            u_ref.at[c, i0 + i, pl.ds(8 * jt, 8), :],
                            pltpu.roll(part, turn, 1),
                            mask=here,
                        )

        for jt in range(2):
            come(own, jt).wait()

        @pl.loop(0, BOX, unroll=LEVEL)
        def _(i):
            for jt in range(2):
                x = levels[pl.ds((own + count * jt) * (PER * BOX) + i, 8, stride=BOX), :]
                l_ref[i, pl.ds(8 + 8 * jt, 8), :] = block_transpose(x, row, lane)

        mi_ref[0] = jnp.zeros((BOX, LANES), F32)
        mi_ref[1] = jnp.zeros((BOX, LANES), F32)
        mi_ref[2] = jnp.zeros((BOX, LANES), F32)

        @pl.loop(1, BOX, unroll=MI)
        def _(i):
            for jt in range(2):
                at = pl.ds(8 + 8 * jt, 8)
                mi_ref[i + 2, pl.ds(8 * jt, 8), :] = l_ref[i, at, :] - l_ref[i - 1, at, :]

        for t in range(3):
            mi_ref[18 + t] = mi_ref[17]

        @pl.loop(0, BOX, unroll=MJ)
        def _(i):
            for jt in range(2):
                here = l_ref[i, pl.ds(8 + 8 * jt, 8), :]
                m = here - l_ref[i, pl.ds(7 + 8 * jt, 8), :]
                if jt == 0:
                    m = jnp.where(top, 0.0, m)
                    mj_ref[i, pl.ds(0, 8), :] = jnp.zeros(TILE, F32)
                else:
                    mj_ref[i, pl.ds(24, 8), :] = jnp.broadcast_to(m[7:8, :], TILE)
                mj_ref[i, pl.ds(8 + 8 * jt, 8), :] = m

        @pl.loop(0, BOX, unroll=WENO)
        def _(i):
            for jt in range(2):
                at = pl.ds(8 * jt, 8)
                padded_at = pl.ds(8 + 8 * jt, 8)
                here = l_ref[i, padded_at, :]
                m = [mi_ref[i + t, at, :] for t in range(6)]
                change = upwind(
                    u_ref[0, i, at, :], m[2], m[3], *[m[t + 1] - m[t] for t in range(5)]
                )
                m = [mj_ref[i, pl.ds(6 + t + 8 * jt, 8), :] for t in range(6)]
                change += upwind(
                    u_ref[1, i, at, :], m[2], m[3], *[m[t + 1] - m[t] for t in range(5)]
                )
                m = here - prev_k(here)
                ahead = next_k(m)
                middle = ahead - m
                back = pltpu.roll(middle, 1, 1)
                front = next_k(middle)
                change += upwind(
                    u_ref[2, i, at, :],
                    m,
                    ahead,
                    jnp.where(k_first, 0.0, pltpu.roll(back, 1, 1)),
                    back,
                    middle,
                    front,
                    next_k(front),
                )
                advected = here - box_step * change
                pa[i, padded_at, :] = advected
                c_ref[i, at, :] = pseudo_step * advected * lax.rsqrt(advected * advected + 1.0)
                s_ref[i, at, :] = jnp.where(advected > 0.0, 1.0, -1.0)

        def sweep(src, dst):
            for jt in range(2):
                at = pl.ds(8 * jt, 8)
                behind_i = None
                cur = src[0, pl.ds(8 + 8 * jt, 8), :]
                for i in range(BOX):
                    s = s_ref[i, at, :]
                    terms = []
                    sc = s * cur
                    if i < BOX - 1:
                        nxt = src[i + 1, pl.ds(8 + 8 * jt, 8), :]
                        sides = s * nxt if behind_i is None else jnp.minimum(s * nxt, s * behind_i)
                    else:
                        nxt = None
                        sides = s * behind_i
                    terms.append(sc - jnp.minimum(sides, sc))
                    lower = src[i, pl.ds(7 + 8 * jt, 8), :]
                    upper = src[i, pl.ds(9 + 8 * jt, 8), :]
                    if jt == 0:
                        lower = jnp.where(top, cur, lower)
                    else:
                        upper = jnp.where(bottom, cur, upper)
                    terms.append(sc - jnp.minimum(jnp.minimum(s * lower, s * upper), sc))
                    lower = jnp.where(k_first, cur, pltpu.roll(cur, 1, 1))
                    upper = jnp.where(k_last, cur, pltpu.roll(cur, LANES - 1, 1))
                    terms.append(sc - jnp.minimum(jnp.minimum(s * lower, s * upper), sc))
                    squared = terms[0] * terms[0] + terms[1] * terms[1] + terms[2] * terms[2]
                    root = squared * lax.rsqrt(jnp.maximum(squared, 1e-37))
                    dst[i, pl.ds(8 + 8 * jt, 8), :] = cur - c_ref[i, at, :] * (root - 1.0)
                    behind_i, cur = cur, nxt

        @pl.loop(0, ITERS // 2)
        def _(_):
            sweep(pa, pb)
            sweep(pb, pa)

        def central(i, jt):
            at = pl.ds(8 + 8 * jt, 8)
            cur = pa[i, at, :]
            c0 = 0.5 * (pa[jnp.minimum(i + 1, BOX - 1), at, :] - pa[jnp.maximum(i - 1, 0), at, :])
            lower = pa[i, pl.ds(7 + 8 * jt, 8), :]
            upper = pa[i, pl.ds(9 + 8 * jt, 8), :]
            if jt == 0:
                lower = jnp.where(top, cur, lower)
            else:
                upper = jnp.where(bottom, cur, upper)
            c1 = 0.5 * (upper - lower)
            c2 = 0.5 * (next_k(cur) - prev_k(cur))
            return cur, c0, c1, c2

        @pl.loop(0, BOX, unroll=CENTRAL)
        def _(i):
            for jt in range(2):
                cur, c0, c1, c2 = central(i, jt)
                size = c0 * c0 + c1 * c1 + c2 * c2
                inverse = jnp.minimum(lax.rsqrt(size), 1.0 / normal_floor)
                at = pl.ds(8 * jt, 8)
                mi_ref[i, at, :] = c0 * inverse
                mj_ref[i, pl.ds(8 + 8 * jt, 8), :] = c1 * inverse
                n3 = c2 * inverse
                k_ref[i, at, :] = next_k(n3) - prev_k(n3)
                scaled = cur * (1.0 / band_width)
                band = jnp.exp(-(scaled * scaled)) * (
                    grid_step * tension / (band_width * math.sqrt(math.pi))
                )
                band = band * alive
                for c, slope in enumerate((c0, c1, c2)):
                    force_out[own, c, i, at, :] = band * slope
                y = block_transpose(cur * alive, row, lane)
                turned[pl.ds((own * 2 + jt) * (PER * BOX) + i, 8, stride=BOX), :] = y

        @pl.loop(0, BOX, unroll=KAPPA)
        def _(i):
            for jt in range(2):
                at = pl.ds(8 * jt, 8)
                padded_at = pl.ds(8 + 8 * jt, 8)
                d1 = mi_ref[jnp.minimum(i + 1, BOX - 1), at, :] - mi_ref[jnp.maximum(i - 1, 0), at, :]
                lower = mj_ref[i, pl.ds(7 + 8 * jt, 8), :]
                upper = mj_ref[i, pl.ds(9 + 8 * jt, 8), :]
                if jt == 0:
                    lower = jnp.where(top, mj_ref[i, padded_at, :], lower)
                else:
                    upper = jnp.where(bottom, mj_ref[i, padded_at, :], upper)
                kappa = 0.5 * (d1 + (upper - lower) + k_ref[i, at, :])
                for c in range(3):
                    force_out[own, c, i, at, :] = force_out[own, c, i, at, :] * kappa
                y = block_transpose(kappa * alive, row, lane)
                turned_kappa[pl.ds((own * 2 + jt) * (PER * BOX) + i, 8, stride=BOX), :] = y

    def come(own, jt):
        return pltpu.make_async_copy(
            level_ref.at[
                pl.ds((first_group + own) * (PER * BOX), PER * BOX), pl.ds(LANES * jt, LANES)
            ],
            levels.at[pl.ds((own + count * jt) * (PER * BOX), PER * BOX), :],
            level_sems.at[own, jt],
        )

    for own in range(count):
        for jt in range(2):
            come(own, jt).start()

    @pl.loop(0, count)
    def _(own):
        one_group(own)


def boxes(first_group, count, owner, corners, rows, level_rows, after):
    smem = pl.BlockSpec(memory_space=pltpu.SMEM)
    hbm = pl.BlockSpec(memory_space=pltpu.HBM)
    vmem = pl.BlockSpec(memory_space=pltpu.VMEM)
    any_ = pl.BlockSpec(memory_space=pl.ANY)
    plane = lambda *lead: pltpu.VMEM((*lead, LANES), F32)
    turned = jax.ShapeDtypeStruct((count * 2 * PER * BOX, LANES), F32)
    return pl.pallas_call(
        functools.partial(box_body, first_group, count),
        out_shape=(jax.ShapeDtypeStruct((count, 3, BOX, BOX, LANES), F32), turned, turned),
        in_specs=[smem, smem, vmem, hbm, any_],
        out_specs=(vmem,) * 3,
        scratch_shapes=[
            plane(3, BOX, BOX),
            plane(BOX, ROWS),
            plane(BOX + 5, BOX),
            plane(BOX, ROWS),
            plane(BOX, ROWS),
            plane(BOX, ROWS),
            plane(BOX, BOX),
            plane(BOX, BOX),
            plane(BOX, BOX),
            plane(count * 2 * PER * BOX),
            pltpu.SemaphoreType.DMA((count, 2)),
        ],
        compiler_params=pltpu.CompilerParams(vmem_limit_bytes=16 * 2**20),
        cost_estimate=pl.CostEstimate(
            flops=30_000_000, bytes_accessed=5_000_000, transcendentals=0
        ),
        name="boxes",
    )(owner, corners, rows, level_rows, after)


def deposit(force_refs, corner_ref, grid_ref, c):
    _, lane = iotas()

    def one_group(ref, own, g):
        for b in range(PER):
            px, py, pz = [corner_ref[g * PER + b, d] for d in range(3)]
            inside = (lane >= pz) & (lane < pz + BOX)
            turn = (pz + LANES - BOX * b) % LANES
            base = c * 1024 + px * 32 + py
            for i0 in (0, 8):
                sums = []
                for i in range(8):
                    for jt in range(2):
                        old = grid_ref[pl.ds(base + (i0 + i) * 32 + 8 * jt, 8), :]
                        push = pltpu.roll(ref[own, c, i0 + i, pl.ds(8 * jt, 8), :], turn, 1)
                        sums.append(old + jnp.where(inside, push, 0.0))
                for i in range(8):
                    for jt in range(2):
                        grid_ref[pl.ds(base + (i0 + i) * 32 + 8 * jt, 8), :] = sums[2 * i + jt]

    done = 0
    for ref in force_refs:
        count = ref.shape[0]

        @pl.loop(0, count)
        def _(own):
            one_group(ref, own, done + own)

        done += count


PLANE = 48


PACKED = jax.ShapeDtypeStruct((2, 3, 8, LANES), F32)
Y_ROWS = 80
X_ROWS = 88


def z_faces(rows_ref, kept_ref, near_ref, far_ref):
    _, lane = iotas()
    even = is_even("gz")

    def one(x, packed):
        out = []
        for c in range(3):
            parts = packed[4 * c : 4 * c + 4]
            for yt in range(4):
                n = x * 4 + yt
                at = pl.multiple_of(c * 1024 + x * 32 + 8 * yt, 8)
                tile = rows_ref[pl.ds(at, 8), :]
                kept_ref[pl.ds(at, 8), :] = tile
                turned = pltpu.roll(tile, n, 1)
                parts = [
                    jnp.where(lane == (n + shift + LANES) % LANES, turned, part)
                    for shift, part in zip((0, 1, -1, -2), parts)
                ]
            out += parts
        return tuple(out)

    packed = lax.fori_loop(0, 32, one, (jnp.zeros(TILE, F32),) * 12, unroll=PLANES)
    for c in range(3):
        first, second, last, before = packed[4 * c : 4 * c + 4]
        lower = (first, pltpu.roll(second, LANES - 1, 1))
        upper = (pltpu.roll(last, 1, 1), pltpu.roll(before, 2, 1))
        for layer in range(2):
            near_ref[layer, c] = jnp.where(even, upper[layer], lower[layer])
            far_ref[layer, c] = jnp.where(even, lower[layer], upper[layer])


def y_faces(rows_ref, z_near, z_far, _, near_ref, far_ref):
    even, z_even = is_even("gy"), is_even("gz")
    for out, upper in ((near_ref, even), (far_ref, jnp.logical_not(even))):
        for c in range(3):
            for n in range(2):
                y = jnp.where(upper, 31 - n, n)
                out[c, pl.ds(32 * n, 32), :] = rows_ref[pl.ds(c * 1024 + y, 32, stride=32), :]
            out[c, pl.ds(64, 8), :] = jnp.where(z_even, z_far[0, c], z_near[0, c])
            out[c, pl.ds(72, 8), :] = jnp.where(z_even, z_near[0, c], z_far[0, c])


def x_faces(rows_ref, z_near, z_far, y_near, y_far, _, near_ref, far_ref):
    even, y_even, z_even = is_even("gx"), is_even("gy"), is_even("gz")
    for out, upper in ((near_ref, even), (far_ref, jnp.logical_not(even))):
        for c in range(3):
            for n in range(2):
                x = jnp.where(upper, 31 - n, n)
                at = pl.multiple_of(c * 1024 + 32 * x, 8)
                out[c, pl.ds(32 * n, 32), :] = rows_ref[pl.ds(at, 32), :]
            x = jnp.where(upper, 31, 0)
            near, far = y_near[c, pl.ds(x, 1), :], y_far[c, pl.ds(x, 1), :]
            out[c, pl.ds(64, 8), :] = jnp.zeros(TILE, F32)
            out[c, pl.ds(64, 1), :] = jnp.where(y_even, far, near)
            out[c, pl.ds(65, 1), :] = jnp.where(y_even, near, far)
            out[c, pl.ds(72, 8), :] = jnp.where(z_even, z_far[0, c], z_near[0, c])
            out[c, pl.ds(80, 8), :] = jnp.where(z_even, z_near[0, c], z_far[0, c])


def exchange(first, second, axis):
    size = lax.axis_size(axis)
    near = [(i, i ^ 1) for i in range(size)]
    far = [(i, (i + 1) % size if i % 2 else (i - 1) % size) for i in range(size)]
    return lax.ppermute(first, axis, near), lax.ppermute(second, axis, far)


def is_even(axis):
    return lax.axis_index(axis) % 2 == 0


def slopes_to_f(centre, v, lower, upper):
    advect = sum(centre[d] * (upper[d] - lower[d]) for d in range(3))
    spread = (upper[0] + lower[0]) + (upper[1] + lower[1]) + (upper[2] + lower[2]) - 6.0 * v
    return viscosity * spread - 0.5 * advect


def along_z(v, before, after, lane):
    lower = jnp.where(lane == 0, before, pltpu.roll(v, 1, 1))
    upper = jnp.where(lane == LANES - 1, after, pltpu.roll(v, LANES - 1, 1))
    return lower, upper


def z_ends(below, above, lane):
    even = lane % 2 == 0
    out = []
    for lower, upper in zip(below, above):
        upper = pltpu.roll(upper, LANES - 1, 1)
        out.append((jnp.where(even, lower, upper), jnp.where(even, upper, lower)))
    return out


def tile_step(ext, planes, plane, yt, ends, n, lane):
    at = [
        pl.multiple_of((c * planes + plane) * PLANE + 8 + 8 * yt, 8) for c in range(3)
    ]
    centre = [ext[pl.ds(at[c], 8), :] for c in range(3)]
    out = []
    for c in range(3):
        v = centre[c]
        end = pltpu.roll(ends[c][yt % 2], (LANES - n) % LANES, 1)
        lower2, upper2 = along_z(v, end, end, lane)
        lower = (ext[pl.ds(at[c] - PLANE, 8), :], ext[pl.ds(at[c] - 1, 8), :], lower2)
        upper = (ext[pl.ds(at[c] + PLANE, 8), :], ext[pl.ds(at[c] + 1, 8), :], upper2)
        out.append(v + grid_step * slopes_to_f(centre, v, lower, upper))
    return out


def packed_step(own, beyond, inner, x_sides, y_sides, outward, row, lane):
    out = []
    for c in range(3):
        v = own[c]
        x_lower = jnp.where(lane < 4, pltpu.roll(x_sides[0][c], 4, 1), pltpu.roll(v, 4, 1))
        x_upper = jnp.where(
            lane >= LANES - 4,
            pltpu.roll(x_sides[1][c], LANES - 4, 1),
            pltpu.roll(v, LANES - 4, 1),
        )
        down = pltpu.roll(v, 1, 0)
        down_side = pltpu.roll(pltpu.roll(y_sides[0][c], 1, 0), LANES - 3, 1)
        y_lower = jnp.where(
            row == 0, jnp.where(lane % 4 == 0, down_side, pltpu.roll(down, 1, 1)), down
        )
        up = pltpu.roll(v, 7, 0)
        up_side = pltpu.roll(pltpu.roll(y_sides[1][c], 7, 0), 3, 1)
        y_upper = jnp.where(
            row == 7, jnp.where(lane % 4 == 3, up_side, pltpu.roll(up, LANES - 1, 1)), up
        )
        pair = (inner[c], beyond[c]) if outward else (beyond[c], inner[c])
        f = slopes_to_f(own, v, (x_lower, y_lower, pair[0]), (x_upper, y_upper, pair[1]))
        out.append(v + grid_step * f)
    return out


def momentum_body(
    vel_ref, face_near, face_far, z_near, z_far, y_near, y_far, x_near, x_far, *refs,
):
    forces, settled, bending, corner_ref = refs[:3], refs[3:6], refs[6:9], refs[9]
    new_out, settled_out, bending_out, ext, later, sides, packed, out_ref, sems, grid_sems = refs[10:20]
    own_faces, z_halos, y_halos, x_halos = refs[20:]
    row, lane = iotas()
    for axis, kept, near, far in (
        ("gz", own_faces, face_near, face_far),
        ("gz", z_halos, z_near, z_far),
        ("gy", y_halos, y_near, y_far),
        ("gx", x_halos, x_near, x_far),
    ):
        upper = jnp.where(is_even(axis), 1, 0)
        kept[upper] = near[...]
        kept[1 - upper] = far[...]
    z_lo, z_hi = own_faces.at[0], own_faces.at[1]
    below, above = z_halos.at[0], z_halos.at[1]
    left, right = y_halos.at[0], y_halos.at[1]
    front, back = x_halos.at[0], x_halos.at[1]

    leaving = []
    for n, (parts, out) in enumerate(((settled, settled_out), (bending, bending_out))):
        group = 0
        for part in parts:
            for own in range(part.shape[0] // (2 * PER * BOX)):
                for jt in range(2):
                    leaving.append(
                        pltpu.make_async_copy(
                            part.at[pl.ds((own * 2 + jt) * (PER * BOX), PER * BOX), :],
                            out.at[
                                pl.ds(group * (PER * BOX), PER * BOX), pl.ds(LANES * jt, LANES)
                            ],
                            sems.at[n, group, jt],
                        )
                    )
                group += 1
    for copy in leaving:
        copy.start()

    for c in range(3):
        base = c * 36 * PLANE
        for plane, halo, layer in ((1, front, 0), (0, front, 1), (34, back, 0), (35, back, 1)):
            ext[pl.ds(base + plane * PLANE + 8, 32), :] = halo[c, pl.ds(32 * layer, 32), :]
        for plane, halo in ((1, front), (34, back)):
            ext[pl.ds(base + plane * PLANE + 7, 1), :] = halo[c, pl.ds(64, 1), :]
            ext[pl.ds(base + plane * PLANE + 40, 1), :] = halo[c, pl.ds(65, 1), :]
        ext[pl.ds(base + 2 * PLANE + 7, 32, stride=PLANE), :] = left[c, pl.ds(0, 32), :]
        ext[pl.ds(base + 2 * PLANE + 40, 32, stride=PLANE), :] = right[c, pl.ds(0, 32), :]

    @pl.loop(0, 32)
    def _(x):
        for c in range(3):
            at = pl.multiple_of((c * 36 + x + 2) * PLANE + 8, 8)
            ext[pl.ds(at, 32), :] = vel_ref[pl.ds(pl.multiple_of(c * 1024 + x * 32, 8), 32), :]

    ends = z_ends([below[0, c] for c in range(3)], [above[0, c] for c in range(3)], lane)

    @pl.loop(0, 32, unroll=PLANES)
    def _(x):
        for yt in range(4):
            new = tile_step(ext, 36, x + 2, yt, ends, x * 4 + yt, lane)
            for c in range(3):
                at = pl.multiple_of((c * 34 + x + 1) * PLANE + 8 + 8 * yt, 8)
                later[pl.ds(at, 8), :] = new[c]

    for halo, plane, x in ((front, 1, 31), (back, 34, 0)):
        side_ends = z_ends(
            [halo[c, pl.ds(72, 8), :] for c in range(3)],
            [halo[c, pl.ds(80, 8), :] for c in range(3)],
            lane,
        )
        for yt in range(4):
            new = tile_step(ext, 36, plane, yt, side_ends, x * 4 + yt, lane)
            for c in range(3):
                later[pl.ds((c * 34 + plane - 1) * PLANE + 8 + 8 * yt, 8), :] = new[c]

    for halo, out_row, y, inside in ((left, 7, 31, 0), (right, 40, 0, 31)):
        for c in range(3):
            sides[c, pl.ds(8, 32), :] = halo[c, pl.ds(0, 32), :]
            for at, end in ((7, front), (40, back)):
                sides[c, pl.ds(at, 1), :] = end[c, pl.ds(64 if out_row == 7 else 65, 1), :]
        for t in range(4):
            at = pl.ds(8 + 8 * t, 8)
            centre = [sides[c, at, :] for c in range(3)]
            where_x = 4 * (8 * t + row) + y // 8
            for c in range(3):
                v = centre[c]
                ends = [
                    jnp.take_along_axis(
                        jnp.broadcast_to(halo[c, pl.ds(64 + 8 * e + y % 8, 1), :], TILE),
                        where_x,
                        axis=1,
                    )
                    for e in range(2)
                ]
                lower2, upper2 = along_z(v, *ends, lane)
                beyond = halo[c, pl.ds(32 + 8 * t, 8), :]
                inner = vel_ref[pl.ds(c * 1024 + 8 * t * 32 + inside, 8, stride=32), :]
                pair = (beyond, inner) if out_row == 7 else (inner, beyond)
                lower = (sides[c, pl.ds(7 + 8 * t, 8), :], pair[0], lower2)
                upper = (sides[c, pl.ds(9 + 8 * t, 8), :], pair[1], upper2)
                new = v + grid_step * slopes_to_f(centre, v, lower, upper)
                rows = pl.ds((c * 34 + 8 * t + 1) * PLANE + out_row, 8, stride=PLANE)
                later[rows, :] = new

    for outward, halo, own_face in ((0, below, z_lo), (1, above, z_hi)):
        x_at, y_at = pl.ds(72 + 8 * outward, 8), pl.ds(64 + 8 * outward, 8)
        new = packed_step(
            [halo[0, c] for c in range(3)],
            [halo[1, c] for c in range(3)],
            [own_face[0, c] for c in range(3)],
            [[side[c, x_at, :] for c in range(3)] for side in (front, back)],
            [[side[c, y_at, :] for c in range(3)] for side in (left, right)],
            outward,
            row,
            lane,
        )
        for c in range(3):
            packed[outward, c] = new[c]

    later_ends = z_ends(
        [packed[0, c] for c in range(3)], [packed[1, c] for c in range(3)], lane
    )

    @pl.loop(0, 32, unroll=PLANES)
    def _(x):
        for yt in range(4):
            new = tile_step(later, 34, x + 1, yt, later_ends, x * 4 + yt, lane)
            for c in range(3):
                at = pl.ds(pl.multiple_of(c * 1024 + x * 32 + 8 * yt, 8), 8)
                out_ref[at, :] = 0.5 * (vel_ref[at, :] + new[c])

    for c in range(3):
        deposit(forces, corner_ref, out_ref, c)
        at = pl.ds(c * 1024, 1024)
        leaving.append(
            pltpu.make_async_copy(out_ref.at[at, :], new_out.at[at, :], grid_sems.at[c])
        )
        leaving[-1].start()
    for copy in leaving:
        copy.wait()


def call(body, out_shape, operands, name, unread=0):
    vmem = pl.BlockSpec(memory_space=pltpu.VMEM)
    specs = [vmem] * (len(operands) - unread) + [pl.BlockSpec(memory_space=pl.ANY)] * unread
    return pl.pallas_call(
        body,
        out_shape=out_shape,
        in_specs=specs,
        out_specs=jax.tree.map(lambda _: vmem, out_shape),
        compiler_params=pltpu.CompilerParams(vmem_limit_bytes=8 * 2**20),
        name=name,
    )(*operands)


def local(velocity, box_level, corners, owner_list):
    slots = box_level.shape[0]
    level_rows = box_level.reshape(slots * BOX, BOX * BOX)
    rows = velocity.reshape(-1, LANES)
    kept = jax.ShapeDtypeStruct(rows.shape, F32)
    rows, *z_own = call(z_faces, (kept, PACKED, PACKED), [rows], "z_faces")
    z_halos = exchange(*z_own, "gz")
    work = functools.partial(
        boxes, owner=owner_list, corners=corners, rows=rows, level_rows=level_rows
    )
    first = work(0, 1, after=z_own[0])
    sent = jax.ShapeDtypeStruct((3, Y_ROWS, LANES), F32)
    faces = call(y_faces, (sent,) * 2, [rows, *z_halos, first[0]], "y_faces", unread=1)
    y_halos = exchange(*faces, "gy")
    second = work(1, 1, after=faces[0])
    sent = jax.ShapeDtypeStruct((3, X_ROWS, LANES), F32)
    faces = call(
        x_faces, (sent,) * 2, [rows, *z_halos, *y_halos, second[0]], "x_faces", unread=1
    )
    x_halos = exchange(*faces, "gx")
    third = work(2, slots // PER - 2, after=faces[0])
    parts = [part for kind in zip(first, second, third) for part in kind]
    operands = [rows, *z_own, *z_halos, *y_halos, *x_halos, *parts]
    hbm = pl.BlockSpec(memory_space=pltpu.HBM)
    boxed = jax.ShapeDtypeStruct(level_rows.shape, F32)
    result, settled, bending = pl.pallas_call(
        momentum_body,
        out_shape=(jax.ShapeDtypeStruct(rows.shape, F32), boxed, boxed),
        in_specs=[pl.BlockSpec(memory_space=pltpu.VMEM)] * len(operands)
        + [pl.BlockSpec(memory_space=pltpu.SMEM)],
        out_specs=(hbm,) * 3,
        scratch_shapes=[
            pltpu.VMEM((3 * 36 * PLANE, LANES), F32),
            pltpu.VMEM((3 * 34 * PLANE, LANES), F32),
            pltpu.VMEM((3, PLANE, LANES), F32),
            pltpu.VMEM((2, 3, 8, LANES), F32),
            pltpu.VMEM(rows.shape, F32),
            pltpu.SemaphoreType.DMA((2, slots // PER, 2)),
            pltpu.SemaphoreType.DMA((3,)),
            pltpu.VMEM((2, *PACKED.shape), F32),
            pltpu.VMEM((2, *PACKED.shape), F32),
            pltpu.VMEM((2, 3, Y_ROWS, LANES), F32),
            pltpu.VMEM((2, 3, X_ROWS, LANES), F32),
        ],
        compiler_params=pltpu.CompilerParams(vmem_limit_bytes=24 * 2**20),
        name="momentum",
    )(*operands, corners)
    return (
        result.reshape(velocity.shape),
        settled.reshape(box_level.shape),
        bending.reshape(box_level.shape),
    )


def solution(mesh):
    placed = (
        P(None, "gx", "gy", "gz"),
        P(("gx", "gy", "gz"), None, None),
        P(("gx", "gy", "gz"), None),
        P(("gx", "gy", "gz")),
    )
    return jax.shard_map(
        local,
        mesh=mesh,
        in_specs=placed,
        out_specs=(
            P(None, "gx", "gy", "gz"),
            P(("gx", "gy", "gz"), None, None),
            P(("gx", "gy", "gz"), None, None),
        ),
        check_vma=False,
    )
```
